32 devices in a mesh: tile: 4 (over z), img: 8 (over y, x, core).
Axes of the slice: x: 2, y: 2, z: 4, core: 2. Of those that a mesh axis runs over, the one named last changes fastest.
Arguments:
- qkv: bfloat16 [8, 4, 8, 32, 1536], P('img', 'tile'), may hold values from -6 to 6
- cotangent: bfloat16 [8, 4, 8, 32, 1024], P('img', 'tile'), may hold values from -48 to 48
- dw_weight: float32 [25, 1536], replicated, may hold values from -1.25 to 1.25
- pw_weight: float32 [32, 1536], replicated, may hold values from -1 to 1
- tile_image: int32 [8, 4], P('img', 'tile'), may hold values from 0 to 2, as said below
- tile_row: int32 [8, 4], P('img', 'tile'), may hold values from 0 to 1, as said below
- tile_col: int32 [8, 4], P('img', 'tile'), may hold values from 0 to 1, as said below
- image_height: int32 [8, 2], P('img'), may hold values from 0 to 2, as said below
- image_width: int32 [8, 2], P('img'), may hold values from 0 to 2, as said below
Outputs:
- grad_qkv: bfloat16 [8, 4, 8, 32, 1536], P('img', 'tile')
- grad_dw: float32 [25, 1536], replicated
- grad_pw: float32 [32, 1536], replicated
The draws below stay inside these ranges and needn't reach their ends.
Inputs may be any that keep to these rules, and one draw needn't show every extreme that they name: Within a group tile_image never falls; each image occupies height * width consecutive tiles; padding tiles come last; the first group holds 2 images of 1 x 2 tiles; the second group holds one image of 2 x 2 tiles. `tile_row`: the tile's row in its image's grid, row-major order; 0 on padding tiles. `tile_col`: the tile's column in its image's grid; 0 on padding tiles. `image_height`: used slots come first; an unused slot has height 0. `image_width`: used slots come first; an unused slot has width 0.
All inputs are finite; a program needn't handle non-finite values.
Results may differ from the reference program's by a relative error of at most 0.005.
Values may be sent and summed in bfloat16 or wider, within the bound.
No kernel may reach another device: no remote copies, remote signals or barrier semaphores. Data moves between devices by JAX's collectives and lax.ppermute only.
A program may use at most 64 MiB of HBM per device.

```python
import math
import jax
import jax.numpy as jnp
from jax import lax

HEADS = 16
HD = 32
TILE_H = 8
TILE_W = 32
C3 = 1536
GROUPS = 8
TILES = 4
MAXIMG = 2
HMAX = 2


def layout(key):
    group_keys = jax.random.split(jax.random.fold_in(key, 9173), GROUPS)

    def one_group(group_key, group_index):
        tall_key, wide_key = jax.random.split(group_key)
        heights = jax.random.randint(tall_key, (MAXIMG,), 1, HMAX + 1)
        widths = jax.random.randint(wide_key, (MAXIMG,), 1, 3)
        slot_ids = jnp.arange(MAXIMG)
        heights = jnp.where(group_index == 0, 1, heights)
        widths = jnp.where(group_index == 0, 2, widths)
        heights = jnp.where(group_index == 1, jnp.where(slot_ids == 0, HMAX, 1), heights)
        widths = jnp.where(group_index == 1, 2, widths)
        capacity = jnp.where(group_index <= 1, TILES, TILES - 1)
        run_ends = jnp.cumsum(heights * widths)
        fitting = run_ends <= capacity
        heights = jnp.where(fitting, heights, 0).astype(jnp.int32)
        widths = jnp.where(fitting, widths, 0).astype(jnp.int32)
        tile_areas = heights * widths
        run_ends = jnp.cumsum(tile_areas)
        starts = run_ends - tile_areas
        places = jnp.arange(TILES)
        image_slot = jnp.sum((run_ends[None, :] <= places[:, None]).astype(jnp.int32), axis=1)
        clipped = jnp.minimum(image_slot, MAXIMG - 1)
        within = places - starts[clipped]
        wide_tiles = jnp.maximum(widths[clipped], 1)
        grid_rows = jnp.where(image_slot < MAXIMG, within // wide_tiles, 0)
        grid_cols = jnp.where(image_slot < MAXIMG, within % wide_tiles, 0)
        return (image_slot.astype(jnp.int32), grid_rows.astype(jnp.int32), grid_cols.astype(jnp.int32), heights, widths)
    return jax.vmap(one_group)(group_keys, jnp.arange(GROUPS))


def draw_tile_image(key, part):
    return layout(key)[0]


def draw_tile_row(key, part):
    return layout(key)[1]


def draw_tile_col(key, part):
    return layout(key)[2]


def draw_image_height(key, part):
    return layout(key)[3]


def draw_image_width(key, part):
    return layout(key)[4]


def shard_levels(stream_key, extent, shards, smallest, largest):
    def one(position, parts):
        steps = jax.random.uniform(jax.random.fold_in(jax.random.fold_in(stream_key, 6), position), (parts,), jnp.float32, smallest / len(shards), largest / len(shards))
        return jnp.repeat(jnp.exp(steps), extent[position] // parts).reshape((-1,) + (1,) * (len(extent) - position - 1))

    factor_of = one(*shards[0])
    for cut in shards[1:]:
        factor_of = factor_of * one(*cut)
    return factor_of


def scatter_about(rng, dims, scale, limit, cuts=(), held_as=jnp.bfloat16):
    array = jax.random.normal(rng, dims, jnp.float32) * scale
    if len(cuts) > 0:
        array = shard_levels(rng, dims, cuts, -0.22, 0.18) * array
    return jnp.clip(array, min=-limit, max=limit).astype(held_as)


def setup_inputs(seed: int = 0) -> dict:
    splits = jax.random.split(jax.random.key(seed), 10)
    qkv = scatter_about(splits[0], (GROUPS, TILES, TILE_H, TILE_W, C3), 1.0, 6.0, ((0, 8), (1, 4)))
    cotangent = scatter_about(splits[1], (GROUPS, TILES, TILE_H, TILE_W, 2 * HEADS * HD), 8.0, 48.0, ((0, 8), (1, 4)))
    dw_weight = scatter_about(splits[2], (25, C3), 25 ** -0.5, 1.25, (), jnp.float32)
    pw_weight = scatter_about(splits[3], (HD, C3), HD ** -0.5, 1.0, (), jnp.float32)
    tile_image = draw_tile_image(jax.random.fold_in(splits[9], 71), 0)
    tile_row = draw_tile_row(jax.random.fold_in(splits[9], 71), 0)
    tile_col = draw_tile_col(jax.random.fold_in(splits[9], 71), 0)
    image_height = draw_image_height(jax.random.fold_in(splits[9], 71), 0)
    image_width = draw_image_width(jax.random.fold_in(splits[9], 71), 0)
    return dict(qkv=qkv, cotangent=cotangent, dw_weight=dw_weight, pw_weight=pw_weight, tile_image=tile_image, tile_row=tile_row, tile_col=tile_col, image_height=image_height, image_width=image_width)


PRECISE = lax.Precision.HIGHEST
EPSILON = 1e-06

def widen_tiles(source, is_live, grid_rows, grid_cols, tiles_tall, tiles_wide):
    tile_ids = jnp.arange(TILES).astype(jnp.int32)
    has_left = (is_live & (grid_cols > 0)).astype(jnp.float32)[:, None, None, None]
    has_right = (is_live & (grid_cols < tiles_wide - 1)).astype(jnp.float32)[:, None, None, None]
    has_above = (is_live & (grid_rows > 0)).astype(jnp.float32)[:, None, None, None]
    has_below = (is_live & (grid_rows < tiles_tall - 1)).astype(jnp.float32)[:, None, None, None]
    left_cols = source[jnp.clip(tile_ids - 1, 0, TILES - 1).astype(jnp.int32)][:, :, TILE_W - 2:] * has_left
    right_cols = source[jnp.clip(tile_ids + 1, 0, TILES - 1).astype(jnp.int32)][:, :, :2] * has_right
    widened = jnp.concatenate([left_cols, source, right_cols], axis=2)
    above_rows = widened[jnp.clip(tile_ids - tiles_wide, 0, TILES - 1).astype(jnp.int32)][:, TILE_H - 2:] * has_above
    below_rows = widened[jnp.clip(tile_ids + tiles_wide, 0, TILES - 1).astype(jnp.int32)][:, :2] * has_below
    return jnp.concatenate([above_rows, widened, below_rows], axis=1)

def attend(flat, image_slot):
    chans = HEADS * HD
    queries = jax.nn.relu(flat[..., :chans]).reshape(TILES, -1, HEADS, HD)
    key_rows = jax.nn.relu(flat[..., chans:2 * chans]).reshape(TILES, -1, HEADS, HD)
    values = flat[..., 2 * chans:].reshape(TILES, -1, HEADS, HD)
    onehot = (image_slot[:, None] == jnp.arange(MAXIMG)[None, :]).astype(jnp.float32)
    states = jnp.einsum('tphi,tphj->tihj', key_rows, values, precision=PRECISE)
    states = jnp.einsum('tm,tihj->mihj', onehot, states, precision=PRECISE)
    states = jnp.einsum('tm,mihj->tihj', onehot, states, precision=PRECISE)
    key_sums = jnp.einsum('tm,thi->mhi', onehot, lax.optimization_barrier(jnp.sum(key_rows, axis=1)), precision=PRECISE)
    key_sums = jnp.einsum('tm,mhi->thi', onehot, key_sums, precision=PRECISE)
    numerator = jnp.einsum('tphi,tihj->tphj', queries, states, precision=PRECISE)
    denominator = jnp.einsum('tphi,thi->tph', queries, key_sums, precision=PRECISE) + EPSILON
    return (numerator / denominator[..., None]).reshape(TILES, -1, chans)

def group_forward(source, dw_weight, pw_weight, image_slot, grid_rows, grid_cols, tiles_tall, tiles_wide):
    is_live = image_slot < MAXIMG
    padded = widen_tiles(source, is_live, grid_rows, grid_cols, tiles_tall, tiles_wide)
    mixed_dw = jnp.zeros_like(source)
    for row_off in range(5):
        for col_off in range(5):
            mixed_dw = mixed_dw + padded[:, row_off:row_off + TILE_H, col_off:col_off + TILE_W] * dw_weight[row_off * 5 + col_off]
    grouped = mixed_dw.reshape(TILES, TILE_H * TILE_W, 3 * HEADS, HD)
    merged = jnp.einsum('tpgi,igo->tpgo', grouped, pw_weight.reshape(HD, 3 * HEADS, HD), precision=PRECISE)
    merged = merged.reshape(TILES, TILE_H * TILE_W, C3)
    central = source.reshape(TILES, TILE_H * TILE_W, C3)
    return jnp.concatenate([attend(central, image_slot), attend(merged, image_slot)], axis=-1)

def reference(qkv, cotangent, dw_weight, pw_weight, tile_image, tile_row, tile_col, image_height, image_width):

    def per_group(running, packed):
        source, cot_tiles, image_slot, grid_rows, grid_cols, heights, widths = packed
        slot_index = jnp.minimum(image_slot, MAXIMG - 1).astype(jnp.int32)
        tiles_tall = heights[slot_index]
        tiles_wide = widths[slot_index]
        is_live = (image_slot < MAXIMG).astype(jnp.float32)[:, None, None, None]
        source = source.astype(jnp.float32) * is_live

        def forward_fn(src, dwk, pwk):
            return group_forward(src, dwk, pwk, image_slot, grid_rows, grid_cols, tiles_tall, tiles_wide)
        result, pullback = jax.vjp(forward_fn, source, dw_weight, pw_weight)
        grad_src, grad_dwk, grad_pwk = pullback(cot_tiles.astype(jnp.float32).reshape(result.shape))
        grad_src = grad_src * is_live
        return ((running[0] + grad_dwk, running[1] + grad_pwk), grad_src.astype(jnp.bfloat16))
    zeros_init = (jnp.zeros_like(dw_weight), jnp.zeros_like(pw_weight))
    (grad_dwk, grad_pwk), grad_src = lax.scan(per_group, zeros_init, (qkv, cotangent, tile_image, tile_row, tile_col, image_height, image_width))
    weight_norm = 1.0 / math.sqrt(GROUPS * TILES * TILE_H * TILE_W)
    return (grad_src, grad_dwk * weight_norm, grad_pwk * weight_norm)
```

```python
import functools
import math

import jax
import jax.numpy as jnp
from jax import lax
from jax.experimental import pallas as pl
from jax.experimental.pallas import tpu as pltpu
from jax.sharding import PartitionSpec as P

EPSILON = 1e-06
LANES = 256
REACH = 2
EDGE = 8
BF16 = jnp.bfloat16
F32 = jnp.float32
PARAMS = pltpu.CompilerParams(vmem_limit_bytes=40 * 1024 * 1024)
SMEM = pl.BlockSpec(memory_space=pltpu.SMEM)


class Place:
    def __init__(self, layout_refs):
        image_ref, row_ref, col_ref, tall_ref, wide_ref = layout_refs
        slot = image_ref[0, 0]
        slots = tall_ref.shape[1]
        tall = wide = start = jnp.int32(0)
        for s in range(slots):
            tall = jnp.where(slot == s, tall_ref[0, s], tall)
            wide = jnp.where(slot == s, wide_ref[0, s], wide)
            start = start + jnp.where(s < slot, tall_ref[0, s] * wide_ref[0, s], 0)
        self.live = slot < slots
        self.tall, self.wide = tall, wide
        self.row, self.col = row_ref[0, 0], col_ref[0, 0]
        self.within = self.row * wide + self.col
        self.index = start + self.within
        self.above = self.live & (self.row > 0)
        self.below = self.live & (self.row < tall - 1)

    def same_image(self, delta):
        other = self.within + delta
        return self.live & (other >= 0) & (other < self.tall * self.wide)


def halo_routes(count):
    if count == 4:
        return [
            ([(s, s ^ m) for s in range(count)], lambda t, m=m: (t ^ m) - t, lambda t, m=m: (t ^ m) - t)
            for m in range(1, count)
        ]
    routes = []
    for k in (1, -1, 2, -2, 3, -3):
        if abs(k) < count:
            pairs = [(s, s + k) for s in range(max(0, -k), min(count, count - k))]
            routes.append((pairs, lambda t, k=k: jnp.int32(k), lambda t, k=k: jnp.int32(-k)))
    return routes


def exchange(value, axis):
    count = lax.axis_size(axis)
    return [lax.ppermute(value, axis, [(s, s ^ m) for s in range(count)]) for m in range(1, count)]


def split(x):
    high = x.astype(BF16)
    return high, (x - high.astype(F32)).astype(BF16)


def contract(a, b, dims):
    return lax.dot_general(a, b, (dims, ((), ())), preferred_element_type=F32)


NN = ((1,), (0,))
NT = ((1,), (1,))
TN = ((0,), (0,))


def dot(a, b, dims):
    total = contract(a[0], b[0], dims)
    if b[1] is not None:
        total = total + contract(a[0], b[1], dims)
    if a[1] is not None:
        total = total + contract(a[1], b[0], dims)
    return total


def exact(x):
    return x.astype(BF16), None


def same_head(head_dim):
    rows = lax.broadcasted_iota(jnp.int32, (LANES, LANES), 0) // head_dim
    cols = lax.broadcasted_iota(jnp.int32, (LANES, LANES), 1) // head_dim
    return rows == cols


def spread(compact, mask):
    tall = jnp.concatenate([compact] * (LANES // compact.shape[0]), axis=0)
    return jnp.where(mask, tall, 0.0)


def gather_blocks(full, mask, head_dim):
    kept = jnp.where(mask, full, 0.0)
    return jnp.sum(kept.reshape(LANES // head_dim, head_dim, LANES), axis=0)


def payload(field, place, delta):
    tall, broad, lanes = field.shape
    size = REACH * broad
    top = field[:REACH].reshape(size, lanes)
    bottom = field[tall - REACH :].reshape(size, lanes)
    left = field[:, :EDGE].reshape(size, lanes)
    right = field[:, broad - EDGE :].reshape(size, lanes)
    rows = jnp.where(delta > 0, bottom, top)
    cols = jnp.where(place.col == 0, right, left)
    beside = (place.wide == 2) & (delta == jnp.where(place.col == 0, 1, -1))
    return jnp.where(beside, cols, rows)


def fill_padded(pad_ref, field, arrived_refs, deltas, place):
    tall, broad, lanes = field.shape
    full = tall + 2 * REACH
    pad_ref[:REACH] = jnp.zeros((REACH, broad + 2 * EDGE, lanes), F32)
    pad_ref[full - REACH :] = jnp.zeros((REACH, broad + 2 * EDGE, lanes), F32)
    pad_ref[REACH : REACH + tall, :EDGE] = jnp.zeros((tall, EDGE, lanes), F32)
    pad_ref[REACH : REACH + tall, EDGE + broad :] = jnp.zeros((tall, EDGE, lanes), F32)
    pad_ref[REACH : REACH + tall, EDGE : EDGE + broad] = field
    two = place.live & (place.wide == 2)
    one = place.live & (place.wide == 1)
    first, second = two & (place.col == 0), two & (place.col == 1)
    upper, lower = slice(0, REACH), slice(full - REACH, full)
    before, after = slice(0, EDGE), slice(EDGE + broad, 2 * EDGE + broad)
    for arrived_ref, delta in zip(arrived_refs, deltas):

        def rows(arrived_ref=arrived_ref):
            return arrived_ref[0].astype(F32).reshape(REACH, broad, lanes)

        def cols(arrived_ref=arrived_ref):
            return arrived_ref[0].astype(F32).reshape(tall, EDGE, lanes)

        def put(condition, where_rows, where_cols, value):
            @pl.when(condition)
            def _():
                pad_ref[where_rows, where_cols] = value()

        middle, height = slice(EDGE, EDGE + broad), slice(REACH, REACH + tall)
        put(place.above & ((one & (delta == -1)) | (two & (delta == -2))), upper, middle, rows)
        put(place.below & ((one & (delta == 1)) | (two & (delta == 2))), lower, middle, rows)
        put(second & (delta == -1), height, before, cols)
        put(first & (delta == 1), height, after, cols)
        put(place.above & first & (delta == -1), upper, after, lambda r=rows: r()[:, :EDGE])
        put(place.above & second & (delta == -3), upper, before, lambda r=rows: r()[:, broad - EDGE :])
        put(place.below & second & (delta == 1), lower, before, lambda r=rows: r()[:, broad - EDGE :])
        put(place.below & first & (delta == 3), lower, after, lambda r=rows: r()[:, :EDGE])


def fill_shifted(shift_ref, pad_ref):
    full, broad = shift_ref.shape[1:3]
    first = EDGE - REACH
    for y in range(full):
        for b in range(2 * REACH + 1):
            shift_ref[b, y] = pad_ref[y, first + b : first + b + broad]


def convolve(shift_ref, kernel_ref, y, flipped):
    taps = 2 * REACH + 1
    total = None
    for a in range(taps):
        for b in range(taps):
            tap = taps * a + b
            if flipped:
                tap = taps * taps - 1 - tap
            term = shift_ref[b, y + a] * kernel_ref[tap : tap + 1]
            total = term if total is None else total + term
    return total


def outgoing_kernel(routes, *refs):
    layout, field_ref, outs = refs[:5], refs[5], refs[6:]
    place = Place(layout)
    field = field_ref[0, 0].astype(F32)
    for (_, target, _), out_ref in zip(routes, outs):
        out_ref[0] = payload(field, place, target(place.index)).astype(BF16)


def forward_kernel(routes, per, head_dim, *refs):
    count = len(routes)
    layout, field_ref = refs[:5], refs[5]
    arrived = refs[6 : 6 + count]
    dw_ref, pw_ref, mixed_ref, merged_ref, state_ref, pad_ref, shift_ref, mix_ref, key0, key1 = refs[
        6 + count :
    ]
    step = pl.program_id(0)
    place = Place(layout)
    tall, broad = field_ref.shape[2:4]
    field = jnp.where(place.live, field_ref[0, 0].astype(F32), 0.0)
    fill_padded(pad_ref, field, arrived, [source(place.index) for _, _, source in routes], place)
    fill_shifted(shift_ref, pad_ref)

    def one_row(y, carry):
        mix_ref[y] = convolve(shift_ref, dw_ref, y, False)
        return carry

    lax.fori_loop(0, tall, one_row, 0)
    mixed = mix_ref[...].reshape(tall * broad, LANES)
    mixed_ref[...] = mixed
    mask = same_head(head_dim)
    blocks = split(spread(pw_ref[...], mask))
    merged = dot(split(mixed), blocks, NN)
    merged_ref[...] = merged
    flat = field.reshape(tall * broad, LANES)
    for part in range(per):

        @pl.when(step == per + part)
        def _():
            keys0, keys1 = jnp.maximum(flat, 0.0), jnp.maximum(merged, 0.0)
            key0[part] = keys0.astype(BF16)
            key1[part] = keys1
            lanes = slice(part * LANES, (part + 1) * LANES)
            state_ref[2 * head_dim :, lanes] = jnp.concatenate(
                [
                    jnp.sum(keys0, axis=0, keepdims=True),
                    jnp.sum(keys1, axis=0, keepdims=True),
                    jnp.zeros((6, LANES), F32),
                ],
                axis=0,
            )

        @pl.when(step == 2 * per + part)
        def _():
            lanes = slice(part * LANES, (part + 1) * LANES)
            state0 = contract(key0[part], flat.astype(BF16), TN)
            state1 = dot(split(key1[part]), split(merged), TN)
            state_ref[:head_dim, lanes] = gather_blocks(state0, mask, head_dim)
            state_ref[head_dim : 2 * head_dim, lanes] = gather_blocks(state1, mask, head_dim)


def total_of(own_ref, others, place):
    total = own_ref[...]
    for m, other in enumerate(others, 1):
        delta = (place.index ^ m) - place.index
        total = total + jnp.where(place.same_image(delta), other[...], 0.0)
    return total


def query_kernel(others, head_dim, *refs):
    layout, own_ref, received = refs[:5], refs[5], refs[6 : 6 + others]
    (source_ref, merged_ref, mixed_ref, cot0_ref, cot1_ref, pw_ref) = refs[6 + others : 12 + others]
    gstate_ref, grad0_ref, gmix_ref, gpw_ref = refs[12 + others :]
    place = Place(layout)
    total = total_of(own_ref, received, place)
    mask = same_head(head_dim)
    ones = (mask.astype(BF16), None)
    positions = merged_ref.shape[0]
    raw0 = jnp.where(place.live, source_ref[0, 0].astype(F32), 0.0).reshape(positions, LANES)
    sums = []
    for scale in range(2):
        raw = raw0 if scale == 0 else merged_ref[...]
        cot_ref = cot0_ref if scale == 0 else cot1_ref
        query = jnp.maximum(raw, 0.0)
        pair = exact(query) if scale == 0 else split(query)
        state = split(spread(total[scale * head_dim : (scale + 1) * head_dim], mask))
        key_sum = total[2 * head_dim + scale : 2 * head_dim + scale + 1]
        cot = cot_ref[0, 0].astype(F32).reshape(positions, LANES)
        over = 1.0 / (dot(split(query * key_sum), ones, NN) + EPSILON)
        result = dot(pair, state, NN) * over
        grad_num = cot * over
        grad_den = -dot(split(cot * result), ones, NN) * over
        num_pair = split(grad_num)
        grad = dot(num_pair, state, NT) + grad_den * key_sum
        grad = jnp.where(raw > 0, grad, 0.0)
        gstate = dot(pair, num_pair, TN)
        gstate_ref[scale * head_dim : (scale + 1) * head_dim] = gather_blocks(gstate, mask, head_dim)
        sums.append(jnp.sum(query * grad_den, axis=0, keepdims=True))
        if scale == 0:
            grad0_ref[...] = grad
        else:
            grad_pair = split(grad)
            gmix_ref[...] = dot(grad_pair, split(spread(pw_ref[...], mask)), NT)
            gpw_ref[...] = gather_blocks(dot(split(mixed_ref[...]), grad_pair, TN), mask, head_dim)
    gstate_ref[2 * head_dim :] = jnp.concatenate(sums + [jnp.zeros((6, LANES), F32)], axis=0)


def value_kernel(others, routes, head_dim, *refs):
    layout, own_ref, received = refs[:5], refs[5], refs[6 : 6 + others]
    refs = refs[6 + others :]
    (ksource_ref, vsource_ref, kmerged_ref, vmerged_ref, kmixed_ref, vmixed_ref) = refs[:6]
    (kpw_ref, vpw_ref, qgrad0_ref, qgmix_ref, qgpw_ref) = refs[6:11]
    grad0_ref, gmix_ref, gpw_ref = refs[11:14]
    outs = refs[14:]
    place = Place(layout)
    total = total_of(own_ref, received, place)
    mask = same_head(head_dim)
    positions = kmerged_ref.shape[0]
    tall, broad = ksource_ref.shape[2:4]
    grad0_ref[0] = qgrad0_ref[...]
    gmix_ref[0] = qgmix_ref[...]
    gpw_ref[0] = qgpw_ref[...]
    for scale in range(2):
        gstate = split(spread(total[scale * head_dim : (scale + 1) * head_dim], mask))
        gsum = total[2 * head_dim + scale : 2 * head_dim + scale + 1]
        if scale == 0:
            raw = jnp.where(place.live, ksource_ref[0, 0].astype(F32), 0.0).reshape(positions, LANES)
            values = jnp.where(place.live, vsource_ref[0, 0].astype(F32), 0.0).reshape(positions, LANES)
            key_pair, value_pair = exact(jnp.maximum(raw, 0.0)), exact(values)
        else:
            raw = kmerged_ref[...]
            key_pair, value_pair = split(jnp.maximum(raw, 0.0)), split(vmerged_ref[...])
        grad_keys = jnp.where(raw > 0, dot(value_pair, gstate, NT) + gsum, 0.0)
        grad_values = dot(key_pair, gstate, NN)
        if scale == 0:
            grad0_ref[1] = grad_keys
            grad0_ref[2] = grad_values
        else:
            for member, grad, mixed_ref, pw_ref in (
                (1, grad_keys, kmixed_ref, kpw_ref),
                (2, grad_values, vmixed_ref, vpw_ref),
            ):
                pair = split(grad)
                gmix_ref[member] = dot(pair, split(spread(pw_ref[...], mask)), NT)
                gpw_ref[member] = gather_blocks(dot(split(mixed_ref[...]), pair, TN), mask, head_dim)
    for (_, target, _), out_ref in zip(routes, outs):
        delta = target(place.index)
        for member in range(3):
            field = gmix_ref[member].reshape(tall, broad, LANES)
            out_ref[member] = payload(field, place, delta).astype(BF16)


def weight_kernel(routes, *refs):
    count = len(routes)
    layout, field_ref = refs[:5], refs[5]
    arrived = refs[6 : 6 + count]
    gmix_ref, gpw_ref, out_ref, pad_ref, shift_ref = refs[6 + count :]
    place = Place(layout)
    tall, broad = field_ref.shape[2:4]
    field = jnp.where(place.live, field_ref[0, 0].astype(F32), 0.0)
    fill_padded(pad_ref, field, arrived, [source(place.index) for _, _, source in routes], place)
    fill_shifted(shift_ref, pad_ref)
    taps = 2 * REACH + 1
    sub = 128
    for part in range(LANES // sub):
        lanes = slice(part * sub, (part + 1) * sub)

        def one_row(y, totals):
            grad = gmix_ref[0, pl.ds(pl.multiple_of(y * broad, broad), broad), lanes]
            new = []
            for a in range(taps):
                for b in range(taps):
                    term = shift_ref[b, y + a, :, lanes] * grad
                    new.append(totals[taps * a + b] + jnp.sum(term.reshape(broad // 8, 8, sub), axis=0))
            return tuple(new)

        zero = jnp.zeros((8, sub), F32)
        totals = lax.fori_loop(0, tall, one_row, (zero,) * (taps * taps))
        for tap in range(taps * taps):
            out_ref[tap : tap + 1, lanes] = jnp.sum(totals[tap], axis=0, keepdims=True)
    head_dim = gpw_ref.shape[1]
    start = out_ref.shape[0] - head_dim
    out_ref[taps * taps : start] = jnp.zeros((start - taps * taps, LANES), F32)
    out_ref[start:] = gpw_ref[0]


def backward_kernel(routes, *refs):
    count = len(routes)
    layout, gmix_ref = refs[:5], refs[5]
    arrived = refs[6 : 6 + count]
    dw_ref, grad0_ref, out_ref, pad_ref, shift_ref = refs[6 + count :]
    place = Place(layout)
    tall, broad = out_ref.shape[2:4]
    field = gmix_ref[0].reshape(tall, broad, LANES)
    fill_padded(pad_ref, field, arrived, [source(place.index) for _, _, source in routes], place)
    fill_shifted(shift_ref, pad_ref)

    def one_row(y, carry):
        grad = convolve(shift_ref, dw_ref, y, True)
        grad = grad + grad0_ref[0, pl.ds(pl.multiple_of(y * broad, broad), broad)]
        out_ref[0, 0, y] = jnp.where(place.live, grad, 0.0).astype(BF16)
        return carry

    lax.fori_loop(0, tall, one_row, 0)


def tile_spec(tall, broad, at):
    return pl.BlockSpec((1, 1, tall, broad, LANES), lambda j: (0, 0, 0, 0, at(j)))


def call(kernel, grid, in_specs, out_specs, out_shape, scratch, flops, moved):
    return pl.pallas_call(
        kernel,
        grid=(grid,),
        in_specs=in_specs,
        out_specs=out_specs,
        out_shape=out_shape,
        scratch_shapes=scratch,
        compiler_params=PARAMS,
        cost_estimate=pl.CostEstimate(flops=flops, bytes_accessed=moved, transcendentals=0),
    )


def local(
    qkv, cotangent, dw_weight, pw_weight, tile_image, tile_row, tile_col, image_height, image_width
):
    tall, broad, channels = qkv.shape[2:]
    positions = tall * broad
    head_dim = pw_weight.shape[0]
    taps = dw_weight.shape[0]
    third = channels // 3
    per = third // LANES
    steps = 3 * per
    tiles, groups = lax.axis_size("tile"), lax.axis_size("img")
    routes = halo_routes(tiles)
    layout = (tile_image, tile_row, tile_col, image_height, image_width)
    layout_specs = [SMEM] * 5
    shape = jax.ShapeDtypeStruct
    edge = REACH * broad
    state_rows = 2 * head_dim + 8

    same = lambda j: j
    flat_spec = lambda rows, at=same: pl.BlockSpec((rows, LANES), lambda j: (0, at(j)))
    member_spec = lambda rows: pl.BlockSpec((1, rows, LANES), lambda j: (j // per, 0, j % per))
    trio_spec = lambda rows: pl.BlockSpec((3, rows, LANES), lambda j: (0, 0, j))
    pad_scratch = [
        pltpu.VMEM((tall + 2 * REACH, broad + 2 * EDGE, LANES), F32),
        pltpu.VMEM((2 * REACH + 1, tall + 2 * REACH, broad, LANES), F32),
    ]
    conv_flops = 2 * taps * positions * channels

    sent = call(
        functools.partial(outgoing_kernel, routes),
        steps,
        layout_specs + [tile_spec(tall, broad, same)],
        [member_spec(edge)] * len(routes),
        [shape((3, edge, third), BF16)] * len(routes),
        [],
        positions * channels,
        2 * positions * channels,
    )(*layout, qkv)
    halo = [lax.ppermute(part, "tile", pairs) for part, (pairs, _, _) in zip(sent, routes)]

    mixed, merged, state = call(
        functools.partial(forward_kernel, routes, per, head_dim),
        steps,
        layout_specs
        + [tile_spec(tall, broad, same)]
        + [member_spec(edge)] * len(routes)
        + [flat_spec(taps), flat_spec(head_dim)],
        [flat_spec(positions), flat_spec(positions), pl.BlockSpec((state_rows, third), lambda j: (0, 0))],
        [
            shape((positions, channels), F32),
            shape((positions, channels), F32),
            shape((state_rows, third), F32),
        ],
        pad_scratch
        + [
            pltpu.VMEM((tall, broad, LANES), F32),
            pltpu.VMEM((per, positions, LANES), BF16),
            pltpu.VMEM((per, positions, LANES), F32),
        ],
        conv_flops * 4,
        12 * positions * channels,
    )(*layout, qkv, *halo, dw_weight, pw_weight)

    received = exchange(state, "tile")
    others = len(received)
    gstate, qgrad0, qgmix, qgpw = call(
        functools.partial(query_kernel, others, head_dim),
        per,
        layout_specs
        + [flat_spec(state_rows)] * (1 + others)
        + [tile_spec(tall, broad, same), flat_spec(positions), flat_spec(positions)]
        + [tile_spec(tall, broad, same), tile_spec(tall, broad, lambda j: j + per), flat_spec(head_dim)],
        [flat_spec(state_rows), flat_spec(positions), flat_spec(positions), flat_spec(head_dim)],
        [
            shape((state_rows, third), F32),
            shape((positions, third), F32),
            shape((positions, third), F32),
            shape((head_dim, third), F32),
        ],
        [],
        conv_flops,
        8 * positions * channels,
    )(*layout, state, *received, qkv, merged, mixed, cotangent, cotangent, pw_weight)

    received = exchange(gstate, "tile")
    k_at, v_at = (lambda j: j + per), (lambda j: j + 2 * per)
    results = call(
        functools.partial(value_kernel, others, routes, head_dim),
        per,
        layout_specs
        + [flat_spec(state_rows)] * (1 + others)
        + [tile_spec(tall, broad, k_at), tile_spec(tall, broad, v_at)]
        + [flat_spec(positions, k_at), flat_spec(positions, v_at)] * 2
        + [flat_spec(head_dim, k_at), flat_spec(head_dim, v_at)]
        + [flat_spec(positions), flat_spec(positions), flat_spec(head_dim)],
        [trio_spec(positions), trio_spec(positions), trio_spec(head_dim)] + [trio_spec(edge)] * len(routes),
        [
            shape((3, positions, third), F32),
            shape((3, positions, third), F32),
            shape((3, head_dim, third), F32),
        ]
        + [shape((3, edge, third), BF16)] * len(routes),
        [],
        conv_flops,
        16 * positions * channels,
    )(
        *layout, gstate, *received, qkv, qkv, merged, merged, mixed, mixed, pw_weight, pw_weight,
        qgrad0, qgmix, qgpw,
    )
    grad0, gmix, gpw = results[:3]
    grad_halo = [lax.ppermute(part, "tile", pairs) for part, (pairs, _, _) in zip(results[3:], routes)]

    gap = -(-taps // 8) * 8
    rows = gap + head_dim
    weights = call(
        functools.partial(weight_kernel, routes),
        steps,
        layout_specs
        + [tile_spec(tall, broad, same)]
        + [member_spec(edge)] * len(routes)
        + [member_spec(positions), member_spec(head_dim)],
        flat_spec(rows),
        shape((rows, channels), F32),
        pad_scratch,
        conv_flops * 4,
        8 * positions * channels,
    )(*layout, qkv, *halo, gmix, gpw)

    padded_rows = -(-rows // groups) * groups
    weights = jnp.pad(weights, ((0, padded_rows - rows), (0, 0)))
    parts = lax.all_to_all(weights.reshape(groups, padded_rows // groups, channels), "img", 0, 0)
    sums = [jnp.sum(parts, axis=0)]
    sums = sums + exchange(sums[0], "tile")
    while len(sums) > 1:
        sums = [sums[i] + sums[i + 1] for i in range(0, len(sums), 2)]
    norm = 1.0 / math.sqrt(positions * tiles * groups)
    share = (sums[0] * norm).astype(BF16)
    shares = lax.all_to_all(jnp.broadcast_to(share[None], (groups,) + share.shape), "img", 0, 0)
    whole = shares.reshape(padded_rows, channels).astype(F32)

    grad_source = call(
        functools.partial(backward_kernel, routes),
        steps,
        layout_specs
        + [member_spec(positions)]
        + [member_spec(edge)] * len(routes)
        + [flat_spec(taps), member_spec(positions)],
        tile_spec(tall, broad, same),
        shape((1, 1, tall, broad, channels), BF16),
        pad_scratch,
        conv_flops * 4,
        10 * positions * channels,
    )(*layout, gmix, *grad_halo, dw_weight, grad0)
    return grad_source, whole[:taps], whole[gap : gap + head_dim]


def solution(mesh):
    placed = (
        P("img", "tile", None, None, None),
        P("img", "tile", None, None, None),
        P(),
        P(),
        P("img", "tile"),
        P("img", "tile"),
        P("img", "tile"),
        P("img", None),
        P("img", None),
    )
    return jax.shard_map(
        local,
        mesh=mesh,
        in_specs=placed,
        out_specs=(P("img", "tile", None, None, None), P(), P()),
        check_vma=False,
    )
```

```python
import functools
import math

import jax
import jax.numpy as jnp
from jax import lax
from jax.experimental import pallas as pl
from jax.experimental.pallas import tpu as pltpu
from jax.sharding import PartitionSpec as P

EPSILON = 1e-06
LANES = 256
REACH = 2
EDGE = 8
COST = 1000
BF16 = jnp.bfloat16
F32 = jnp.float32
PARAMS = pltpu.CompilerParams(vmem_limit_bytes=16 * 1024 * 1024)
SMEM = pl.BlockSpec(memory_space=pltpu.SMEM)


class Place:
    def __init__(self, layout_refs):
        image_ref, row_ref, col_ref, tall_ref, wide_ref = layout_refs
        slot = image_ref[0, 0]
        slots = tall_ref.shape[1]
        tall = wide = start = jnp.int32(0)
        for s in range(slots):
            tall = jnp.where(slot == s, tall_ref[0, s], tall)
            wide = jnp.where(slot == s, wide_ref[0, s], wide)
            start = start + jnp.where(s < slot, tall_ref[0, s] * wide_ref[0, s], 0)
        self.live = slot < slots
        self.tall, self.wide = tall, wide
        self.row, self.col = row_ref[0, 0], col_ref[0, 0]
        self.within = self.row * wide + self.col
        self.index = start + self.within
        self.above = self.live & (self.row > 0)
        self.below = self.live & (self.row < tall - 1)

    def same_image(self, delta):
        other = self.within + delta
        return self.live & (other >= 0) & (other < self.tall * self.wide)


class Routes:
    def __init__(self, count):
        self.count = count
        self.relayed = count == 4
        self.shifts = [k for k in (1, -1, 2, -2, 3, -3) if abs(k) < count]
        self.sent = 2 if self.relayed else len(self.shifts)
        self.arriving = 3 if self.relayed else len(self.shifts)

    def targets(self, place):
        if not self.relayed:
            return [jnp.int32(k) for k in self.shifts]
        near, far, last = ((place.index ^ m) - place.index for m in (1, 2, 3))
        return [near, jnp.where(place.same_image(far), far, last)]

    def sources(self, place):
        if not self.relayed:
            return [jnp.int32(-k) for k in self.shifts]
        return [(place.index ^ m) - place.index for m in (1, 2, 3)]

    def move(self, sent):
        count = self.count
        if not self.relayed:
            return [
                lax.ppermute(part, "tile", [(s, s + k) for s in range(max(0, -k), min(count, count - k))])
                for part, k in zip(sent, self.shifts)
            ]
        near, far = (
            lax.ppermute(part, "tile", [(s, s ^ m) for s in range(count)]) for part, m in zip(sent, (1, 2))
        )
        return [near, far, lax.ppermute(far, "tile", [(s, s ^ 1) for s in range(count)])]


def exchange(value, axis, masks=None):
    count = lax.axis_size(axis)
    masks = range(1, count) if masks is None else masks
    return [lax.ppermute(value, axis, [(s, s ^ m) for s in range(count)]) for m in masks]


def split(x):
    high = x.astype(BF16)
    return high, (x - high.astype(F32)).astype(BF16)


def contract(a, b, dims):
    return lax.dot_general(a, b, (dims, ((), ())), preferred_element_type=F32)


NN = ((1,), (0,))
NT = ((1,), (1,))
TN = ((0,), (0,))


def dot(a, b, dims):
    total = contract(a[0], b[0], dims)
    if b[1] is not None:
        total = total + contract(a[0], b[1], dims)
    if a[1] is not None:
        total = total + contract(a[1], b[0], dims)
    return total


def exact(x):
    return x.astype(BF16), None


def same_head(head_dim):
    rows = lax.broadcasted_iota(jnp.int32, (LANES, LANES), 0) // head_dim
    cols = lax.broadcasted_iota(jnp.int32, (LANES, LANES), 1) // head_dim
    return rows == cols


def spread(compact, mask):
    tall = jnp.concatenate([compact] * (LANES // compact.shape[0]), axis=0)
    return jnp.where(mask, tall, 0.0)


def gather_blocks(full, mask, head_dim):
    kept = jnp.where(mask, full, 0.0)
    return jnp.sum(kept.reshape(LANES // head_dim, head_dim, LANES), axis=0)


def payload(field, place, delta):
    tall, broad, lanes = field.shape
    size = REACH * broad
    top = field[:REACH].reshape(size, lanes)
    bottom = field[tall - REACH :].reshape(size, lanes)
    left = field[:, :EDGE].reshape(size, lanes)
    right = field[:, broad - EDGE :].reshape(size, lanes)
    rows = jnp.where(delta > 0, bottom, top)
    cols = jnp.where(place.col == 0, right, left)
    beside = (place.wide == 2) & (delta == jnp.where(place.col == 0, 1, -1))
    return jnp.where(beside, cols, rows)


def edge_of(ref, size):
    rows = ref[0] if len(ref.shape) == 3 else ref[:size]
    return rows.astype(F32)


def pack_state(state, total):
    rows = jnp.concatenate([state, total, jnp.zeros((7, LANES), F32)], axis=0)
    return jnp.concatenate(split(rows), axis=0)


def unpack_state(ref, offset):
    rows = ref[offset:].astype(F32)
    half = rows.shape[0] // 2
    return rows[:half] + rows[half:]


def total_state(own_ref, others, place, offset, others_offset):
    total = unpack_state(own_ref, offset)
    for m, other in enumerate(others, 1):
        delta = (place.index ^ m) - place.index
        total = total + jnp.where(place.same_image(delta), unpack_state(other, others_offset), 0.0)
    return total


def fill_padded(pad_ref, field, arrived_refs, deltas, place):
    tall, broad, lanes = field.shape
    full = tall + 2 * REACH
    pad_ref[:REACH] = jnp.zeros((REACH, broad + 2 * EDGE, lanes), F32)
    pad_ref[full - REACH :] = jnp.zeros((REACH, broad + 2 * EDGE, lanes), F32)
    pad_ref[REACH : REACH + tall, :EDGE] = jnp.zeros((tall, EDGE, lanes), F32)
    pad_ref[REACH : REACH + tall, EDGE + broad :] = jnp.zeros((tall, EDGE, lanes), F32)
    pad_ref[REACH : REACH + tall, EDGE : EDGE + broad] = field
    two = place.live & (place.wide == 2)
    one = place.live & (place.wide == 1)
    first, second = two & (place.col == 0), two & (place.col == 1)
    upper, lower = slice(0, REACH), slice(full - REACH, full)
    before, after = slice(0, EDGE), slice(EDGE + broad, 2 * EDGE + broad)
    for arrived_ref, delta in zip(arrived_refs, deltas):

        def rows(arrived_ref=arrived_ref):
            return edge_of(arrived_ref, REACH * broad).reshape(REACH, broad, lanes)

        def cols(arrived_ref=arrived_ref):
            return edge_of(arrived_ref, REACH * broad).reshape(tall, EDGE, lanes)

        def put(condition, where_rows, where_cols, value):
            @pl.when(condition)
            def _():
                pad_ref[where_rows, where_cols] = value()

        middle, height = slice(EDGE, EDGE + broad), slice(REACH, REACH + tall)
        put(place.above & ((one & (delta == -1)) | (two & (delta == -2))), upper, middle, rows)
        put(place.below & ((one & (delta == 1)) | (two & (delta == 2))), lower, middle, rows)
        put(second & (delta == -1), height, before, cols)
        put(first & (delta == 1), height, after, cols)
        put(place.above & first & (delta == -1), upper, after, lambda r=rows: r()[:, :EDGE])
        put(place.above & second & (delta == -3), upper, before, lambda r=rows: r()[:, broad - EDGE :])
        put(place.below & second & (delta == 1), lower, before, lambda r=rows: r()[:, broad - EDGE :])
        put(place.below & first & (delta == 3), lower, after, lambda r=rows: r()[:, :EDGE])


def fill_shifted(shift_ref, pad_ref):
    full, broad = shift_ref.shape[1:3]
    first = EDGE - REACH
    for y in range(full):
        for b in range(2 * REACH + 1):
            shift_ref[b, y] = pad_ref[y, first + b : first + b + broad]


def convolve(shift_ref, kernel_ref, y, flipped):
    taps = 2 * REACH + 1
    total = None
    for a in range(taps):
        for b in range(taps):
            tap = taps * a + b
            if flipped:
                tap = taps * taps - 1 - tap
            term = shift_ref[b, y + a] * kernel_ref[tap : tap + 1]
            total = term if total is None else total + term
    return total


def read_field(ref, place):
    return jnp.where(place.live, ref[0, 0].astype(F32), 0.0)


def outgoing_kernel(routes, *refs):
    layout, field_ref, outs = refs[:5], refs[5], refs[6:]
    place = Place(layout)
    field = field_ref[0, 0].astype(F32)
    for delta, out_ref in zip(routes.targets(place), outs):
        out_ref[0] = payload(field, place, delta).astype(BF16)


def source_state_kernel(routes, head_dim, *refs):
    layout, (query_ref, key_ref, value_ref), outs = refs[:5], refs[5:8], refs[8:]
    place = Place(layout)
    field = query_ref[0, 0].astype(F32)
    size = REACH * field.shape[1]
    positions = field.shape[0] * field.shape[1]
    keys = jnp.maximum(read_field(key_ref, place), 0.0).reshape(positions, LANES)
    values = read_field(value_ref, place).reshape(positions, LANES)
    state = contract(keys.astype(BF16), values.astype(BF16), TN)
    state = gather_blocks(state, same_head(head_dim), head_dim)
    packed = pack_state(state, jnp.sum(keys, axis=0, keepdims=True))
    for delta, out_ref in zip(routes.targets(place), outs):
        out_ref[:size] = payload(field, place, delta).astype(BF16)
        out_ref[size:] = packed


def convolve_all(routes, place, field, arrived, pad_ref, shift_ref, mix_ref, kernel_ref, flipped):
    fill_padded(pad_ref, field, arrived, routes.sources(place), place)
    fill_shifted(shift_ref, pad_ref)

    def one_row(y, carry):
        mix_ref[y] = convolve(shift_ref, kernel_ref, y, flipped)
        return carry

    lax.fori_loop(0, field.shape[0], one_row, 0)


def forward_kernel(routes, per, head_dim, with_state, *refs):
    count = routes.arriving
    layout, field_ref = refs[:5], refs[5]
    arrived = refs[6 : 6 + count]
    refs = refs[6 + count :]
    dw_ref, pw_ref, mixed_ref, merged_ref = refs[:4]
    if with_state:
        state_ref, pad_ref, shift_ref, mix_ref, key_ref = refs[4:]
    else:
        pad_ref, shift_ref, mix_ref = refs[4:]
    step = pl.program_id(0)
    place = Place(layout)
    field = read_field(field_ref, place)
    convolve_all(routes, place, field, arrived, pad_ref, shift_ref, mix_ref, dw_ref, False)
    mixed = mix_ref[...].reshape(-1, LANES)
    mixed_ref[0] = mixed
    mask = same_head(head_dim)
    merged = dot(split(mixed), split(spread(pw_ref[...], mask)), NN)
    merged_ref[0] = merged
    if not with_state:
        return
    for part in range(per):

        @pl.when(step == part)
        def _():
            key_ref[part] = jnp.maximum(merged, 0.0)

        @pl.when(step == per + part)
        def _():
            keys = key_ref[part]
            state = gather_blocks(dot(split(keys), split(merged), TN), mask, head_dim)
            lanes = slice(part * LANES, (part + 1) * LANES)
            state_ref[:, lanes] = pack_state(state, jnp.sum(keys, axis=0, keepdims=True))


def query_gradients(raw, exactly, total, cot_ref, head_dim, mask):
    ones = (mask.astype(BF16), None)
    query = jnp.maximum(raw, 0.0)
    pair = exact(query) if exactly else split(query)
    state = split(spread(total[:head_dim], mask))
    key_sum = total[head_dim : head_dim + 1]
    cot = cot_ref[0, 0].astype(F32).reshape(raw.shape)
    over = 1.0 / (dot(split(query * key_sum), ones, NN) + EPSILON)
    result = dot(pair, state, NN) * over
    grad_num = cot * over
    grad_den = -dot(split(cot * result), ones, NN) * over
    num_pair = split(grad_num)
    grad = jnp.where(raw > 0, dot(num_pair, state, NT) + grad_den * key_sum, 0.0)
    gstate = gather_blocks(dot(pair, num_pair, TN), mask, head_dim)
    return grad, pack_state(gstate, jnp.sum(query * grad_den, axis=0, keepdims=True))


def source_query_kernel(others, offset, others_offset, head_dim, *refs):
    layout, own_ref, received = refs[:5], refs[5], refs[6 : 6 + others]
    source_ref, cot_ref, grad_ref, gstate_ref = refs[6 + others :]
    place = Place(layout)
    total = total_state(own_ref, received, place, offset, others_offset)
    raw = read_field(source_ref, place).reshape(-1, LANES)
    grad_ref[0], gstate_ref[...] = query_gradients(raw, True, total, cot_ref, head_dim, same_head(head_dim))


def merged_query_kernel(others, routes, head_dim, *refs):
    layout, own_ref, received = refs[:5], refs[5], refs[6 : 6 + others]
    refs = refs[6 + others :]
    merged_ref, mixed_ref, cot_ref, pw_ref, packed_ref, gstate_ref, gmix_ref, gpw_ref = refs[:8]
    outs = refs[8:]
    tall, broad = cot_ref.shape[2:4]
    place = Place(layout)
    mask = same_head(head_dim)
    total = total_state(own_ref, received, place, 0, 0)
    grad, gstate_ref[...] = query_gradients(merged_ref[0], False, total, cot_ref, head_dim, mask)
    pair = split(grad)
    gmix = dot(pair, split(spread(pw_ref[...], mask)), NT)
    gmix_ref[0] = gmix
    gpw_ref[0] = gather_blocks(dot(split(mixed_ref[0]), pair, TN), mask, head_dim)
    field = gmix.reshape(tall, broad, LANES)
    for delta, out_ref in zip(routes.targets(place), outs):
        out_ref[: REACH * broad] = payload(field, place, delta).astype(BF16)
        out_ref[REACH * broad :] = packed_ref[...]


def key_gradients(raw, key_pair, value_pair, total, head_dim, mask):
    gstate = split(spread(total[:head_dim], mask))
    gsum = total[head_dim : head_dim + 1]
    grad_keys = jnp.where(raw > 0, dot(value_pair, gstate, NT) + gsum, 0.0)
    return grad_keys, dot(key_pair, gstate, NN)


def source_value_kernel(others, offset, others_offset, head_dim, *refs):
    layout, own_ref, received = refs[:5], refs[5], refs[6 : 6 + others]
    key_ref, value_ref, grad_ref = refs[6 + others :]
    place = Place(layout)
    total = total_state(own_ref, received, place, offset, others_offset)
    raw = read_field(key_ref, place).reshape(-1, LANES)
    values = read_field(value_ref, place).reshape(-1, LANES)
    grad_ref[0], grad_ref[1] = key_gradients(
        raw, exact(jnp.maximum(raw, 0.0)), exact(values), total, head_dim, same_head(head_dim)
    )


def merged_value_kernel(others, routes, tall, head_dim, *refs):
    layout, own_ref, received = refs[:5], refs[5], refs[6 : 6 + others]
    merged_ref, mixed_ref, kpw_ref, vpw_ref, gmix_ref, gpw_ref = refs[6 + others : 12 + others]
    outs = refs[12 + others :]
    place = Place(layout)
    mask = same_head(head_dim)
    total = total_state(own_ref, received, place, 0, 0)
    raw = merged_ref[0]
    grads = key_gradients(raw, split(jnp.maximum(raw, 0.0)), split(merged_ref[1]), total, head_dim, mask)
    for member, (grad, pw_ref) in enumerate(zip(grads, (kpw_ref, vpw_ref))):
        pair = split(grad)
        gmix = dot(pair, split(spread(pw_ref[...], mask)), NT)
        gmix_ref[member] = gmix
        gpw_ref[member] = gather_blocks(dot(split(mixed_ref[member]), pair, TN), mask, head_dim)
        field = gmix.reshape(tall, -1, LANES)
        for delta, out_ref in zip(routes.targets(place), outs):
            out_ref[member] = payload(field, place, delta).astype(BF16)


def weight_kernel(routes, halves, *refs):
    count = routes.arriving
    layout, field_ref = refs[:5], refs[5]
    arrived = refs[6 : 6 + count]
    refs = refs[6 + count :]
    gmix_ref, gpw_ref, spot_ref = refs[:3]
    outs, (pad_ref, shift_ref, sum_ref) = refs[3:-3], refs[-3:]
    place = Place(layout)
    field = read_field(field_ref, place)
    tall, broad = field.shape[:2]
    fill_padded(pad_ref, field, arrived, routes.sources(place), place)
    fill_shifted(shift_ref, pad_ref)
    taps = 2 * REACH + 1
    sub = 128
    for part in range(LANES // sub):
        lanes = slice(part * sub, (part + 1) * sub)

        def one_row(y, totals):
            grad = gmix_ref[0, pl.ds(pl.multiple_of(y * broad, broad), broad), lanes]
            new = []
            for a in range(taps):
                for b in range(taps):
                    term = shift_ref[b, y + a, :, lanes] * grad
                    new.append(totals[taps * a + b] + jnp.sum(term.reshape(broad // 8, 8, sub), axis=0))
            return tuple(new)

        zero = jnp.zeros((8, sub), F32)
        totals = lax.fori_loop(0, tall, one_row, (zero,) * (taps * taps))
        for tap in range(taps * taps):
            sum_ref[tap : tap + 1, lanes] = jnp.sum(totals[tap], axis=0, keepdims=True)
    start = sum_ref.shape[0] - gpw_ref.shape[1]
    sum_ref[taps * taps : start] = jnp.zeros((start - taps * taps, LANES), F32)
    sum_ref[start:] = gpw_ref[0]
    if not halves:
        outs[0][...] = sum_ref[...]
        return
    rows = outs[0].shape[1]
    odd = spot_ref[0] % 2 == 1
    for part in range(outs[0].shape[0]):
        even_rows = sum_ref[2 * part * rows : (2 * part + 1) * rows]
        odd_rows = sum_ref[(2 * part + 1) * rows : (2 * part + 2) * rows]
        outs[0][part] = jnp.where(odd, even_rows, odd_rows)
        outs[1][part] = jnp.where(odd, odd_rows, even_rows)


def scatter_kernel(spot_ref, keep_q, come_q, keep_kv, come_kv, own_ref, *outs):
    quarter = spot_ref[0] // 2
    third = keep_q.shape[2]
    for m, out_ref in enumerate((own_ref,) + outs):
        at = quarter ^ m
        out_ref[:, :third] = keep_q[at] + come_q[at]
        out_ref[:, third:] = keep_kv[at] + come_kv[at]


def sum_kernel(norm, *refs):
    parts, out_ref = [ref[...] for ref in refs[:-1]], refs[-1]
    while len(parts) > 1:
        parts = [parts[i] + parts[i + 1] for i in range(0, len(parts), 2)]
    out_ref[...] = parts[0] * norm


def collect_kernel(spot_ref, *refs):
    parts, out_ref = refs[:-1], refs[-1]
    quarter = spot_ref[0] // 2
    for m, part in enumerate(parts):
        out_ref[quarter ^ m] = part[...]


def finish_kernel(taps, spot_ref, own_ref, come_ref, dw_ref, pw_ref, whole_ref):
    odd = spot_ref[0] % 2 == 1
    quarters, rows = own_ref.shape[:2]
    for part in range(quarters):
        own, come = own_ref[part], come_ref[part]
        whole_ref[2 * part * rows : (2 * part + 1) * rows] = jnp.where(odd, come, own)
        whole_ref[(2 * part + 1) * rows : (2 * part + 2) * rows] = jnp.where(odd, own, come)
    dw_ref[...] = whole_ref[:taps]
    pw_ref[...] = whole_ref[whole_ref.shape[0] - pw_ref.shape[0] :]


def backward_kernel(routes, *refs):
    count = routes.arriving
    layout, gmix_ref = refs[:5], refs[5]
    arrived = refs[6 : 6 + count]
    dw_ref, grad0_ref = refs[6 + count : 8 + count]
    out_ref, pad_ref, shift_ref, mix_ref = refs[8 + count :]
    place = Place(layout)
    tall, broad = out_ref.shape[2:4]
    field = gmix_ref[0].reshape(tall, broad, LANES)
    convolve_all(routes, place, field, arrived, pad_ref, shift_ref, mix_ref, dw_ref, True)
    grad = mix_ref[...] + grad0_ref[0].reshape(tall, broad, LANES)
    out_ref[0, 0] = jnp.where(place.live, grad, 0.0).astype(BF16)


def call(kernel, grid, in_specs, out_specs, out_shape, scratch=(), after=(), onto=()):
    inputs, extra = len(in_specs), len(onto) + len(after)

    def body(*refs):
        kernel(*refs[:inputs], *refs[inputs + extra :])

    run = pl.pallas_call(
        body,
        grid=(grid,),
        in_specs=list(in_specs) + [pl.BlockSpec(memory_space=pl.ANY)] * extra,
        out_specs=out_specs,
        out_shape=out_shape,
        scratch_shapes=list(scratch),
        input_output_aliases={inputs: 0} if onto else {},
        compiler_params=PARAMS,
        cost_estimate=pl.CostEstimate(flops=COST, bytes_accessed=COST, transcendentals=0),
    )
    return lambda *args: run(*args, *onto, *after)


def local(
    qkv, cotangent, dw_weight, pw_weight, tile_image, tile_row, tile_col, image_height, image_width
):
    tall, broad, channels = qkv.shape[2:]
    positions = tall * broad
    head_dim = pw_weight.shape[0]
    taps = dw_weight.shape[0]
    third = channels // 3
    per = third // LANES
    tiles, groups = lax.axis_size("tile"), lax.axis_size("img")
    routes = Routes(tiles)
    layout = (tile_image, tile_row, tile_col, image_height, image_width)
    head_specs = [SMEM] * 5
    edge = REACH * broad
    packed = 2 * (head_dim + 8)
    shape = jax.ShapeDtypeStruct
    spot = lax.axis_index("img").astype(jnp.int32).reshape(1)

    def tile_spec(first):
        return pl.BlockSpec((1, 1, tall, broad, LANES), lambda j: (0, 0, 0, 0, first * per + j))

    def flat_spec(rows, first=0):
        return pl.BlockSpec((rows, LANES), lambda j: (0, first * per + j))

    def member_spec(rows):
        return pl.BlockSpec((1, rows, LANES), lambda j: (j // per, 0, j % per))

    def pair_spec(rows):
        return pl.BlockSpec((2, rows, LANES), lambda j: (0, 0, j))

    def whole_spec(*dims):
        return pl.BlockSpec(dims, lambda j: (0,) * len(dims))

    pad_scratch = [
        pltpu.VMEM((tall + 2 * REACH, broad + 2 * EDGE, LANES), F32),
        pltpu.VMEM((2 * REACH + 1, tall + 2 * REACH, broad, LANES), F32),
    ]
    mix_scratch = [pltpu.VMEM((tall, broad, LANES), F32)]
    low, high = edge, edge + packed

    sent_kv = call(
        functools.partial(outgoing_kernel, routes),
        2 * per,
        head_specs + [tile_spec(1)],
        [member_spec(edge)] * routes.sent,
        [shape((2, edge, third), BF16)] * routes.sent,
    )(*layout, qkv)
    halo_kv = routes.move(sent_kv)
    sent_q = call(
        functools.partial(source_state_kernel, routes, head_dim),
        per,
        head_specs + [tile_spec(0), tile_spec(1), tile_spec(2)],
        [flat_spec(high)] * routes.sent,
        [shape((high, third), BF16)] * routes.sent,
    )(*layout, qkv, qkv, qkv)
    halo_q = routes.move(sent_q)

    def forward(first, count, halo, halo_spec):
        with_state = first > 0
        outs = [member_spec(positions)] * 2
        shapes = [shape((count, positions, third), F32)] * 2
        scratch = pad_scratch + mix_scratch
        if with_state:
            outs.append(whole_spec(packed, third))
            shapes.append(shape((packed, third), BF16))
            scratch = scratch + [pltpu.VMEM((per, positions, LANES), F32)]
        return call(
            functools.partial(forward_kernel, routes, per, head_dim, with_state),
            count * per,
            head_specs
            + [tile_spec(first)]
            + [halo_spec] * routes.arriving
            + [flat_spec(taps, first), flat_spec(head_dim, first)],
            outs,
            shapes,
            scratch,
        )(*layout, qkv, *halo, dw_weight, pw_weight)

    mixed_kv, merged_kv, state = forward(1, 2, halo_kv, member_spec(edge))
    state_from = exchange(state, "tile")
    others = len(state_from)
    mixed_q, merged_q = forward(0, 1, halo_q, flat_spec(high))

    source_from = halo_q if routes.relayed else exchange(sent_q[0][low:], "tile")
    from_rows, from_offset = (high, low) if routes.relayed else (packed, 0)
    grad0_q, gstate0 = call(
        functools.partial(source_query_kernel, others, low, from_offset, head_dim),
        per,
        head_specs
        + [flat_spec(high)]
        + [flat_spec(from_rows)] * others
        + [tile_spec(0), tile_spec(0)],
        [member_spec(positions), flat_spec(packed)],
        [shape((1, positions, third), F32), shape((packed, third), BF16)],
    )(*layout, sent_q[0], *source_from, qkv, cotangent)

    gstate, gmix_q, gpw_q, *sent_q2 = call(
        functools.partial(merged_query_kernel, others, routes, head_dim),
        per,
        head_specs
        + [flat_spec(packed)] * (1 + others)
        + [member_spec(positions), member_spec(positions), tile_spec(1), flat_spec(head_dim), flat_spec(packed)],
        [flat_spec(packed), member_spec(positions), member_spec(head_dim)] + [flat_spec(high)] * routes.sent,
        [
            shape((packed, third), BF16),
            shape((1, positions, third), F32),
            shape((1, head_dim, third), F32),
        ]
        + [shape((high, third), BF16)] * routes.sent,
    )(*layout, state, *state_from, merged_q, mixed_q, cotangent, pw_weight, gstate0)
    gstate_from = exchange(gstate, "tile")
    halo_q2 = routes.move(sent_q2)

    gap = -(-taps // 8) * 8
    rows = gap + head_dim
    halves = groups == 8 and rows % groups == 0
    eighth = rows // groups

    def weights(first, count, halo, halo_spec, gmix, gpw, after=()):
        if halves:
            outs = [pl.BlockSpec((4, eighth, LANES), lambda j: (0, 0, j))] * 2
            shapes = [shape((4, eighth, count * third), F32)] * 2
        else:
            outs, shapes = [flat_spec(rows)], [shape((rows, count * third), F32)]
        return call(
            functools.partial(weight_kernel, routes, halves),
            count * per,
            head_specs
            + [tile_spec(first)]
            + [halo_spec] * routes.arriving
            + [member_spec(positions), member_spec(head_dim), SMEM],
            outs,
            shapes,
            pad_scratch + [pltpu.VMEM((rows, LANES), F32)],
            after,
        )(*layout, qkv, *halo, gmix, gpw, spot)

    weights_q = weights(0, 1, halo_q, flat_spec(high), gmix_q, gpw_q)

    gmix_kv, gpw_kv, *sent_kv2 = call(
        functools.partial(merged_value_kernel, others, routes, tall, head_dim),
        per,
        head_specs
        + [flat_spec(packed)] * (1 + others)
        + [pair_spec(positions)] * 2
        + [flat_spec(head_dim, 1), flat_spec(head_dim, 2)],
        [pair_spec(positions), pair_spec(head_dim)] + [pair_spec(edge)] * routes.sent,
        [shape((2, positions, third), F32), shape((2, head_dim, third), F32)]
        + [shape((2, edge, third), BF16)] * routes.sent,
        after=(weights_q[0],),
    )(*layout, gstate, *gstate_from, merged_kv, mixed_kv, pw_weight, pw_weight)
    halo_kv2 = routes.move(sent_kv2)
    weights_kv = weights(1, 2, halo_kv, member_spec(edge), gmix_kv, gpw_kv, (halo_q2[1],))

    back_from = halo_q2 if routes.relayed else exchange(sent_q2[0][low:], "tile")
    grad0_kv = call(
        functools.partial(source_value_kernel, others, low, from_offset, head_dim),
        per,
        head_specs
        + [flat_spec(high)]
        + [flat_spec(from_rows)] * others
        + [tile_spec(1), tile_spec(2)],
        pair_spec(positions),
        shape((2, positions, third), F32),
    )(*layout, sent_q2[0], *back_from, qkv, qkv)

    def backward(first, count, gmix, halo, halo_spec, grad0, onto=()):
        return call(
            functools.partial(backward_kernel, routes),
            count * per,
            head_specs
            + [member_spec(positions)]
            + [halo_spec] * routes.arriving
            + [flat_spec(taps, first), member_spec(positions)],
            tile_spec(first),
            shape((1, 1, tall, broad, channels), BF16),
            pad_scratch + mix_scratch,
            onto=onto,
        )(*layout, gmix, *halo, dw_weight, grad0)

    grad_query = backward(0, 1, gmix_q, halo_q2, flat_spec(high), grad0_q)
    grad_source = backward(1, 2, gmix_kv, halo_kv2, member_spec(edge), grad0_kv, (grad_query,))
    norm = 1.0 / math.sqrt(positions * tiles * groups)
    if halves:
        come_q = exchange(weights_q[0], "img", (1,))[0]
        come_kv = exchange(weights_kv[0], "img", (1,))[0]
        part = shape((eighth, channels), F32)
        parts = call(
            scatter_kernel,
            1,
            [SMEM]
            + [whole_spec(4, eighth, third)] * 2
            + [whole_spec(4, eighth, 2 * third)] * 2,
            [whole_spec(eighth, channels)] * 4,
            [part] * 4,
        )(spot, weights_q[1], come_q, weights_kv[1], come_kv)
        count = lax.axis_size("img")
        moved = [
            lax.ppermute(part_m, "img", [(s, s ^ (2 * m)) for s in range(count)])
            for m, part_m in enumerate(parts[1:], 1)
        ]

        def add(values, factor, after):
            return call(
                functools.partial(sum_kernel, factor),
                1,
                [whole_spec(eighth, channels)] * len(values),
                whole_spec(eighth, channels),
                part,
                after=after,
            )(*values)

        share = add([parts[0]] + moved, 1.0, (grad_query, halo_kv2[1]))
        share = add([share] + exchange(share, "tile"), norm, (grad0_kv,))
        quarters = call(
            collect_kernel,
            1,
            [SMEM] + [whole_spec(eighth, channels)] * 4,
            whole_spec(4, eighth, channels),
            shape((4, eighth, channels), F32),
            after=(grad_source,),
        )(spot, share, *exchange(share, "img", (2, 4, 6)))
        grad_dw, grad_pw = call(
            functools.partial(finish_kernel, taps),
            1,
            [SMEM] + [whole_spec(4, eighth, channels)] * 2,
            [whole_spec(taps, channels), whole_spec(head_dim, channels)],
            [shape((taps, channels), F32), shape((head_dim, channels), F32)],
            [pltpu.VMEM((rows, channels), F32)],
        )(spot, quarters, exchange(quarters, "img", (1,))[0])
    else:
        whole = jnp.concatenate([weights_q[0], weights_kv[0]], axis=1)
        whole = lax.psum(whole, ("tile", "img")) * norm
        grad_dw, grad_pw = whole[:taps], whole[gap:]

    return grad_source, grad_dw, grad_pw


def solution(mesh):
    placed = (
        P("img", "tile", None, None, None),
        P("img", "tile", None, None, None),
        P(),
        P(),
        P("img", "tile"),
        P("img", "tile"),
        P("img", "tile"),
        P("img", None),
        P("img", None),
    )
    return jax.shard_map(
        local,
        mesh=mesh,
        in_specs=placed,
        out_specs=(P("img", "tile", None, None, None), P(), P()),
        check_vma=False,
    )
```

```python
import functools
import math

import jax
import jax.numpy as jnp
from jax import lax
from jax.experimental import pallas as pl
from jax.experimental.pallas import tpu as pltpu
from jax.sharding import PartitionSpec as P

EPSILON = 1e-06
LANES = 256
REACH = 2
EDGE = 8
BYTES_PER_US = 3_690_000
BF16 = jnp.bfloat16
F32 = jnp.float32
PARAMS = pltpu.CompilerParams(vmem_limit_bytes=16 * 1024 * 1024)
SMEM = pl.BlockSpec(memory_space=pltpu.SMEM)


class Place:
    def __init__(self, info_ref):
        slots = (info_ref.shape[0] - 4) // 2
        slot = info_ref[0]
        tall = wide = start = jnp.int32(0)
        for s in range(slots):
            tall_s, wide_s = info_ref[4 + s], info_ref[4 + slots + s]
            tall = jnp.where(slot == s, tall_s, tall)
            wide = jnp.where(slot == s, wide_s, wide)
            start = start + jnp.where(s < slot, tall_s * wide_s, 0)
        self.live = slot < slots
        self.tall, self.wide = tall, wide
        self.row, self.col = info_ref[1], info_ref[2]
        self.group = info_ref[3]
        self.within = self.row * wide + self.col
        self.index = start + self.within
        self.above = self.live & (self.row > 0)
        self.below = self.live & (self.row < tall - 1)

    def same_image(self, delta):
        other = self.within + delta
        return self.live & (other >= 0) & (other < self.tall * self.wide)


class Routes:
    def __init__(self, count):
        self.count = count
        self.relayed = count == 4
        self.shifts = [k for k in (1, -1, 2, -2, 3, -3) if abs(k) < count]
        self.sent = 2 if self.relayed else len(self.shifts)
        self.arriving = 3 if self.relayed else len(self.shifts)

    def targets(self, place):
        if not self.relayed:
            return [jnp.int32(k) for k in self.shifts]
        near, far, last = ((place.index ^ m) - place.index for m in (1, 2, 3))
        return [near, jnp.where(place.same_image(far), far, last)]

    def sources(self, place):
        if not self.relayed:
            return [jnp.int32(-k) for k in self.shifts]
        return [(place.index ^ m) - place.index for m in (1, 2, 3)]

    def move(self, sent, direct=False, hand_on=lambda far: far):
        count = self.count
        if not self.relayed:
            return [
                lax.ppermute(part, "tile", [(s, s + k) for s in range(max(0, -k), min(count, count - k))])
                for part, k in zip(sent, self.shifts)
            ]
        near, far = (
            lax.ppermute(part, "tile", [(s, s ^ m) for s in range(count)]) for part, m in zip(sent, (1, 2))
        )
        if direct:
            return [near, far, lax.ppermute(sent[1], "tile", [(s, s ^ 3) for s in range(count)])]
        return [near, far, lax.ppermute(hand_on(far), "tile", [(s, s ^ 1) for s in range(count)])]


def exchange(value, axis, masks=None):
    count = lax.axis_size(axis)
    masks = range(1, count) if masks is None else masks
    return [lax.ppermute(value, axis, [(s, s ^ m) for s in range(count)]) for m in masks]


def split(x):
    high = x.astype(BF16)
    return high, (x - high.astype(F32)).astype(BF16)


def contract(a, b, dims):
    return lax.dot_general(a, b, (dims, ((), ())), preferred_element_type=F32)


NN = ((1,), (0,))
NT = ((1,), (1,))
TN = ((0,), (0,))


def dot(a, b, dims):
    total = contract(a[0], b[0], dims)
    if b[1] is not None:
        total = total + contract(a[0], b[1], dims)
    if a[1] is not None:
        total = total + contract(a[1], b[0], dims)
    return total


def exact(x):
    return x.astype(BF16), None


def same_head(head_dim):
    rows = lax.broadcasted_iota(jnp.int32, (LANES, LANES), 0) // head_dim
    cols = lax.broadcasted_iota(jnp.int32, (LANES, LANES), 1) // head_dim
    return rows == cols


def spread(compact, mask):
    tall = jnp.concatenate([compact] * (LANES // compact.shape[0]), axis=0)
    return jnp.where(mask, tall, 0.0)


def gather_blocks(full, mask, head_dim):
    kept = jnp.where(mask, full, 0.0)
    return jnp.sum(kept.reshape(LANES // head_dim, head_dim, LANES), axis=0)


def payload(field, place, delta):
    tall, broad, lanes = field.shape
    size = REACH * broad
    top = field[:REACH].reshape(size, lanes)
    bottom = field[tall - REACH :].reshape(size, lanes)
    left = field[:, :EDGE].reshape(size, lanes)
    right = field[:, broad - EDGE :].reshape(size, lanes)
    rows = jnp.where(delta > 0, bottom, top)
    cols = jnp.where(place.col == 0, right, left)
    beside = (place.wide == 2) & (delta == jnp.where(place.col == 0, 1, -1))
    return jnp.where(beside, cols, rows)


def edge_of(ref, size):
    rows = ref[0] if len(ref.shape) == 3 else ref[:size]
    return rows.astype(F32)


def pack_state(state, total):
    rows = jnp.concatenate([state, total, jnp.zeros((7, state.shape[1]), F32)], axis=0)
    return jnp.concatenate(split(rows), axis=0)


def unpack_state(ref, offset):
    rows = ref[offset:].astype(F32)
    half = rows.shape[0] // 2
    return rows[:half] + rows[half:]


def total_state(own_ref, others, place, offset, others_offset):
    total = unpack_state(own_ref, offset)
    for m, other in enumerate(others, 1):
        delta = (place.index ^ m) - place.index
        total = total + jnp.where(place.same_image(delta), unpack_state(other, others_offset), 0.0)
    return total


def fill_padded(pad_ref, field, arrived_refs, deltas, place):
    tall, broad, lanes = field.shape
    size = REACH * broad
    two = place.live & (place.wide == 2)
    one = place.live & (place.wide == 1)
    first, second = two & (place.col == 0), two & (place.col == 1)

    def choose(condition, value, other):
        return jnp.where(condition, value, other)

    above = below = jnp.zeros((REACH, broad, lanes), F32)
    above_side = below_side = jnp.zeros((REACH, EDGE, lanes), F32)
    side = jnp.zeros((tall, EDGE, lanes), F32)
    for arrived_ref, delta in zip(arrived_refs, deltas):
        edges = edge_of(arrived_ref, size)
        rows, cols = edges.reshape(REACH, broad, lanes), edges.reshape(tall, EDGE, lanes)
        begin, end = rows[:, :EDGE], rows[:, broad - EDGE :]
        above = choose((one & (delta == -1)) | (two & (delta == -2)), rows, above)
        below = choose((one & (delta == 1)) | (two & (delta == 2)), rows, below)
        side = choose((first & (delta == 1)) | (second & (delta == -1)), cols, side)
        above_side = choose(first & (delta == -1), begin, choose(second & (delta == -3), end, above_side))
        below_side = choose(second & (delta == 1), end, choose(first & (delta == 3), begin, below_side))
    column = lax.broadcasted_iota(jnp.int32, (1, EDGE, lanes), 1)
    reached = (first & (column < REACH)) | (second & (column >= EDGE - REACH))
    upper, lower = slice(0, REACH), slice(REACH + tall, 2 * REACH + tall)
    pad_ref[upper, :broad] = choose(place.above, above, 0.0)
    pad_ref[lower, :broad] = choose(place.below, below, 0.0)
    pad_ref[upper, broad:] = choose(reached & place.above, above_side, 0.0)
    pad_ref[lower, broad:] = choose(reached & place.below, below_side, 0.0)
    pad_ref[REACH : REACH + tall, broad:] = choose(reached, side, 0.0)
    pad_ref[REACH : REACH + tall, :broad] = field


def convolve(pad_ref, kernel_ref, mix_ref, flipped):
    taps = 2 * REACH + 1
    tall, broad, lanes = mix_ref.shape
    ring = broad + EDGE
    sub = 128
    for start in range(0, lanes, sub):
        at = slice(start, start + sub)
        for y in range(tall):
            rows = [pad_ref[y + a, :, at] for a in range(taps)]
            total = None
            for b in range(taps):
                part = None
                for a in range(taps):
                    tap = taps * a + b
                    if flipped:
                        tap = taps * taps - 1 - tap
                    term = rows[a] * kernel_ref[tap : tap + 1, at]
                    part = term if part is None else part + term
                if b != REACH:
                    part = pltpu.roll(part, (REACH - b) % ring, 0)
                total = part[:broad] if total is None else total + part[:broad]
            mix_ref[y, :, at] = total


def read_field(ref, place, at=slice(None)):
    return jnp.where(place.live, ref[0, 0, :, :, at].astype(F32), 0.0)


def outgoing_kernel(routes, layout, key_ref, value_ref, *outs):
    place = Place(layout)
    for member, field_ref in enumerate((key_ref, value_ref)):
        field = field_ref[0, 0].astype(F32)
        for delta, out_ref in zip(routes.targets(place), outs):
            out_ref[member] = payload(field, place, delta).astype(BF16)


def source_state_kernel(routes, head_dim, *refs):
    layout, (query_ref, key_ref, value_ref), outs = refs[0], refs[1:4], refs[4:]
    place = Place(layout)
    mask = same_head(head_dim)
    for at in parts_of(query_ref.shape[4]):
        field = query_ref[0, 0, :, :, at].astype(F32)
        size = REACH * field.shape[1]
        keys = read_field(key_ref, place, at).reshape(-1, LANES)
        keys = jnp.maximum(keys, 0.0)
        values = read_field(value_ref, place, at).reshape(-1, LANES)
        state = gather_blocks(contract(keys.astype(BF16), values.astype(BF16), TN), mask, head_dim)
        packed = pack_state(state, jnp.sum(keys, axis=0, keepdims=True))
        for delta, out_ref in zip(routes.targets(place), outs):
            out_ref[:size, at] = payload(field, place, delta).astype(BF16)
            out_ref[size:, at] = packed


def forward_kernel(routes, per, head_dim, with_state, *refs):
    count = routes.arriving
    layout, field_ref = refs[:2]
    arrived = refs[2 : 2 + count]
    refs = refs[2 + count :]
    dw_ref, pw_ref, mixed_ref, merged_ref, padded_ref = refs[:5]
    if with_state:
        state_ref, mix_ref, key_ref = refs[5:]
    else:
        (mix_ref,) = refs[5:]
    step = pl.program_id(0)
    place = Place(layout)
    field = read_field(field_ref, place)
    padded = padded_ref.at[0]
    fill_padded(padded, field, arrived, routes.sources(place), place)
    convolve(padded, dw_ref, mix_ref, False)
    mixed = mix_ref[...].reshape(-1, LANES)
    mixed_ref[0] = mixed
    mask = same_head(head_dim)
    merged = dot(split(mixed), split(spread(pw_ref[...], mask)), NN)
    merged_ref[0] = merged
    if not with_state:
        return
    for part in range(per):

        @pl.when(step == part)
        def _():
            key_ref[part] = jnp.maximum(merged, 0.0)

        @pl.when(step == per + part)
        def _():
            keys = key_ref[part]
            state = gather_blocks(dot(split(keys), split(merged), TN), mask, head_dim)
            lanes = slice(part * LANES, (part + 1) * LANES)
            state_ref[:, lanes] = pack_state(state, jnp.sum(keys, axis=0, keepdims=True))


def parts_of(lanes):
    return [slice(start, start + LANES) for start in range(0, lanes, LANES)]


def query_gradients(raw, exactly, total, cot, head_dim, mask):
    ones = (mask.astype(BF16), None)
    query = jnp.maximum(raw, 0.0)
    pair = exact(query) if exactly else split(query)
    state = split(spread(total[:head_dim], mask))
    key_sum = total[head_dim : head_dim + 1]
    over = 1.0 / (dot(split(query * key_sum), ones, NN) + EPSILON)
    result = dot(pair, state, NN) * over
    grad_num = cot * over
    grad_den = -dot(split(cot * result), ones, NN) * over
    num_pair = split(grad_num)
    grad = jnp.where(raw > 0, dot(num_pair, state, NT) + grad_den * key_sum, 0.0)
    gstate = gather_blocks(dot(pair, num_pair, TN), mask, head_dim)
    return grad, pack_state(gstate, jnp.sum(query * grad_den, axis=0, keepdims=True))


def source_query_kernel(others, offset, others_offset, head_dim, *refs):
    layout, own_ref, received = refs[0], refs[1], refs[2 : 2 + others]
    source_ref, cot_ref, grad_ref, gstate_ref = refs[2 + others :]
    place = Place(layout)
    mask = same_head(head_dim)
    total = total_state(own_ref, received, place, offset, others_offset)
    for at in parts_of(gstate_ref.shape[1]):
        raw = read_field(source_ref, place, at).reshape(-1, LANES)
        cot = cot_ref[0, 0, :, :, at].astype(F32).reshape(raw.shape)
        grad_ref[0, :, at], gstate_ref[:, at] = query_gradients(raw, True, total[:, at], cot, head_dim, mask)


def merged_query_kernel(others, head_dim, *refs):
    layout, own_ref, received = refs[0], refs[1], refs[2 : 2 + others]
    merged_ref, mixed_ref, cot_ref, pw_ref, gstate_ref, gmix_ref, gpw_ref = refs[2 + others :]
    place = Place(layout)
    mask = same_head(head_dim)
    total = total_state(own_ref, received, place, 0, 0)
    for at in parts_of(gstate_ref.shape[1]):
        raw = merged_ref[0, :, at]
        cot = cot_ref[0, 0, :, :, at].astype(F32).reshape(raw.shape)
        grad, gstate_ref[:, at] = query_gradients(raw, False, total[:, at], cot, head_dim, mask)
        pair = split(grad)
        gmix_ref[0, :, at] = dot(pair, split(spread(pw_ref[:, at], mask)), NT)
        gpw_ref[0, :, at] = gather_blocks(dot(split(mixed_ref[0, :, at]), pair, TN), mask, head_dim)


def key_gradients(raw, key_pair, value_pair, total, head_dim, mask):
    gstate = split(spread(total[:head_dim], mask))
    gsum = total[head_dim : head_dim + 1]
    grad_keys = jnp.where(raw > 0, dot(value_pair, gstate, NT) + gsum, 0.0)
    return grad_keys, dot(key_pair, gstate, NN)


def source_value_kernel(others, offset, others_offset, head_dim, *refs):
    layout, own_ref, received = refs[0], refs[1], refs[2 : 2 + others]
    key_ref, value_ref, grad_ref = refs[2 + others :]
    place = Place(layout)
    mask = same_head(head_dim)
    total = total_state(own_ref, received, place, offset, others_offset)
    for at in parts_of(grad_ref.shape[2]):
        raw = read_field(key_ref, place, at).reshape(-1, LANES)
        values = read_field(value_ref, place, at).reshape(-1, LANES)
        grad_ref[0, :, at], grad_ref[1, :, at] = key_gradients(
            raw, exact(jnp.maximum(raw, 0.0)), exact(values), total[:, at], head_dim, mask
        )


def merged_value_kernel(others, routes, tall, head_dim, *refs):
    layout, own_ref, received = refs[0], refs[1], refs[2 : 2 + others]
    merged_ref, mixed_ref, kpw_ref, vpw_ref, qgmix_ref, packed_ref, gmix_ref, gpw_ref = refs[2 + others : 10 + others]
    outs = refs[10 + others :]
    place = Place(layout)
    mask = same_head(head_dim)
    total = total_state(own_ref, received, place, 0, 0)
    size = (outs[0].shape[0] - packed_ref.shape[0]) // 3

    def send(member, at, gmix):
        field = gmix.reshape(tall, -1, LANES)
        for delta, out_ref in zip(routes.targets(place), outs):
            out_ref[member * size : (member + 1) * size, at] = payload(field, place, delta).astype(BF16)

    for at in parts_of(gmix_ref.shape[2]):
        for out_ref in outs:
            out_ref[3 * size :, at] = packed_ref[:, at]
        send(0, at, qgmix_ref[0, :, at])
        raw = merged_ref[0, :, at]
        pairs = split(jnp.maximum(raw, 0.0)), split(merged_ref[1, :, at])
        grads = key_gradients(raw, *pairs, total[:, at], head_dim, mask)
        for member, (grad, pw_ref) in enumerate(zip(grads, (kpw_ref, vpw_ref))):
            pair = split(grad)
            gmix = dot(pair, split(spread(pw_ref[:, at], mask)), NT)
            gmix_ref[member, :, at] = gmix
            gpw_ref[member, :, at] = gather_blocks(dot(split(mixed_ref[member, :, at]), pair, TN), mask, head_dim)
            send(1 + member, at, gmix)


def weight_kernel(routes, halves, *refs):
    layout, padded_ref, gmix_ref, gpw_ref = refs[:4]
    refs = refs[4:]
    place = Place(layout)
    ring, sub = padded_ref.shape[2], 128
    tall, broad = padded_ref.shape[1] - 2 * REACH, ring - EDGE
    outs, sum_ref = refs[:-1], refs[-1]
    taps = 2 * REACH + 1
    for part in range(LANES // sub):
        lanes = slice(part * sub, (part + 1) * sub)

        def one_row(y, totals):
            grad = gmix_ref[0, pl.ds(pl.multiple_of(y * broad, broad), broad), lanes]
            grad = jnp.concatenate([grad, jnp.zeros((EDGE, sub), F32)], axis=0)
            moved = [grad if b == REACH else pltpu.roll(grad, (b - REACH) % ring, 0) for b in range(taps)]
            new = list(totals)
            for a in range(taps):
                row = padded_ref[0, y + a, :, lanes]
                for b in range(taps):
                    term = (row * moved[b]).reshape(ring // 8, 8, sub)
                    new[taps * a + b] = new[taps * a + b] + jnp.sum(term, axis=0)
            return tuple(new)

        zero = jnp.zeros((8, sub), F32)
        totals = lax.fori_loop(0, tall, one_row, (zero,) * (taps * taps), unroll=2)
        for tap in range(taps * taps):
            sum_ref[tap : tap + 1, lanes] = jnp.sum(totals[tap], axis=0, keepdims=True)
    start = sum_ref.shape[0] - gpw_ref.shape[1]
    sum_ref[taps * taps : start] = jnp.zeros((start - taps * taps, LANES), F32)
    sum_ref[start:] = gpw_ref[0]
    if not halves:
        outs[0][...] = sum_ref[...]
        return
    rows = outs[0].shape[1]
    odd = place.group % 2 == 1
    for part in range(outs[0].shape[0]):
        even_rows = sum_ref[2 * part * rows : (2 * part + 1) * rows]
        odd_rows = sum_ref[(2 * part + 1) * rows : (2 * part + 2) * rows]
        outs[0][part] = jnp.where(odd, even_rows, odd_rows)
        outs[1][part] = jnp.where(odd, odd_rows, even_rows)


def scatter_kernel(layout, keep_q, come_q, keep_kv, come_kv, own_ref, *outs):
    quarter = Place(layout).group // 2
    third = keep_q.shape[2]
    for m, out_ref in enumerate((own_ref,) + outs):
        at = quarter ^ m
        out_ref[:, :third] = keep_q[at] + come_q[at]
        out_ref[:, third:] = keep_kv[at] + come_kv[at]


def sum_kernel(norm, *refs):
    parts, out_ref = [ref[...] for ref in refs[:-1]], refs[-1]
    while len(parts) > 1:
        parts = [parts[i] + parts[i + 1] for i in range(0, len(parts), 2)]
    out_ref[...] = parts[0] * norm


def collect_kernel(layout, *refs):
    parts, out_ref = refs[:-1], refs[-1]
    quarter = Place(layout).group // 2
    for m, part in enumerate(parts):
        out_ref[quarter ^ m] = part[...]


def finish_kernel(taps, layout, own_ref, come_ref, dw_ref, pw_ref, whole_ref):
    odd = Place(layout).group % 2 == 1
    quarters, rows = own_ref.shape[:2]
    for part in range(quarters):
        own, come = own_ref[part], come_ref[part]
        whole_ref[2 * part * rows : (2 * part + 1) * rows] = jnp.where(odd, come, own)
        whole_ref[(2 * part + 1) * rows : (2 * part + 2) * rows] = jnp.where(odd, own, come)
    dw_ref[...] = whole_ref[:taps]
    pw_ref[...] = whole_ref[whole_ref.shape[0] - pw_ref.shape[0] :]


def copy_kernel(in_ref, out_ref):
    out_ref[...] = in_ref[...]


def backward_kernel(routes, *refs):
    count = routes.arriving
    layout, gmix_ref = refs[:2]
    arrived = refs[2 : 2 + count]
    dw_ref, grad0_ref, out_ref, pad_ref, mix_ref = refs[2 + count :]
    place = Place(layout)
    tall, broad = out_ref.shape[2:4]
    field = gmix_ref[0].reshape(tall, broad, LANES)
    fill_padded(pad_ref, field, arrived, routes.sources(place), place)
    convolve(pad_ref, dw_ref, mix_ref, True)
    grad = mix_ref[...] + grad0_ref[0].reshape(tall, broad, LANES)
    out_ref[0, 0] = jnp.where(place.live, grad, 0.0).astype(BF16)


def call(cost, kernel, grid, in_specs, out_specs, out_shape, scratch=(), after=(), onto=()):
    inputs, extra = len(in_specs), len(onto) + len(after)

    def body(*refs):
        kernel(*refs[:inputs], *refs[inputs + extra :])

    run = pl.pallas_call(
        body,
        grid=(grid,),
        in_specs=list(in_specs) + [pl.BlockSpec(memory_space=pl.ANY)] * extra,
        out_specs=out_specs,
        out_shape=out_shape,
        scratch_shapes=list(scratch),
        input_output_aliases={inputs: 0} if onto else {},
        compiler_params=PARAMS,
        cost_estimate=pl.CostEstimate(
            flops=0, bytes_accessed=int(cost * BYTES_PER_US), transcendentals=0
        ),
    )
    return lambda *args: run(*args, *onto, *after)


def in_hbm(x):
    return pltpu.with_memory_space_constraint(x, pltpu.HBM)


def local(
    qkv, cotangent, dw_weight, pw_weight, tile_image, tile_row, tile_col, image_height, image_width
):
    tall, broad, channels = qkv.shape[2:]
    positions = tall * broad
    head_dim = pw_weight.shape[0]
    taps = dw_weight.shape[0]
    third = channels // 3
    per = third // LANES
    tiles, groups = lax.axis_size("tile"), lax.axis_size("img")
    routes = Routes(tiles)
    head_specs = [SMEM]
    edge = REACH * broad
    packed = 2 * (head_dim + 8)
    padded_shape = (tall + 2 * REACH, broad + EDGE)
    shape = jax.ShapeDtypeStruct
    spot = lax.axis_index("img").astype(jnp.int32)
    scalars = (tile_image, tile_row, tile_col, spot, image_height, image_width)
    layout = jnp.concatenate([x.reshape(-1) for x in scalars])
    qkv, cotangent = in_hbm(qkv), in_hbm(cotangent)

    def tile_spec(first):
        return pl.BlockSpec((1, 1, tall, broad, LANES), lambda j: (0, 0, 0, 0, first * per + j))

    def third_spec(first):
        return pl.BlockSpec((1, 1, tall, broad, third), lambda j: (0, 0, 0, 0, first))

    def flat_spec(rows, first=0):
        return pl.BlockSpec((rows, LANES), lambda j: (0, first * per + j))

    def wide_spec(rows, first=0):
        return pl.BlockSpec((rows, third), lambda j: (0, first))

    def member_spec(*dims):
        return pl.BlockSpec((1, *dims, LANES), lambda j: (j // per,) + (0,) * len(dims) + (j % per,))

    def edge_spec(first):
        return pl.BlockSpec((edge, LANES), lambda j: (first + j // per, j % per))

    def whole_spec(*dims):
        return pl.BlockSpec(dims, lambda j: (0,) * len(dims))

    mix_scratch = [pltpu.VMEM((tall, broad, LANES), F32)]
    low, high = edge, edge + packed

    sent_kv = call(
        1.2,
        functools.partial(outgoing_kernel, routes),
        1,
        head_specs + [third_spec(1), third_spec(2)],
        [whole_spec(2, edge, third)] * routes.sent,
        [shape((2, edge, third), BF16)] * routes.sent,
    )(layout, qkv, qkv)
    halo_kv = routes.move(sent_kv)
    sent_q = call(
        1.5,
        functools.partial(source_state_kernel, routes, head_dim),
        1,
        head_specs + [third_spec(0), third_spec(1), third_spec(2)],
        [whole_spec(high, third)] * routes.sent,
        [shape((high, third), BF16)] * routes.sent,
        after=(halo_kv[0],),
    )(layout, qkv, qkv, qkv)
    halo_q = routes.move(sent_q, direct=True)

    def forward(first, count, halo, halo_spec):
        with_state = first > 0
        outs = [member_spec(positions)] * 2 + [member_spec(*padded_shape)]
        shapes = [pltpu.HBM((count, positions, third), F32)] * 2
        shapes.append(pltpu.HBM((count, *padded_shape, third), F32))
        scratch = mix_scratch
        if with_state:
            outs.append(whole_spec(packed, third))
            shapes.append(shape((packed, third), BF16))
            scratch = scratch + [pltpu.VMEM((per, positions, LANES), F32)]
        return call(
            1.7 * count * per,
            functools.partial(forward_kernel, routes, per, head_dim, with_state),
            count * per,
            head_specs
            + [tile_spec(first)]
            + [halo_spec] * routes.arriving
            + [flat_spec(taps, first), flat_spec(head_dim, first)],
            outs,
            shapes,
            scratch,
        )(layout, qkv, *halo, dw_weight, pw_weight)

    mixed_kv, merged_kv, padded_kv, state = forward(1, 2, halo_kv, member_spec(edge))
    state_from = exchange(state, "tile")
    others = len(state_from)
    mixed_q, merged_q, padded_q = forward(0, 1, halo_q, flat_spec(high))

    source_from = halo_q if routes.relayed else exchange(sent_q[0][low:], "tile")
    from_rows, from_offset = (high, low) if routes.relayed else (packed, 0)
    grad0_q, gstate0 = call(
        2.9,
        functools.partial(source_query_kernel, others, low, from_offset, head_dim),
        1,
        head_specs
        + [whole_spec(high, third)]
        + [whole_spec(from_rows, third)] * others
        + [third_spec(0), third_spec(0)],
        [whole_spec(1, positions, third), whole_spec(packed, third)],
        [pltpu.HBM((1, positions, third), F32), shape((packed, third), BF16)],
    )(layout, sent_q[0], *source_from, qkv, cotangent)

    gstate, gmix_q, gpw_q = call(
        3.2,
        functools.partial(merged_query_kernel, others, head_dim),
        1,
        head_specs
        + [whole_spec(packed, third)] * (1 + others)
        + [whole_spec(1, positions, third)] * 2
        + [third_spec(1), wide_spec(head_dim)],
        [whole_spec(packed, third), whole_spec(1, positions, third), whole_spec(1, head_dim, third)],
        [
            shape((packed, third), BF16),
            shape((1, positions, third), F32),
            shape((1, head_dim, third), F32),
        ],
        after=(gstate0,),
    )(layout, state, *state_from, in_hbm(merged_q), in_hbm(mixed_q), cotangent, pw_weight)
    gstate_from = exchange(gstate, "tile")

    gap = -(-taps // 8) * 8
    rows = gap + head_dim
    halves = groups == 8 and rows % groups == 0
    eighth = rows // groups

    def weights(count, padded, gmix, gpw, after=()):
        if halves:
            outs = [pl.BlockSpec((4, eighth, LANES), lambda j: (0, 0, j))] * 2
            shapes = [shape((4, eighth, count * third), F32)] * 2
        else:
            outs, shapes = [flat_spec(rows)], [shape((rows, count * third), F32)]
        return call(
            1.2 * count * per,
            functools.partial(weight_kernel, routes, halves),
            count * per,
            head_specs + [member_spec(*padded_shape), member_spec(positions), member_spec(head_dim)],
            outs,
            shapes,
            [pltpu.VMEM((rows, LANES), F32)],
            after,
        )(layout, in_hbm(padded), gmix, gpw)

    weights_q = weights(1, padded_q, gmix_q, gpw_q)
    total_rows = 3 * edge + packed
    gmix_kv, gpw_kv, *sent_back = call(
        3.2,
        functools.partial(merged_value_kernel, others, routes, tall, head_dim),
        1,
        head_specs
        + [whole_spec(packed, third)] * (1 + others)
        + [whole_spec(2, positions, third)] * 2
        + [wide_spec(head_dim, 1), wide_spec(head_dim, 2)]
        + [whole_spec(1, positions, third), whole_spec(packed, third)],
        [whole_spec(2, positions, third), whole_spec(2, head_dim, third)]
        + [whole_spec(total_rows, third)] * routes.sent,
        [shape((2, positions, third), F32), shape((2, head_dim, third), F32)]
        + [shape((total_rows, third), BF16)] * routes.sent,
        after=(weights_q[0],),
    )(
        layout, gstate, *gstate_from, in_hbm(merged_kv), in_hbm(mixed_kv), pw_weight, pw_weight,
        gmix_q, gstate0,
    )
    weights_kv = weights(2, padded_kv, gmix_kv, gpw_kv)

    def after_weights(far):
        return call(
            0.5,
            copy_kernel,
            1,
            [whole_spec(total_rows, third)],
            whole_spec(total_rows, third),
            shape((total_rows, third), BF16),
            after=(weights_kv[0],),
        )(far)

    halo_back = routes.move(sent_back, hand_on=after_weights)

    back_from = halo_back if routes.relayed else exchange(sent_back[0][3 * edge :], "tile")
    back_rows, back_offset = (total_rows, 3 * edge) if routes.relayed else (packed, 0)
    grad0_kv = call(
        1.5,
        functools.partial(source_value_kernel, others, 3 * edge, back_offset, head_dim),
        1,
        head_specs
        + [whole_spec(total_rows, third)]
        + [whole_spec(back_rows, third)] * others
        + [third_spec(1), third_spec(2)],
        whole_spec(2, positions, third),
        shape((2, positions, third), F32),
    )(layout, sent_back[0], *back_from, qkv, qkv)

    def backward(first, count, gmix, grad0, onto=()):
        return call(
            1.2 * count * per,
            functools.partial(backward_kernel, routes),
            count * per,
            head_specs
            + [member_spec(positions)]
            + [edge_spec(first)] * routes.arriving
            + [flat_spec(taps, first), member_spec(positions)],
            tile_spec(first),
            pltpu.HBM((1, 1, tall, broad, channels), BF16),
            [pltpu.VMEM((*padded_shape, LANES), F32)] + mix_scratch,
            onto=onto,
        )(layout, gmix, *halo_back, dw_weight, grad0)

    grad_query = in_hbm(backward(0, 1, gmix_q, in_hbm(grad0_q)))
    grad_source = backward(1, 2, gmix_kv, grad0_kv, (grad_query,))

    norm = 1.0 / math.sqrt(positions * tiles * groups)
    if halves:
        come_q = exchange(weights_q[0], "img", (1,))[0]
        come_kv = exchange(weights_kv[0], "img", (1,))[0]
        part = shape((eighth, channels), F32)
        parts = call(
            0.5,
            scatter_kernel,
            1,
            [SMEM]
            + [whole_spec(4, eighth, third)] * 2
            + [whole_spec(4, eighth, 2 * third)] * 2,
            [whole_spec(eighth, channels)] * 4,
            [part] * 4,
        )(layout, weights_q[1], come_q, weights_kv[1], come_kv)
        count = lax.axis_size("img")
        moved = [
            lax.ppermute(part_m, "img", [(s, s ^ (2 * m)) for s in range(count)])
            for m, part_m in enumerate(parts[1:], 1)
        ]

        def add(values, factor, after):
            return call(
                0.3,
                functools.partial(sum_kernel, factor),
                1,
                [whole_spec(eighth, channels)] * len(values),
                whole_spec(eighth, channels),
                part,
                after=after,
            )(*values)

        share = add([parts[0]] + moved, 1.0, (grad_query,))
        share = add([share] + exchange(share, "tile"), norm, (grad0_kv,))
        quarters = call(
            0.5,
            collect_kernel,
            1,
            [SMEM] + [whole_spec(eighth, channels)] * 4,
            whole_spec(4, eighth, channels),
            shape((4, eighth, channels), F32),
            after=(in_hbm(grad_source),),
        )(layout, share, *exchange(share, "img", (2, 4, 6)))
        grad_dw, grad_pw = call(
            0.8,
            functools.partial(finish_kernel, taps),
            1,
            [SMEM] + [whole_spec(4, eighth, channels)] * 2,
            [whole_spec(taps, channels), whole_spec(head_dim, channels)],
            [shape((taps, channels), F32), shape((head_dim, channels), F32)],
            [pltpu.VMEM((rows, channels), F32)],
        )(layout, quarters, exchange(quarters, "img", (1,))[0])
    else:
        whole = jnp.concatenate([weights_q[0], weights_kv[0]], axis=1)
        whole = lax.psum(whole, ("tile", "img")) * norm
        grad_dw, grad_pw = whole[:taps], whole[gap:]

    return grad_source, grad_dw, grad_pw


def solution(mesh):
    placed = (
        P("img", "tile", None, None, None),
        P("img", "tile", None, None, None),
        P(),
        P(),
        P("img", "tile"),
        P("img", "tile"),
        P("img", "tile"),
        P("img", None),
        P("img", None),
    )
    return jax.shard_map(
        local,
        mesh=mesh,
        in_specs=placed,
        out_specs=(P("img", "tile", None, None, None), P(), P()),
        check_vma=False,
    )
```

```python
import functools
import math

import jax
import jax.numpy as jnp
from jax import lax
from jax.experimental import pallas as pl
from jax.experimental.pallas import tpu as pltpu
from jax.sharding import PartitionSpec as P

EPSILON = 1e-06
LANES = 256
REACH = 2
EDGE = 8
BYTES_PER_US = 3_690_000
BF16 = jnp.bfloat16
F32 = jnp.float32
PARAMS = pltpu.CompilerParams(vmem_limit_bytes=16 * 1024 * 1024)


class Place:
    def __init__(self, info_ref):
        slots = (info_ref.shape[0] - 4) // 2
        slot = info_ref[0]
        tall = wide = start = jnp.int32(0)
        for s in range(slots):
            tall_s, wide_s = info_ref[4 + s], info_ref[4 + slots + s]
            tall = jnp.where(slot == s, tall_s, tall)
            wide = jnp.where(slot == s, wide_s, wide)
            start = start + jnp.where(s < slot, tall_s * wide_s, 0)
        self.live = slot < slots
        self.tall, self.wide = tall, wide
        self.row, self.col = info_ref[1], info_ref[2]
        self.group = info_ref[3]
        self.within = self.row * wide + self.col
        self.index = start + self.within
        self.above = self.live & (self.row > 0)
        self.below = self.live & (self.row < tall - 1)

    def same_image(self, delta):
        other = self.within + delta
        return self.live & (other >= 0) & (other < self.tall * self.wide)


class Routes:
    def __init__(self, count):
        self.count = count
        self.relayed = count == 4
        self.shifts = [k for k in (1, -1, 2, -2, 3, -3) if abs(k) < count]
        self.sent = 2 if self.relayed else len(self.shifts)
        self.arriving = 3 if self.relayed else len(self.shifts)

    def targets(self, place, direct=False):
        if not self.relayed:
            return [jnp.int32(k) for k in self.shifts]
        near, far, last = ((place.index ^ m) - place.index for m in (1, 2, 3))
        if direct:
            return [near, far, last, last]
        return [near, jnp.where(place.same_image(far), far, last)]

    def sources(self, place, direct=False):
        if not self.relayed:
            return [jnp.int32(-k) for k in self.shifts]
        near, far, last = ((place.index ^ m) - place.index for m in (1, 2, 3))
        if direct:
            outer = jnp.abs(last) == 3
            return [near, far, jnp.where(outer, 0, last), jnp.where(outer, last, 0)]
        return [near, far, last]

    def direct_rows(self, edge):
        return [edge, edge, edge, REACH * EDGE] if self.relayed else [edge] * self.sent

    def move(self, sent, hand_on=lambda near, far: far):
        count = self.count
        if not self.relayed:
            return [
                lax.ppermute(part, "tile", [(s, s + k) for s in range(max(0, -k), min(count, count - k))])
                for part, k in zip(sent, self.shifts)
            ]
        near, far = (
            lax.ppermute(part, "tile", [(s, s ^ m) for s in range(count)]) for part, m in zip(sent, (1, 2))
        )
        return [near, far, lax.ppermute(hand_on(near, far), "tile", [(s, s ^ 1) for s in range(count)])]

    def move_direct(self, sent):
        if not self.relayed:
            return self.move(sent)
        targets = ((1, 0, 3, 2), (2, 3, 0, 1), (0, 2, 1, 3), (3, 1, 2, 0))
        return [lax.ppermute(part, "tile", list(enumerate(to))) for part, to in zip(sent, targets)]


def exchange(value, axis, masks=None):
    count = lax.axis_size(axis)
    masks = range(1, count) if masks is None else masks
    return [lax.ppermute(value, axis, [(s, s ^ m) for s in range(count)]) for m in masks]


def split(x):
    high = x.astype(BF16)
    return high, (x - high.astype(F32)).astype(BF16)


def contract(a, b, dims):
    return lax.dot_general(a, b, (dims, ((), ())), preferred_element_type=F32)


NN = ((1,), (0,))
NT = ((1,), (1,))
TN = ((0,), (0,))


def dot(a, b, dims):
    total = contract(a[0], b[0], dims)
    if b[1] is not None:
        total = total + contract(a[0], b[1], dims)
    if a[1] is not None:
        total = total + contract(a[1], b[0], dims)
    return total


def exact(x):
    return x.astype(BF16), None


def same_head(head_dim):
    rows = lax.broadcasted_iota(jnp.int32, (LANES, LANES), 0) // head_dim
    cols = lax.broadcasted_iota(jnp.int32, (LANES, LANES), 1) // head_dim
    return rows == cols


def spread(compact, mask):
    tall = jnp.concatenate([compact] * (LANES // compact.shape[0]), axis=0)
    return jnp.where(mask, tall, 0.0)


def gather_blocks(full, mask, head_dim):
    kept = jnp.where(mask, full, 0.0)
    return jnp.sum(kept.reshape(LANES // head_dim, head_dim, LANES), axis=0)


def payload(field, place, delta):
    tall, broad, lanes = field.shape
    size = REACH * broad
    top = field[:REACH].reshape(size, lanes)
    bottom = field[tall - REACH :].reshape(size, lanes)
    left = field[:, :EDGE].reshape(size, lanes)
    right = field[:, broad - EDGE :].reshape(size, lanes)
    rows = jnp.where(delta > 0, bottom, top)
    cols = jnp.where(place.col == 0, right, left)
    beside = (place.wide == 2) & (delta == jnp.where(place.col == 0, 1, -1))
    return jnp.where(beside, cols, rows)


def lanes_at(block):
    start = block * LANES
    return pl.ds(start if isinstance(start, int) else pl.multiple_of(start, LANES), LANES)


def pack_state(state, total):
    rows = jnp.concatenate([state, total, jnp.zeros((7, state.shape[1]), F32)], axis=0)
    return jnp.concatenate(split(rows), axis=0)


def unpack_state(ref, offset):
    rows = ref[offset:].astype(F32)
    half = rows.shape[0] // 2
    return rows[:half] + rows[half:]


def total_state(own_ref, others, place, offset, others_offset):
    total = unpack_state(own_ref, offset)
    for m, other in enumerate(others, 1):
        delta = (place.index ^ m) - place.index
        total = total + jnp.where(place.same_image(delta), unpack_state(other, others_offset), 0.0)
    return total


def corner_payload(field, delta):
    tall, broad, lanes = field.shape
    corner = jnp.where(delta > 0, field[tall - REACH :, broad - EDGE :], field[:REACH, :EDGE])
    return corner.reshape(REACH * EDGE, lanes)


def fill_padded(pad_ref, field, arrived, deltas, place):
    tall, broad, lanes = field.shape
    two = place.live & (place.wide == 2)
    one = place.live & (place.wide == 1)
    first, second = two & (place.col == 0), two & (place.col == 1)

    def choose(condition, value, other):
        return jnp.where(condition, value, other)

    above = below = jnp.zeros((REACH, broad, lanes), F32)
    above_side = below_side = jnp.zeros((REACH, EDGE, lanes), F32)
    side = jnp.zeros((tall, EDGE, lanes), F32)
    for edges, delta in zip(arrived, deltas):
        edges = edges.astype(F32)
        if edges.shape[0] == REACH * EDGE:
            corner = edges.reshape(REACH, EDGE, lanes)
            above_side = choose(second & (delta == -3), corner, above_side)
            below_side = choose(first & (delta == 3), corner, below_side)
            continue
        rows, cols = edges.reshape(REACH, broad, lanes), edges.reshape(tall, EDGE, lanes)
        begin, end = rows[:, :EDGE], rows[:, broad - EDGE :]
        above = choose((one & (delta == -1)) | (two & (delta == -2)), rows, above)
        below = choose((one & (delta == 1)) | (two & (delta == 2)), rows, below)
        side = choose((first & (delta == 1)) | (second & (delta == -1)), cols, side)
        above_side = choose(first & (delta == -1), begin, choose(second & (delta == -3), end, above_side))
        below_side = choose(second & (delta == 1), end, choose(first & (delta == 3), begin, below_side))
    column = lax.broadcasted_iota(jnp.int32, (1, EDGE, lanes), 1)
    reached = (first & (column < REACH)) | (second & (column >= EDGE - REACH))
    upper, lower = slice(0, REACH), slice(REACH + tall, 2 * REACH + tall)
    pad_ref[upper, :broad] = choose(place.above, above, 0.0)
    pad_ref[lower, :broad] = choose(place.below, below, 0.0)
    pad_ref[upper, broad:] = choose(reached & place.above, above_side, 0.0)
    pad_ref[lower, broad:] = choose(reached & place.below, below_side, 0.0)
    pad_ref[REACH : REACH + tall, broad:] = choose(reached, side, 0.0)
    pad_ref[REACH : REACH + tall, :broad] = field


def convolve(pad_ref, kernel_ref, mix_ref, flipped):
    taps = 2 * REACH + 1
    tall, broad, lanes = mix_ref.shape
    ring = broad + EDGE
    sub = 128
    for start in range(0, lanes, sub):
        at = slice(start, start + sub)
        for y in range(tall):
            rows = [pad_ref[y + a, :, at] for a in range(taps)]
            total = None
            for b in range(taps):
                part = None
                for a in range(taps):
                    tap = taps * a + b
                    if flipped:
                        tap = taps * taps - 1 - tap
                    term = rows[a] * kernel_ref[tap : tap + 1, at]
                    part = term if part is None else part + term
                if b != REACH:
                    part = pltpu.roll(part, (REACH - b) % ring, 0)
                total = part[:broad] if total is None else total + part[:broad]
            mix_ref[y, :, at] = total


def read_field(ref, place, at=slice(None)):
    return jnp.where(place.live, ref[0, 0, :, :, at].astype(F32), 0.0)


def outgoing_kernel(routes, layout, key_ref, value_ref, *outs):
    place = Place(layout)
    for member, field_ref in enumerate((key_ref, value_ref)):
        field = field_ref[0, 0].astype(F32)
        for delta, out_ref in zip(routes.targets(place, True), outs):
            full = out_ref.shape[1] == REACH * field.shape[1]
            sent = payload(field, place, delta) if full else corner_payload(field, delta)
            out_ref[member] = sent.astype(BF16)


def thirds(ref, at):
    third = ref.shape[4] // 3
    return [slice(member * third + at.start, member * third + at.stop) for member in range(3)]


def source_state_kernel(routes, head_dim, layout, field_ref, *refs):
    weight_refs, outs, held, sems = refs[:2], refs[2:-3], refs[-3:-1], refs[-1]
    loads = [pltpu.make_async_copy(a, b, sems.at[i]) for i, (a, b) in enumerate(zip(weight_refs, held))]
    for load in loads:
        load.start()
    place = Place(layout)
    mask = same_head(head_dim)
    size = REACH * field_ref.shape[3]
    for at in parts_of(outs[0].shape[1]):
        query_at, key_at, value_at = thirds(field_ref, at)
        field = field_ref[0, 0, :, :, query_at].astype(F32)
        keys = jnp.maximum(read_field(field_ref, place, key_at).reshape(-1, LANES), 0.0)
        values = read_field(field_ref, place, value_at).reshape(-1, LANES)
        state = gather_blocks(contract(keys.astype(BF16), values.astype(BF16), TN), mask, head_dim)
        packed = pack_state(state, jnp.sum(keys, axis=0, keepdims=True))
        for delta, out_ref in zip(routes.targets(place), outs):
            out_ref[:size, at] = payload(field, place, delta).astype(BF16)
            out_ref[size:, at] = packed
    for load in loads:
        load.wait()


def forward_kernel(routes, first, count, head_dim, direct, *refs):
    layout, field_ref = refs[:2]
    place = Place(layout)
    deltas = routes.sources(place, direct)
    arrived, refs = refs[2 : 2 + len(deltas)], refs[2 + len(deltas) :]
    dw_ref, pw_ref, mixed_ref, merged_ref, padded_ref = refs[:5]
    mix_ref = refs[-1]
    mask = same_head(head_dim)
    per = mixed_ref.shape[2] // LANES
    size = REACH * field_ref.shape[3]

    def one_block(block, carry):
        at, member, within = lanes_at(first * per + block), block // per, lanes_at(block % per)
        field = read_field(field_ref, place, at)
        if len(arrived[0].shape) == 3:
            edges = [ref[member, :, within] for ref in arrived]
        else:
            edges = [ref[:size, within] for ref in arrived]
        padded = padded_ref.at[member, :, :, within]
        fill_padded(padded, field, edges, deltas, place)
        convolve(padded, dw_ref.at[:, at], mix_ref, False)
        mixed = mix_ref[...].reshape(-1, LANES)
        mixed_ref[member, :, within] = mixed
        merged_ref[member, :, within] = dot(split(mixed), split(spread(pw_ref[:, at], mask)), NN)
        return carry

    lax.fori_loop(0, count * per, one_block, 0)
    if first == 0:
        return
    state_ref = refs[-2]
    for at in parts_of(state_ref.shape[1]):
        keys = jnp.maximum(merged_ref[0, :, at], 0.0)
        state = gather_blocks(dot(split(keys), split(merged_ref[1, :, at]), TN), mask, head_dim)
        state_ref[:, at] = pack_state(state, jnp.sum(keys, axis=0, keepdims=True))


def parts_of(lanes):
    return [slice(start, start + LANES) for start in range(0, lanes, LANES)]


def query_gradients(raw, exactly, total, cot, head_dim, mask):
    ones = (mask.astype(BF16), None)
    query = jnp.maximum(raw, 0.0)
    pair = exact(query) if exactly else split(query)
    state = split(spread(total[:head_dim], mask))
    key_sum = total[head_dim : head_dim + 1]
    over = 1.0 / (dot(split(query * key_sum), ones, NN) + EPSILON)
    result = dot(pair, state, NN) * over
    grad_num = cot * over
    grad_den = -dot(split(cot * result), ones, NN) * over
    num_pair = split(grad_num)
    grad = jnp.where(raw > 0, dot(num_pair, state, NT) + grad_den * key_sum, 0.0)
    gstate = gather_blocks(dot(pair, num_pair, TN), mask, head_dim)
    return grad, pack_state(gstate, jnp.sum(query * grad_den, axis=0, keepdims=True))


def source_query_kernel(others, offset, others_offset, head_dim, *refs):
    layout, own_ref, received = refs[0], refs[1], refs[2 : 2 + others]
    source_ref, cot_ref, grad_ref, gstate_ref = refs[2 + others :]
    place = Place(layout)
    mask = same_head(head_dim)
    total = total_state(own_ref, received, place, offset, others_offset)
    for at in parts_of(gstate_ref.shape[1]):
        raw = read_field(source_ref, place, at).reshape(-1, LANES)
        cot = cot_ref[0, 0, :, :, at].astype(F32).reshape(raw.shape)
        grad_ref[0, :, at], gstate_ref[:, at] = query_gradients(raw, True, total[:, at], cot, head_dim, mask)


def merged_query_kernel(others, head_dim, *refs):
    layout, own_ref, received = refs[0], refs[1], refs[2 : 2 + others]
    merged_ref, mixed_ref, cot_ref, pw_ref, gstate_ref, gmix_ref, gpw_ref = refs[2 + others :]
    place = Place(layout)
    mask = same_head(head_dim)
    total = total_state(own_ref, received, place, 0, 0)
    third = gstate_ref.shape[1]
    for at in parts_of(third):
        raw = merged_ref[0, :, at]
        cot = cot_ref[0, 0, :, :, third + at.start : third + at.stop].astype(F32).reshape(raw.shape)
        grad, gstate_ref[:, at] = query_gradients(raw, False, total[:, at], cot, head_dim, mask)
        pair = split(grad)
        gmix_ref[0, :, at] = dot(pair, split(spread(pw_ref[:, at], mask)), NT)
        gpw_ref[0, :, at] = gather_blocks(dot(split(mixed_ref[0, :, at]), pair, TN), mask, head_dim)


def key_gradients(raw, key_pair, value_pair, total, head_dim, mask):
    gstate = split(spread(total[:head_dim], mask))
    gsum = total[head_dim : head_dim + 1]
    grad_keys = jnp.where(raw > 0, dot(value_pair, gstate, NT) + gsum, 0.0)
    return grad_keys, dot(key_pair, gstate, NN)


def source_value_kernel(others, offset, others_offset, head_dim, *refs):
    layout, own_ref, received = refs[0], refs[1], refs[2 : 2 + others]
    field_ref, grad_ref = refs[2 + others :]
    place = Place(layout)
    mask = same_head(head_dim)
    total = total_state(own_ref, received, place, offset, others_offset)
    for at in parts_of(grad_ref.shape[2]):
        _, key_at, value_at = thirds(field_ref, at)
        raw = read_field(field_ref, place, key_at).reshape(-1, LANES)
        values = read_field(field_ref, place, value_at).reshape(-1, LANES)
        grad_ref[0, :, at], grad_ref[1, :, at] = key_gradients(
            raw, exact(jnp.maximum(raw, 0.0)), exact(values), total[:, at], head_dim, mask
        )


def merged_value_kernel(others, routes, tall, head_dim, *refs):
    layout, own_ref, received = refs[0], refs[1], refs[2 : 2 + others]
    merged_ref, mixed_ref, pw_ref, qgmix_ref, packed_ref, gmix_ref, gpw_ref = refs[2 + others : 9 + others]
    outs = refs[9 + others :]
    place = Place(layout)
    mask = same_head(head_dim)
    total = total_state(own_ref, received, place, 0, 0)
    size = (outs[0].shape[0] - packed_ref.shape[0]) // 3

    def send(member, at, gmix):
        field = gmix.reshape(tall, -1, LANES)
        for delta, out_ref in zip(routes.targets(place), outs):
            out_ref[member * size : (member + 1) * size, at] = payload(field, place, delta).astype(BF16)

    for at in parts_of(gmix_ref.shape[2]):
        for out_ref in outs:
            out_ref[3 * size :, at] = packed_ref[:, at]
        send(0, at, qgmix_ref[0, :, at])
        raw = merged_ref[0, :, at]
        pairs = split(jnp.maximum(raw, 0.0)), split(merged_ref[1, :, at])
        grads = key_gradients(raw, *pairs, total[:, at], head_dim, mask)
        third = gmix_ref.shape[2]
        for member, grad in enumerate(grads):
            pair = split(grad)
            begin = (1 + member) * third + at.start
            gmix = dot(pair, split(spread(pw_ref[:, begin : begin + LANES], mask)), NT)
            gmix_ref[member, :, at] = gmix
            gpw_ref[member, :, at] = gather_blocks(dot(split(mixed_ref[member, :, at]), pair, TN), mask, head_dim)
            send(1 + member, at, gmix)


def weight_kernel(halves, layout, padded_ref, gmix_ref, gpw_ref, *refs):
    outs, sum_ref = refs[:-1], refs[-1]
    ring, sub = padded_ref.shape[2], 128
    tall, broad = padded_ref.shape[1] - 2 * REACH, ring - EDGE
    taps = 2 * REACH + 1
    count, head_dim, third = gpw_ref.shape
    start = sum_ref.shape[0] - head_dim
    odd = Place(layout).group % 2 == 1
    each = third // sub

    def one_block(block, carry):
        member = block // each
        at = pl.ds(pl.multiple_of(block % each * sub, sub), sub)
        out_at = pl.ds(pl.multiple_of(block * sub, sub), sub)

        def one_row(y, totals):
            grad = gmix_ref[member, pl.ds(pl.multiple_of(y * broad, broad), broad), at]
            grad = jnp.concatenate([grad, jnp.zeros((EDGE, sub), F32)], axis=0)
            moved = [grad if b == REACH else pltpu.roll(grad, (b - REACH) % ring, 0) for b in range(taps)]
            new = list(totals)
            for a in range(taps):
                row = padded_ref[member, y + a, :, at]
                for b in range(taps):
                    term = (row * moved[b]).reshape(ring // 8, 8, sub)
                    new[taps * a + b] = new[taps * a + b] + jnp.sum(term, axis=0)
            return tuple(new)

        zero = jnp.zeros((8, sub), F32)
        totals = lax.fori_loop(0, tall, one_row, (zero,) * (taps * taps), unroll=2)
        for tap in range(taps * taps):
            sum_ref[tap : tap + 1] = jnp.sum(totals[tap], axis=0, keepdims=True)
        sum_ref[taps * taps : start] = jnp.zeros((start - taps * taps, sub), F32)
        sum_ref[start:] = gpw_ref[member, :, at]
        if not halves:
            outs[0][:, out_at] = sum_ref[...]
            return carry
        rows = outs[0].shape[1]
        for part in range(outs[0].shape[0]):
            even_rows = sum_ref[2 * part * rows : (2 * part + 1) * rows]
            odd_rows = sum_ref[(2 * part + 1) * rows : (2 * part + 2) * rows]
            outs[0][part, :, out_at] = jnp.where(odd, even_rows, odd_rows)
            outs[1][part, :, out_at] = jnp.where(odd, odd_rows, even_rows)
        return carry

    lax.fori_loop(0, count * each, one_block, 0)


def scatter_kernel(layout, keep_q, come_q, keep_kv, come_kv, own_ref, *outs):
    quarter = Place(layout).group // 2
    third = keep_q.shape[2]
    for m, out_ref in enumerate((own_ref,) + outs):
        at = quarter ^ m
        out_ref[:, :third] = keep_q[at] + come_q[at]
        out_ref[:, third:] = keep_kv[at] + come_kv[at]


def sum_kernel(norm, *refs):
    parts, out_ref = [ref[...] for ref in refs[:-1]], refs[-1]
    while len(parts) > 1:
        parts = [parts[i] + parts[i + 1] for i in range(0, len(parts), 2)]
    out_ref[...] = parts[0] * norm


def collect_kernel(layout, *refs):
    parts, out_ref = refs[:-1], refs[-1]
    quarter = Place(layout).group // 2
    for m, part in enumerate(parts):
        out_ref[quarter ^ m] = part[...]


def finish_kernel(taps, layout, own_ref, come_ref, dw_ref, pw_ref, whole_ref):
    odd = Place(layout).group % 2 == 1
    quarters, rows = own_ref.shape[:2]
    for part in range(quarters):
        own, come = own_ref[part], come_ref[part]
        whole_ref[2 * part * rows : (2 * part + 1) * rows] = jnp.where(odd, come, own)
        whole_ref[(2 * part + 1) * rows : (2 * part + 2) * rows] = jnp.where(odd, own, come)
    dw_ref[...] = whole_ref[:taps]
    pw_ref[...] = whole_ref[whole_ref.shape[0] - pw_ref.shape[0] :]


def copy_kernel(*refs):
    half = len(refs) // 2
    for in_ref, out_ref in zip(refs[:half], refs[half:]):
        out_ref[...] = in_ref[...]


def backward_kernel(routes, first, *refs):
    layout, gmix_ref = refs[:2]
    arrived = refs[2 : 2 + routes.arriving]
    dw_ref, grad0_ref, out_ref, pad_ref, mix_ref, done_ref, sems = refs[2 + routes.arriving :]
    place = Place(layout)
    deltas = routes.sources(place)
    tall, broad = out_ref.shape[2:4]
    count, _, third = gmix_ref.shape
    per, size = third // LANES, REACH * broad

    def one_block(block, carry):
        at, member, within = lanes_at(first * per + block), block // per, lanes_at(block % per)
        begin = pl.multiple_of((first + member) * size, size)
        edges = [ref[pl.ds(begin, size), within] for ref in arrived]
        field = gmix_ref[member, :, within].reshape(tall, broad, LANES)
        fill_padded(pad_ref, field, edges, deltas, place)
        convolve(pad_ref, dw_ref.at[:, at], mix_ref, True)
        grad = mix_ref[...] + grad0_ref[member, :, within].reshape(tall, broad, LANES)
        done_ref[block] = jnp.where(place.live, grad, 0.0).astype(BF16)
        write(block).start()
        return carry

    def write(block):
        target = out_ref.at[0, 0, :, :, lanes_at(first * per + block)]
        return pltpu.make_async_copy(done_ref.at[block], target, sems.at[block])

    lax.fori_loop(0, count * per, one_block, 0)
    for block in range(count * per):
        write(block).wait()


def in_hbm(x):
    return pltpu.with_memory_space_constraint(x, pltpu.HBM)


def call(cost, kernel, out_shape, args, scratch=(), after=(), in_place=0, out_space=pltpu.VMEM, onto=()):
    inputs, extra = len(args), len(onto) + len(after)

    def body(*refs):
        kernel(*refs[:inputs], *refs[inputs + extra :])

    spaces = [pltpu.SMEM if x.dtype == jnp.int32 else pltpu.VMEM for x in args]
    spaces[inputs - in_place :] = [pl.ANY] * in_place
    spaces += [out_space] * len(onto) + [pl.ANY] * len(after)
    return pl.pallas_call(
        body,
        in_specs=[pl.BlockSpec(memory_space=space) for space in spaces],
        out_specs=jax.tree.map(lambda _: pl.BlockSpec(memory_space=out_space), out_shape),
        out_shape=out_shape,
        scratch_shapes=list(scratch),
        input_output_aliases={inputs: 0} if onto else {},
        compiler_params=PARAMS,
        cost_estimate=pl.CostEstimate(
            flops=0, bytes_accessed=int(cost * BYTES_PER_US), transcendentals=0
        ),
    )(*args, *onto, *after)


def local(
    qkv, cotangent, dw_weight, pw_weight, tile_image, tile_row, tile_col, image_height, image_width
):
    tall, broad, channels = qkv.shape[2:]
    positions = tall * broad
    head_dim = pw_weight.shape[0]
    taps = dw_weight.shape[0]
    third = channels // 3
    tiles, groups = lax.axis_size("tile"), lax.axis_size("img")
    routes = Routes(tiles)
    edge = REACH * broad
    packed = 2 * (head_dim + 8)
    padded_shape = (tall + 2 * REACH, broad + EDGE)
    spot = lax.axis_index("img").astype(jnp.int32)
    scalars = (tile_image, tile_row, tile_col, spot, image_height, image_width)
    layout = jnp.concatenate([x.reshape(-1) for x in scalars])
    part = functools.partial

    def wide(*dims):
        return jax.ShapeDtypeStruct(dims, F32)

    def narrow(*dims):
        return jax.ShapeDtypeStruct(dims, BF16)

    mix_scratch = [pltpu.VMEM((tall, broad, LANES), F32)]
    low, high = edge, edge + packed

    sent_kv = pl.pallas_call(
        part(outgoing_kernel, routes),
        grid=(1,),
        in_specs=[pl.BlockSpec(memory_space=pltpu.SMEM)]
        + [pl.BlockSpec((1, 1, tall, broad, third), lambda j, m=m: (0, 0, 0, 0, m)) for m in (1, 2)],
        out_specs=[pl.BlockSpec((2, size, third), lambda j: (0, 0, 0)) for size in routes.direct_rows(edge)],
        out_shape=[narrow(2, size, third) for size in routes.direct_rows(edge)],
        compiler_params=PARAMS,
    )(layout, in_hbm(qkv), in_hbm(qkv))
    halo_kv = routes.move_direct(sent_kv)
    *sent_q, dw_weight, pw_weight = call(
        1.0,
        part(source_state_kernel, routes, head_dim),
        [narrow(high, third)] * routes.sent + [wide(taps, channels), wide(head_dim, channels)],
        (layout, qkv, in_hbm(dw_weight), in_hbm(pw_weight)),
        [pltpu.SemaphoreType.DMA((2,))],
        in_place=2,
    )
    sent_q = call(0.3, copy_kernel, [narrow(high, third)] * routes.sent, sent_q, after=tuple(halo_kv))

    def forward(first, count, halo, direct):
        return call(
            1.5 * count * third / LANES,
            part(forward_kernel, routes, first, count, head_dim, direct),
            [wide(count, positions, third)] * 2
            + [wide(count, *padded_shape, third)]
            + [narrow(packed, third)] * (first > 0),
            (layout, qkv, *halo, dw_weight, pw_weight),
            mix_scratch,
        )

    mixed_kv, merged_kv, padded_kv, state = forward(1, 2, halo_kv, True)

    def copied(far, tokens):
        return call(0.3, copy_kernel, jax.ShapeDtypeStruct(far.shape, far.dtype), (far,), after=tokens)

    halo_q = routes.move(sent_q, hand_on=lambda near, far: copied(far, (state,)))
    state_from = exchange(state, "tile")
    others = len(state_from)
    mixed_q, merged_q, padded_q = forward(0, 1, halo_q, False)

    gstate, gmix_q, gpw_q = call(
        3.0,
        part(merged_query_kernel, others, head_dim),
        [narrow(packed, third), wide(1, positions, third), wide(1, head_dim, third)],
        (layout, state, *state_from, merged_q, mixed_q, cotangent, pw_weight),
    )
    gstate_from = exchange(gstate, "tile")

    source_from = halo_q if routes.relayed else exchange(sent_q[0][low:], "tile")
    from_offset = low if routes.relayed else 0
    grad0_q, gstate0 = call(
        2.5,
        part(source_query_kernel, others, low, from_offset, head_dim),
        [wide(1, positions, third), narrow(packed, third)],
        (layout, sent_q[0], *source_from, qkv, cotangent),
        after=(gstate,),
    )

    gap = -(-taps // 8) * 8
    rows = gap + head_dim
    halves = groups == 8 and rows % groups == 0
    eighth = rows // groups

    def weights(count, padded, gmix, gpw):
        return call(
            1.0 * count * third / LANES,
            part(weight_kernel, halves),
            [wide(4, eighth, count * third)] * 2 if halves else [wide(rows, count * third)],
            (layout, padded, gmix, gpw),
            [pltpu.VMEM((rows, 128), F32)],
        )

    weights_q = weights(1, padded_q, gmix_q, gpw_q)
    total_rows = 3 * edge + packed
    gmix_kv, gpw_kv, *sent_back = call(
        3.0,
        part(merged_value_kernel, others, routes, tall, head_dim),
        [wide(2, positions, third), wide(2, head_dim, third)] + [narrow(total_rows, third)] * routes.sent,
        (layout, gstate, *gstate_from, merged_kv, mixed_kv, pw_weight, gmix_q, gstate0),
        after=(weights_q[0],),
    )
    weights_kv = weights(2, padded_kv, gmix_kv, gpw_kv)

    norm = 1.0 / math.sqrt(positions * tiles * groups)
    ready = weights_kv
    if halves:
        come_q = exchange(weights_q[0], "img", (1,))[0]
        come_kv = exchange(weights_kv[0], "img", (1,))[0]
        share_shape = wide(eighth, channels)
        shares = call(
            0.5, scatter_kernel, [share_shape] * 4, (layout, weights_q[1], come_q, weights_kv[1], come_kv)
        )
        moved = [
            lax.ppermute(share, "img", [(s, s ^ (2 * m)) for s in range(groups)])
            for m, share in enumerate(shares[1:], 1)
        ]
        ready = shares[:1]

    halo_back = routes.move(sent_back, hand_on=lambda near, far: copied(far, (near, *ready)))

    back_from = halo_back if routes.relayed else exchange(sent_back[0][3 * edge :], "tile")
    back_offset = 3 * edge if routes.relayed else 0
    grad0_kv = call(
        1.5,
        part(source_value_kernel, others, 3 * edge, back_offset, head_dim),
        wide(2, positions, third),
        (layout, sent_back[0], *back_from, qkv),
    )

    def backward(first, gmix, grad0, onto=()):
        blocks = gmix.shape[0] * third // LANES
        return call(
            1.0 * blocks,
            part(backward_kernel, routes, first),
            pltpu.HBM((1, 1, tall, broad, channels), BF16),
            (layout, gmix, *halo_back, dw_weight, grad0),
            [pltpu.VMEM((*padded_shape, LANES), F32)]
            + mix_scratch
            + [pltpu.VMEM((blocks, tall, broad, LANES), BF16), pltpu.SemaphoreType.DMA((blocks,))],
            out_space=pltpu.HBM,
            onto=onto,
        )

    grad_query = in_hbm(backward(0, gmix_q, grad0_q))
    grad_source = backward(1, gmix_kv, grad0_kv, (grad_query,))

    if halves:
        total = call(0.3, part(sum_kernel, 1.0), share_shape, [shares[0]] + moved)
        total = call(
            0.3, part(sum_kernel, norm), share_shape, [total] + exchange(total, "tile"), after=(grad_query,)
        )
        quarters = call(
            0.5,
            collect_kernel,
            wide(4, eighth, channels),
            (layout, total, *exchange(total, "img", (2, 4, 6))),
            after=(in_hbm(grad_source),),
        )
        grad_dw, grad_pw = call(
            0.8,
            part(finish_kernel, taps),
            [wide(taps, channels), wide(head_dim, channels)],
            (layout, quarters, exchange(quarters, "img", (1,))[0]),
            [pltpu.VMEM((rows, channels), F32)],
        )
    else:
        whole = jnp.concatenate([weights_q[0], weights_kv[0]], axis=1)
        whole = lax.psum(whole, ("tile", "img")) * norm
        grad_dw, grad_pw = whole[:taps], whole[gap:]
    return grad_source, grad_dw, grad_pw


def solution(mesh):
    placed = (
        P("img", "tile", None, None, None),
        P("img", "tile", None, None, None),
        P(),
        P(),
        P("img", "tile"),
        P("img", "tile"),
        P("img", "tile"),
        P("img", None),
        P("img", None),
    )
    return jax.shard_map(
        local,
        mesh=mesh,
        in_specs=placed,
        out_specs=(P("img", "tile", None, None, None), P(), P()),
        check_vma=False,
    )
```

```python
import functools
import math

import jax
import jax.numpy as jnp
from jax import lax
from jax.experimental import pallas as pl
from jax.experimental.pallas import tpu as pltpu
from jax.sharding import PartitionSpec as P

EPSILON = 1e-06
LANES = 256
REACH = 2
EDGE = 8
BYTES_PER_US = 3_690_000
BF16 = jnp.bfloat16
F32 = jnp.float32
PARAMS = pltpu.CompilerParams(vmem_limit_bytes=16 * 1024 * 1024)


class Place:
    def __init__(self, info_ref):
        slots = (info_ref.shape[0] - 4) // 2
        slot = info_ref[0]
        tall = wide = start = jnp.int32(0)
        for s in range(slots):
            tall_s, wide_s = info_ref[4 + s], info_ref[4 + slots + s]
            tall = jnp.where(slot == s, tall_s, tall)
            wide = jnp.where(slot == s, wide_s, wide)
            start = start + jnp.where(s < slot, tall_s * wide_s, 0)
        self.live = slot < slots
        self.tall, self.wide = tall, wide
        self.row, self.col = info_ref[1], info_ref[2]
        self.group = info_ref[3]
        self.within = self.row * wide + self.col
        self.index = start + self.within
        self.above = self.live & (self.row > 0)
        self.below = self.live & (self.row < tall - 1)

    def same_image(self, delta):
        other = self.within + delta
        return self.live & (other >= 0) & (other < self.tall * self.wide)


class Routes:
    def __init__(self, count):
        self.count = count
        self.relayed = count == 4
        self.shifts = [k for k in (1, -1, 2, -2, 3, -3) if abs(k) < count]
        self.sent = 2 if self.relayed else len(self.shifts)
        self.arriving = 3 if self.relayed else len(self.shifts)

    def targets(self, place, direct=False):
        if not self.relayed:
            return [jnp.int32(k) for k in self.shifts]
        near, far, last = ((place.index ^ m) - place.index for m in (1, 2, 3))
        if direct:
            return [near, far, last, last]
        return [near, jnp.where(place.same_image(far), far, last)]

    def sources(self, place, direct=False):
        if not self.relayed:
            return [jnp.int32(-k) for k in self.shifts]
        near, far, last = ((place.index ^ m) - place.index for m in (1, 2, 3))
        if direct:
            outer = jnp.abs(last) == 3
            return [near, far, jnp.where(outer, 0, last), jnp.where(outer, last, 0)]
        return [near, far, last]

    def direct_rows(self, edge):
        return [edge, edge, edge, REACH * EDGE] if self.relayed else [edge] * self.sent

    def move(self, sent, hand_on=lambda near, far: far):
        count = self.count
        if not self.relayed:
            return [
                lax.ppermute(part, "tile", [(s, s + k) for s in range(max(0, -k), min(count, count - k))])
                for part, k in zip(sent, self.shifts)
            ]
        near, far = (
            lax.ppermute(part, "tile", [(s, s ^ m) for s in range(count)]) for part, m in zip(sent, (1, 2))
        )
        return [near, far, lax.ppermute(hand_on(near, far), "tile", [(s, s ^ 1) for s in range(count)])]

    def move_direct(self, sent):
        if not self.relayed:
            return self.move(sent)
        targets = ((1, 0, 3, 2), (2, 3, 0, 1), (0, 2, 1, 3), (3, 1, 2, 0))
        return [lax.ppermute(part, "tile", list(enumerate(to))) for part, to in zip(sent, targets)]


def exchange(value, axis, masks=None):
    count = lax.axis_size(axis)
    masks = range(1, count) if masks is None else masks
    return [lax.ppermute(value, axis, [(s, s ^ m) for s in range(count)]) for m in masks]


def split(x):
    high = x.astype(BF16)
    return high, (x - high.astype(F32)).astype(BF16)


def contract(a, b, dims):
    return lax.dot_general(a, b, (dims, ((), ())), preferred_element_type=F32)


NN = ((1,), (0,))
NT = ((1,), (1,))
TN = ((0,), (0,))


def dot(a, b, dims):
    total = contract(a[0], b[0], dims)
    if b[1] is not None:
        total = total + contract(a[0], b[1], dims)
    if a[1] is not None:
        total = total + contract(a[1], b[0], dims)
    return total


def exact(x):
    return x.astype(BF16), None


def same_head(head_dim):
    rows = lax.broadcasted_iota(jnp.int32, (LANES, LANES), 0) // head_dim
    cols = lax.broadcasted_iota(jnp.int32, (LANES, LANES), 1) // head_dim
    return rows == cols


def spread(compact, mask):
    tall = jnp.concatenate([compact] * (LANES // compact.shape[0]), axis=0)
    return jnp.where(mask, tall, 0.0)


def gather_blocks(full, mask, head_dim):
    kept = jnp.where(mask, full, 0.0)
    return jnp.sum(kept.reshape(LANES // head_dim, head_dim, LANES), axis=0)


def payload(field, place, delta):
    tall, broad, lanes = field.shape
    size = REACH * broad
    top = field[:REACH].reshape(size, lanes)
    bottom = field[tall - REACH :].reshape(size, lanes)
    left = field[:, :EDGE].reshape(size, lanes)
    right = field[:, broad - EDGE :].reshape(size, lanes)
    rows = jnp.where(delta > 0, bottom, top)
    cols = jnp.where(place.col == 0, right, left)
    beside = (place.wide == 2) & (delta == jnp.where(place.col == 0, 1, -1))
    return jnp.where(beside, cols, rows)


def lanes_at(block):
    start = block * LANES
    return pl.ds(start if isinstance(start, int) else pl.multiple_of(start, LANES), LANES)


def pack_state(state, total):
    rows = jnp.concatenate([state, total, jnp.zeros((7, state.shape[1]), F32)], axis=0)
    return jnp.concatenate(split(rows), axis=0)


def unpack_state(ref, offset):
    rows = ref[offset:].astype(F32)
    half = rows.shape[0] // 2
    return rows[:half] + rows[half:]


def total_state(own_ref, others, place, offset, others_offset):
    total = unpack_state(own_ref, offset)
    for m, other in enumerate(others, 1):
        delta = (place.index ^ m) - place.index
        total = total + jnp.where(place.same_image(delta), unpack_state(other, others_offset), 0.0)
    return total


def corner_payload(field, delta):
    tall, broad, lanes = field.shape
    corner = jnp.where(delta > 0, field[tall - REACH :, broad - EDGE :], field[:REACH, :EDGE])
    return corner.reshape(REACH * EDGE, lanes)


def fill_padded(pad_ref, field, arrived, deltas, place):
    tall, broad, lanes = field.shape
    two = place.live & (place.wide == 2)
    one = place.live & (place.wide == 1)
    first, second = two & (place.col == 0), two & (place.col == 1)

    def choose(condition, value, other):
        return jnp.where(condition, value, other)

    above = below = jnp.zeros((REACH, broad, lanes), F32)
    above_side = below_side = jnp.zeros((REACH, EDGE, lanes), F32)
    side = jnp.zeros((tall, EDGE, lanes), F32)
    for edges, delta in zip(arrived, deltas):
        edges = edges.astype(F32)
        if edges.shape[0] == REACH * EDGE:
            corner = edges.reshape(REACH, EDGE, lanes)
            above_side = choose(second & (delta == -3), corner, above_side)
            below_side = choose(first & (delta == 3), corner, below_side)
            continue
        rows, cols = edges.reshape(REACH, broad, lanes), edges.reshape(tall, EDGE, lanes)
        begin, end = rows[:, :EDGE], rows[:, broad - EDGE :]
        above = choose((one & (delta == -1)) | (two & (delta == -2)), rows, above)
        below = choose((one & (delta == 1)) | (two & (delta == 2)), rows, below)
        side = choose((first & (delta == 1)) | (second & (delta == -1)), cols, side)
        above_side = choose(first & (delta == -1), begin, choose(second & (delta == -3), end, above_side))
        below_side = choose(second & (delta == 1), end, choose(first & (delta == 3), begin, below_side))
    column = lax.broadcasted_iota(jnp.int32, (1, EDGE, lanes), 1)
    reached = (first & (column < REACH)) | (second & (column >= EDGE - REACH))
    upper, lower = slice(0, REACH), slice(REACH + tall, 2 * REACH + tall)
    pad_ref[upper, :broad] = choose(place.above, above, 0.0)
    pad_ref[lower, :broad] = choose(place.below, below, 0.0)
    pad_ref[upper, broad:] = choose(reached & place.above, above_side, 0.0)
    pad_ref[lower, broad:] = choose(reached & place.below, below_side, 0.0)
    pad_ref[REACH : REACH + tall, broad:] = choose(reached, side, 0.0)
    pad_ref[REACH : REACH + tall, :broad] = field


def convolve(pad_ref, kernel_ref, emit, flipped):
    taps = 2 * REACH + 1
    tall, broad, lanes = pad_ref.shape[0] - 2 * REACH, pad_ref.shape[1] - EDGE, pad_ref.shape[2]
    ring = broad + EDGE
    sub = 128
    for start in range(0, lanes, sub):
        at = slice(start, start + sub)
        for y in range(tall):
            rows = [pad_ref[y + a, :, at] for a in range(taps)]
            total = None
            for b in range(taps):
                part = None
                for a in range(taps):
                    tap = taps * a + b
                    if flipped:
                        tap = taps * taps - 1 - tap
                    row = rows[a][:broad] if b == REACH else rows[a]
                    term = row * kernel_ref[tap : tap + 1, at]
                    part = term if part is None else part + term
                if b != REACH:
                    part = pltpu.roll(part, (REACH - b) % ring, 0)
                total = part[:broad] if total is None else total + part[:broad]
            emit(y, at, total)


def read_field(ref, place, at=slice(None)):
    return jnp.where(place.live, ref[0, 0, :, :, at].astype(F32), 0.0)


def outgoing_kernel(routes, layout, key_ref, value_ref, *outs):
    place = Place(layout)
    for member, field_ref in enumerate((key_ref, value_ref)):
        field = field_ref[0, 0].astype(F32)
        for delta, out_ref in zip(routes.targets(place, True), outs):
            full = out_ref.shape[1] == REACH * field.shape[1]
            sent = payload(field, place, delta) if full else corner_payload(field, delta)
            out_ref[member] = sent.astype(BF16)


def thirds(ref, at):
    third = ref.shape[4] // 3
    return [slice(member * third + at.start, member * third + at.stop) for member in range(3)]


def source_state_kernel(routes, head_dim, layout, field_ref, *refs):
    weight_refs, outs, held, sems = refs[:2], refs[2:-3], refs[-3:-1], refs[-1]
    loads = [pltpu.make_async_copy(a, b, sems.at[i]) for i, (a, b) in enumerate(zip(weight_refs, held))]
    for load in loads:
        load.start()
    place = Place(layout)
    mask = same_head(head_dim)
    size = REACH * field_ref.shape[3]
    for at in parts_of(outs[0].shape[1]):
        query_at, key_at, value_at = thirds(field_ref, at)
        field = field_ref[0, 0, :, :, query_at].astype(F32)
        keys = jnp.maximum(read_field(field_ref, place, key_at).reshape(-1, LANES), 0.0)
        values = read_field(field_ref, place, value_at).reshape(-1, LANES)
        state = gather_blocks(contract(keys.astype(BF16), values.astype(BF16), TN), mask, head_dim)
        packed = pack_state(state, jnp.sum(keys, axis=0, keepdims=True))
        for delta, out_ref in zip(routes.targets(place), outs):
            out_ref[:size, at] = payload(field, place, delta).astype(BF16)
            out_ref[size:, at] = packed
    for load in loads:
        load.wait()


def forward_kernel(routes, first, count, head_dim, direct, *refs):
    layout, field_ref = refs[:2]
    place = Place(layout)
    deltas = routes.sources(place, direct)
    arrived, refs = refs[2 : 2 + len(deltas)], refs[2 + len(deltas) :]
    dw_ref, pw_ref, mixed_ref, merged_ref, padded_ref = refs[:5]
    mask = same_head(head_dim)
    per = mixed_ref.shape[2] // LANES
    size = REACH * field_ref.shape[3]

    def one_block(block, carry):
        at, member, within = lanes_at(first * per + block), block // per, lanes_at(block % per)
        field = read_field(field_ref, place, at)
        if len(arrived[0].shape) == 3:
            edges = [ref[member, :, within] for ref in arrived]
        else:
            edges = [ref[:size, within] for ref in arrived]
        padded = padded_ref.at[member, :, :, within]
        fill_padded(padded, field, edges, deltas, place)
        target = mixed_ref.at[member, :, within]
        broad = field.shape[1]

        def emit(y, sub, total):
            target[y * broad : (y + 1) * broad, sub] = total

        convolve(padded, dw_ref.at[:, at], emit, False)
        mixed = target[...]
        merged_ref[member, :, within] = dot(split(mixed), split(spread(pw_ref[:, at], mask)), NN)
        return carry

    lax.fori_loop(0, count * per, one_block, 0, unroll=2)
    if first == 0:
        return
    state_ref = refs[5]
    for at in parts_of(state_ref.shape[1]):
        keys = jnp.maximum(merged_ref[0, :, at], 0.0)
        state = gather_blocks(dot(split(keys), split(merged_ref[1, :, at]), TN), mask, head_dim)
        state_ref[:, at] = pack_state(state, jnp.sum(keys, axis=0, keepdims=True))


def parts_of(lanes):
    return [slice(start, start + LANES) for start in range(0, lanes, LANES)]


def query_gradients(raw, exactly, total, cot, head_dim, mask):
    ones = (mask.astype(BF16), None)
    query = jnp.maximum(raw, 0.0)
    pair = exact(query) if exactly else split(query)
    state = split(spread(total[:head_dim], mask))
    key_sum = total[head_dim : head_dim + 1]
    over = 1.0 / (dot(split(query * key_sum), ones, NN) + EPSILON)
    result = dot(pair, state, NN) * over
    grad_num = cot * over
    grad_den = -dot(split(cot * result), ones, NN) * over
    num_pair = split(grad_num)
    grad = jnp.where(raw > 0, dot(num_pair, state, NT) + grad_den * key_sum, 0.0)
    gstate = gather_blocks(dot(pair, num_pair, TN), mask, head_dim)
    return grad, pack_state(gstate, jnp.sum(query * grad_den, axis=0, keepdims=True))


def source_query_kernel(others, offset, others_offset, head_dim, *refs):
    layout, own_ref, received = refs[0], refs[1], refs[2 : 2 + others]
    source_ref, cot_ref, grad_ref, gstate_ref = refs[2 + others :]
    place = Place(layout)
    mask = same_head(head_dim)
    total = total_state(own_ref, received, place, offset, others_offset)
    for at in parts_of(gstate_ref.shape[1]):
        raw = read_field(source_ref, place, at).reshape(-1, LANES)
        cot = cot_ref[0, 0, :, :, at].astype(F32).reshape(raw.shape)
        grad_ref[0, :, at], gstate_ref[:, at] = query_gradients(raw, True, total[:, at], cot, head_dim, mask)


def merged_query_kernel(others, head_dim, *refs):
    layout, own_ref, received = refs[0], refs[1], refs[2 : 2 + others]
    merged_ref, mixed_ref, cot_ref, pw_ref, gstate_ref, gmix_ref, gpw_ref = refs[2 + others :]
    place = Place(layout)
    mask = same_head(head_dim)
    total = total_state(own_ref, received, place, 0, 0)
    third = gstate_ref.shape[1]
    for at in parts_of(third):
        raw = merged_ref[0, :, at]
        cot = cot_ref[0, 0, :, :, third + at.start : third + at.stop].astype(F32).reshape(raw.shape)
        grad, gstate_ref[:, at] = query_gradients(raw, False, total[:, at], cot, head_dim, mask)
        pair = split(grad)
        gmix_ref[0, :, at] = dot(pair, split(spread(pw_ref[:, at], mask)), NT)
        gpw_ref[0, :, at] = gather_blocks(dot(split(mixed_ref[0, :, at]), pair, TN), mask, head_dim)


def key_gradients(raw, key_pair, value_pair, total, head_dim, mask):
    gstate = split(spread(total[:head_dim], mask))
    gsum = total[head_dim : head_dim + 1]
    grad_keys = jnp.where(raw > 0, dot(value_pair, gstate, NT) + gsum, 0.0)
    return grad_keys, dot(key_pair, gstate, NN)


def source_value_kernel(others, offset, others_offset, head_dim, *refs):
    layout, own_ref, received = refs[0], refs[1], refs[2 : 2 + others]
    field_ref, grad_ref = refs[2 + others :]
    place = Place(layout)
    mask = same_head(head_dim)
    total = total_state(own_ref, received, place, offset, others_offset)
    for at in parts_of(grad_ref.shape[2]):
        _, key_at, value_at = thirds(field_ref, at)
        raw = read_field(field_ref, place, key_at).reshape(-1, LANES)
        values = read_field(field_ref, place, value_at).reshape(-1, LANES)
        grad_ref[0, :, at], grad_ref[1, :, at] = key_gradients(
            raw, exact(jnp.maximum(raw, 0.0)), exact(values), total[:, at], head_dim, mask
        )


def merged_value_kernel(others, routes, tall, head_dim, *refs):
    layout, own_ref, received = refs[0], refs[1], refs[2 : 2 + others]
    merged_ref, mixed_ref, pw_ref, qgmix_ref, packed_ref, gmix_ref, gpw_ref = refs[2 + others : 9 + others]
    outs = refs[9 + others :]
    place = Place(layout)
    mask = same_head(head_dim)
    total = total_state(own_ref, received, place, 0, 0)
    size = (outs[0].shape[0] - packed_ref.shape[0]) // 3

    def send(member, at, gmix):
        field = gmix.reshape(tall, -1, LANES)
        for delta, out_ref in zip(routes.targets(place), outs):
            out_ref[member * size : (member + 1) * size, at] = payload(field, place, delta).astype(BF16)

    for at in parts_of(gmix_ref.shape[2]):
        for out_ref in outs:
            out_ref[3 * size :, at] = packed_ref[:, at]
        send(0, at, qgmix_ref[0, :, at])
        raw = merged_ref[0, :, at]
        pairs = split(jnp.maximum(raw, 0.0)), split(merged_ref[1, :, at])
        grads = key_gradients(raw, *pairs, total[:, at], head_dim, mask)
        third = gmix_ref.shape[2]
        for member, grad in enumerate(grads):
            pair = split(grad)
            begin = (1 + member) * third + at.start
            gmix = dot(pair, split(spread(pw_ref[:, begin : begin + LANES], mask)), NT)
            gmix_ref[member, :, at] = gmix
            gpw_ref[member, :, at] = gather_blocks(dot(split(mixed_ref[member, :, at]), pair, TN), mask, head_dim)
            send(1 + member, at, gmix)


def weight_kernel(halves, layout, padded_ref, gmix_ref, gpw_ref, *refs):
    outs, sum_ref = refs[:-1], refs[-1]
    ring, sub = padded_ref.shape[2], 128
    tall, broad = padded_ref.shape[1] - 2 * REACH, ring - EDGE
    taps = 2 * REACH + 1
    count, head_dim, third = gpw_ref.shape
    start = sum_ref.shape[0] - head_dim
    odd = Place(layout).group % 2 == 1
    each = third // sub

    def one_block(block, carry):
        member = block // each
        at = pl.ds(pl.multiple_of(block % each * sub, sub), sub)
        out_at = pl.ds(pl.multiple_of(block * sub, sub), sub)

        def one_row(y, totals):
            grad = gmix_ref[member, pl.ds(pl.multiple_of(y * broad, broad), broad), at]
            longer = jnp.concatenate([grad, jnp.zeros((EDGE, sub), F32)], axis=0)
            moved = [grad if b == REACH else pltpu.roll(longer, (b - REACH) % ring, 0) for b in range(taps)]
            new = list(totals)
            for a in range(taps):
                row = padded_ref[member, y + a, :, at]
                for b in range(taps):
                    term = row[: moved[b].shape[0]] * moved[b]
                    term = term.reshape(term.shape[0] // 8, 8, sub)
                    new[taps * a + b] = new[taps * a + b] + jnp.sum(term, axis=0)
            return tuple(new)

        zero = jnp.zeros((8, sub), F32)
        totals = lax.fori_loop(0, tall, one_row, (zero,) * (taps * taps), unroll=2)
        for tap in range(taps * taps):
            sum_ref[tap : tap + 1] = jnp.sum(totals[tap], axis=0, keepdims=True)
        sum_ref[taps * taps : start] = jnp.zeros((start - taps * taps, sub), F32)
        sum_ref[start:] = gpw_ref[member, :, at]
        if not halves:
            outs[0][:, out_at] = sum_ref[...]
            return carry
        rows = outs[0].shape[1]
        for part in range(outs[0].shape[0]):
            even_rows = sum_ref[2 * part * rows : (2 * part + 1) * rows]
            odd_rows = sum_ref[(2 * part + 1) * rows : (2 * part + 2) * rows]
            outs[0][part, :, out_at] = jnp.where(odd, even_rows, odd_rows)
            outs[1][part, :, out_at] = jnp.where(odd, odd_rows, even_rows)
        return carry

    lax.fori_loop(0, count * each, one_block, 0)


def scatter_kernel(layout, keep_q, come_q, keep_kv, come_kv, own_ref, *outs):
    quarter = Place(layout).group // 2
    third = keep_q.shape[2]
    for m, out_ref in enumerate((own_ref,) + outs):
        at = quarter ^ m
        out_ref[:, :third] = keep_q[at] + come_q[at]
        out_ref[:, third:] = keep_kv[at] + come_kv[at]


def sum_kernel(norm, *refs):
    parts, out_ref = [ref[...] for ref in refs[:-1]], refs[-1]
    while len(parts) > 1:
        parts = [parts[i] + parts[i + 1] for i in range(0, len(parts), 2)]
    out_ref[...] = parts[0] * norm


def collect_kernel(layout, *refs):
    parts, out_ref = refs[:-1], refs[-1]
    quarter = Place(layout).group // 2
    for m, part in enumerate(parts):
        out_ref[quarter ^ m] = part[...]


def finish_kernel(taps, layout, own_ref, come_ref, dw_ref, pw_ref, whole_ref):
    odd = Place(layout).group % 2 == 1
    quarters, rows = own_ref.shape[:2]
    for part in range(quarters):
        own, come = own_ref[part], come_ref[part]
        whole_ref[2 * part * rows : (2 * part + 1) * rows] = jnp.where(odd, come, own)
        whole_ref[(2 * part + 1) * rows : (2 * part + 2) * rows] = jnp.where(odd, own, come)
    dw_ref[...] = whole_ref[:taps]
    pw_ref[...] = whole_ref[whole_ref.shape[0] - pw_ref.shape[0] :]


def copy_kernel(*refs):
    half = len(refs) // 2
    for in_ref, out_ref in zip(refs[:half], refs[half:]):
        out_ref[...] = in_ref[...]


def backward_kernel(routes, first, *refs):
    layout, gmix_ref = refs[:2]
    arrived = refs[2 : 2 + routes.arriving]
    dw_ref, grad0_ref, out_ref, pad_ref, done_ref, sems = refs[2 + routes.arriving :]
    place = Place(layout)
    deltas = routes.sources(place)
    tall, broad = out_ref.shape[2:4]
    count, _, third = gmix_ref.shape
    per, size = third // LANES, REACH * broad

    def one_block(block, carry):
        at, member, within = lanes_at(first * per + block), block // per, lanes_at(block % per)
        begin = pl.multiple_of((first + member) * size, size)
        edges = [ref[pl.ds(begin, size), within] for ref in arrived]
        field = gmix_ref[member, :, within].reshape(tall, broad, LANES)
        fill_padded(pad_ref, field, edges, deltas, place)
        grad0 = grad0_ref.at[member, :, within]

        def emit(y, sub, total):
            total = total + grad0[y * broad : (y + 1) * broad, sub]
            done_ref[block, y, :, sub] = jnp.where(place.live, total, 0.0).astype(BF16)

        convolve(pad_ref, dw_ref.at[:, at], emit, True)
        write(block).start()
        return carry

    def write(block):
        target = out_ref.at[0, 0, :, :, lanes_at(first * per + block)]
        return pltpu.make_async_copy(done_ref.at[block], target, sems.at[block])

    lax.fori_loop(0, count * per, one_block, 0)
    for block in range(count * per):
        write(block).wait()


def in_hbm(x):
    return pltpu.with_memory_space_constraint(x, pltpu.HBM)


def call(cost, kernel, out_shape, args, scratch=(), after=(), in_place=0, out_space=pltpu.VMEM, onto=()):
    inputs, extra = len(args), len(onto) + len(after)

    def body(*refs):
        kernel(*refs[:inputs], *refs[inputs + extra :])

    spaces = [pltpu.SMEM if x.dtype == jnp.int32 else pltpu.VMEM for x in args]
    spaces[inputs - in_place :] = [pl.ANY] * in_place
    spaces += [out_space] * len(onto) + [pl.ANY] * len(after)
    return pl.pallas_call(
        body,
        in_specs=[pl.BlockSpec(memory_space=space) for space in spaces],
        out_specs=jax.tree.map(lambda _: pl.BlockSpec(memory_space=out_space), out_shape),
        out_shape=out_shape,
        scratch_shapes=list(scratch),
        input_output_aliases={inputs: 0} if onto else {},
        compiler_params=PARAMS,
        cost_estimate=pl.CostEstimate(
            flops=0, bytes_accessed=int(cost * BYTES_PER_US), transcendentals=0
        ),
    )(*args, *onto, *after)


def local(
    qkv, cotangent, dw_weight, pw_weight, tile_image, tile_row, tile_col, image_height, image_width
):
    tall, broad, channels = qkv.shape[2:]
    positions = tall * broad
    head_dim = pw_weight.shape[0]
    taps = dw_weight.shape[0]
    third = channels // 3
    tiles, groups = lax.axis_size("tile"), lax.axis_size("img")
    routes = Routes(tiles)
    edge = REACH * broad
    packed = 2 * (head_dim + 8)
    padded_shape = (tall + 2 * REACH, broad + EDGE)
    spot = lax.axis_index("img").astype(jnp.int32)
    scalars = (tile_image, tile_row, tile_col, spot, image_height, image_width)
    layout = jnp.concatenate([x.reshape(-1) for x in scalars])
    part = functools.partial

    def wide(*dims):
        return jax.ShapeDtypeStruct(dims, F32)

    def narrow(*dims):
        return jax.ShapeDtypeStruct(dims, BF16)

    low, high = edge, edge + packed

    sent_kv = pl.pallas_call(
        part(outgoing_kernel, routes),
        grid=(1,),
        in_specs=[pl.BlockSpec(memory_space=pltpu.SMEM)]
        + [pl.BlockSpec((1, 1, tall, broad, third), lambda j, m=m: (0, 0, 0, 0, m)) for m in (1, 2)],
        out_specs=[pl.BlockSpec((2, size, third), lambda j: (0, 0, 0)) for size in routes.direct_rows(edge)],
        out_shape=[narrow(2, size, third) for size in routes.direct_rows(edge)],
        compiler_params=PARAMS,
    )(layout, in_hbm(qkv), in_hbm(qkv))
    halo_kv = routes.move_direct(sent_kv)
    *sent_q, dw_weight, pw_weight = call(
        1.0,
        part(source_state_kernel, routes, head_dim),
        [narrow(high, third)] * routes.sent + [wide(taps, channels), wide(head_dim, channels)],
        (layout, qkv, in_hbm(dw_weight), in_hbm(pw_weight)),
        [pltpu.SemaphoreType.DMA((2,))],
        in_place=2,
    )
    sent_q = call(0.3, copy_kernel, [narrow(high, third)] * routes.sent, sent_q, after=tuple(halo_kv))

    def forward(first, count, halo, direct):
        return call(
            1.5 * count * third / LANES,
            part(forward_kernel, routes, first, count, head_dim, direct),
            [wide(count, positions, third)] * 2
            + [wide(count, *padded_shape, third)]
            + [narrow(packed, third)] * (first > 0),
            (layout, qkv, *halo, dw_weight, pw_weight),
        )

    mixed_kv, merged_kv, padded_kv, state = forward(1, 2, halo_kv, True)

    def copied(far, tokens):
        return call(0.3, copy_kernel, jax.ShapeDtypeStruct(far.shape, far.dtype), (far,), after=tokens)

    halo_q = routes.move(sent_q, hand_on=lambda near, far: copied(far, (state,)))
    state_from = exchange(state, "tile")
    others = len(state_from)
    mixed_q, merged_q, padded_q = forward(0, 1, halo_q, False)

    gstate, gmix_q, gpw_q = call(
        3.0,
        part(merged_query_kernel, others, head_dim),
        [narrow(packed, third), wide(1, positions, third), wide(1, head_dim, third)],
        (layout, state, *state_from, merged_q, mixed_q, cotangent, pw_weight),
    )
    gstate_from = exchange(gstate, "tile")

    source_from = halo_q if routes.relayed else exchange(sent_q[0][low:], "tile")
    from_offset = low if routes.relayed else 0
    grad0_q, gstate0 = call(
        2.5,
        part(source_query_kernel, others, low, from_offset, head_dim),
        [wide(1, positions, third), narrow(packed, third)],
        (layout, sent_q[0], *source_from, qkv, cotangent),
        after=(gstate,),
    )

    gap = -(-taps // 8) * 8
    rows = gap + head_dim
    halves = groups == 8 and rows % groups == 0
    eighth = rows // groups

    def weights(count, padded, gmix, gpw):
        return call(
            1.0 * count * third / LANES,
            part(weight_kernel, halves),
            [wide(4, eighth, count * third)] * 2 if halves else [wide(rows, count * third)],
            (layout, padded, gmix, gpw),
            [pltpu.VMEM((rows, 128), F32)],
        )

    weights_q = weights(1, padded_q, gmix_q, gpw_q)
    total_rows = 3 * edge + packed
    gmix_kv, gpw_kv, *sent_back = call(
        3.0,
        part(merged_value_kernel, others, routes, tall, head_dim),
        [wide(2, positions, third), wide(2, head_dim, third)] + [narrow(total_rows, third)] * routes.sent,
        (layout, gstate, *gstate_from, merged_kv, mixed_kv, pw_weight, gmix_q, gstate0),
        after=(weights_q[0],),
    )
    weights_kv = weights(2, padded_kv, gmix_kv, gpw_kv)

    norm = 1.0 / math.sqrt(positions * tiles * groups)
    ready = weights_kv
    if halves:
        come_q = exchange(weights_q[0], "img", (1,))[0]
        come_kv = exchange(weights_kv[0], "img", (1,))[0]
        share_shape = wide(eighth, channels)
        shares = call(
            0.5, scatter_kernel, [share_shape] * 4, (layout, weights_q[1], come_q, weights_kv[1], come_kv)
        )
        moved = [
            lax.ppermute(share, "img", [(s, s ^ (2 * m)) for s in range(groups)])
            for m, share in enumerate(shares[1:], 1)
        ]
        ready = shares[:1]

    halo_back = routes.move(sent_back, hand_on=lambda near, far: copied(far, (near, *ready)))

    back_from = halo_back if routes.relayed else exchange(sent_back[0][3 * edge :], "tile")
    back_offset = 3 * edge if routes.relayed else 0
    grad0_kv = call(
        1.5,
        part(source_value_kernel, others, 3 * edge, back_offset, head_dim),
        wide(2, positions, third),
        (layout, sent_back[0], *back_from, qkv),
    )

    def backward(first, gmix, grad0, onto=()):
        blocks = gmix.shape[0] * third // LANES
        return call(
            1.0 * blocks,
            part(backward_kernel, routes, first),
            pltpu.HBM((1, 1, tall, broad, channels), BF16),
            (layout, gmix, *halo_back, dw_weight, grad0),
            [pltpu.VMEM((*padded_shape, LANES), F32)]
            + [pltpu.VMEM((blocks, tall, broad, LANES), BF16), pltpu.SemaphoreType.DMA((blocks,))],
            out_space=pltpu.HBM,
            onto=onto,
        )

    grad_query = in_hbm(backward(0, gmix_q, grad0_q))
    grad_source = backward(1, gmix_kv, grad0_kv, (grad_query,))

    if halves:
        total = call(0.3, part(sum_kernel, 1.0), share_shape, [shares[0]] + moved)
        total = call(
            0.3, part(sum_kernel, norm), share_shape, [total] + exchange(total, "tile"), after=(grad_query, grad0_kv)
        )
        quarters = call(
            0.5,
            collect_kernel,
            wide(4, eighth, channels),
            (layout, total, *exchange(total, "img", (2, 4, 6))),
            after=(in_hbm(grad_source),),
        )
        grad_dw, grad_pw = call(
            0.8,
            part(finish_kernel, taps),
            [wide(taps, channels), wide(head_dim, channels)],
            (layout, quarters, exchange(quarters, "img", (1,))[0]),
            [pltpu.VMEM((rows, channels), F32)],
        )
    else:
        whole = jnp.concatenate([weights_q[0], weights_kv[0]], axis=1)
        whole = lax.psum(whole, ("tile", "img")) * norm
        grad_dw, grad_pw = whole[:taps], whole[gap:]
    return grad_source, grad_dw, grad_pw


def solution(mesh):
    placed = (
        P("img", "tile", None, None, None),
        P("img", "tile", None, None, None),
        P(),
        P(),
        P("img", "tile"),
        P("img", "tile"),
        P("img", "tile"),
        P("img", None),
        P("img", None),
    )
    return jax.shard_map(
        local,
        mesh=mesh,
        in_specs=placed,
        out_specs=(P("img", "tile", None, None, None), P(), P()),
        check_vma=False,
    )
```

```python
import functools
import math

import jax
import jax.numpy as jnp
from jax import lax
from jax.experimental import pallas as pl
from jax.experimental.pallas import tpu as pltpu
from jax.sharding import PartitionSpec as P

EPSILON = 1e-06
LANES = 256
REACH = 2
EDGE = 8
BYTES_PER_US = 3_690_000
BF16 = jnp.bfloat16
F32 = jnp.float32
PARAMS = pltpu.CompilerParams(vmem_limit_bytes=16 * 1024 * 1024)


class Place:
    def __init__(self, info_ref):
        slots = (info_ref.shape[0] - 4) // 2
        slot = info_ref[0]
        tall = wide = start = jnp.int32(0)
        for s in range(slots):
            tall_s, wide_s = info_ref[4 + s], info_ref[4 + slots + s]
            tall = jnp.where(slot == s, tall_s, tall)
            wide = jnp.where(slot == s, wide_s, wide)
            start = start + jnp.where(s < slot, tall_s * wide_s, 0)
        self.live = slot < slots
        self.tall, self.wide = tall, wide
        self.row, self.col = info_ref[1], info_ref[2]
        self.group = info_ref[3]
        self.within = self.row * wide + self.col
        self.index = start + self.within
        self.above = self.live & (self.row > 0)
        self.below = self.live & (self.row < tall - 1)

    def same_image(self, delta):
        other = self.within + delta
        return self.live & (other >= 0) & (other < self.tall * self.wide)


class Routes:
    def __init__(self, count):
        self.count = count
        self.relayed = count == 4
        self.shifts = [k for k in (1, -1, 2, -2, 3, -3) if abs(k) < count]
        self.sent = 2 if self.relayed else len(self.shifts)
        self.arriving = 3 if self.relayed else len(self.shifts)

    def targets(self, place, direct=False):
        if not self.relayed:
            return [jnp.int32(k) for k in self.shifts]
        near, far, last = ((place.index ^ m) - place.index for m in (1, 2, 3))
        if direct:
            return [near, far, last, last]
        return [near, jnp.where(place.same_image(far), far, last)]

    def sources(self, place, direct=False):
        if not self.relayed:
            return [jnp.int32(-k) for k in self.shifts]
        near, far, last = ((place.index ^ m) - place.index for m in (1, 2, 3))
        if direct:
            outer = jnp.abs(last) == 3
            return [near, far, jnp.where(outer, 0, last), jnp.where(outer, last, 0)]
        return [near, far, last]

    def direct_rows(self, edge):
        return [edge, edge, edge, REACH * EDGE] if self.relayed else [edge] * self.sent

    def move(self, sent, hand_on=lambda near, far: far):
        count = self.count
        if not self.relayed:
            return [
                lax.ppermute(part, "tile", [(s, s + k) for s in range(max(0, -k), min(count, count - k))])
                for part, k in zip(sent, self.shifts)
            ]
        near, far = (
            lax.ppermute(part, "tile", [(s, s ^ m) for s in range(count)]) for part, m in zip(sent, (1, 2))
        )
        return [near, far, lax.ppermute(hand_on(near, far), "tile", [(s, s ^ 1) for s in range(count)])]

    def move_direct(self, sent):
        if not self.relayed:
            return self.move(sent)
        targets = ((1, 0, 3, 2), (2, 3, 0, 1), (0, 2, 1, 3), (3, 1, 2, 0))
        return [lax.ppermute(part, "tile", list(enumerate(to))) for part, to in zip(sent, targets)]


def exchange(value, axis, masks=None):
    count = lax.axis_size(axis)
    masks = range(1, count) if masks is None else masks
    return [lax.ppermute(value, axis, [(s, s ^ m) for s in range(count)]) for m in masks]


def split(x):
    high = x.astype(BF16)
    return high, (x - high.astype(F32)).astype(BF16)


def contract(a, b, dims):
    return lax.dot_general(a, b, (dims, ((), ())), preferred_element_type=F32)


NN = ((1,), (0,))
NT = ((1,), (1,))
TN = ((0,), (0,))


def dot(a, b, dims):
    total = contract(a[0], b[0], dims)
    if b[1] is not None:
        total = total + contract(a[0], b[1], dims)
    if a[1] is not None:
        total = total + contract(a[1], b[0], dims)
    return total


def exact(x):
    return x.astype(BF16), None


def same_head(head_dim):
    rows = lax.broadcasted_iota(jnp.int32, (LANES, LANES), 0) // head_dim
    cols = lax.broadcasted_iota(jnp.int32, (LANES, LANES), 1) // head_dim
    return rows == cols


def spread(compact, mask):
    tall = jnp.concatenate([compact] * (LANES // compact.shape[0]), axis=0)
    return jnp.where(mask, tall, 0.0)


def gather_blocks(full, mask, head_dim):
    kept = jnp.where(mask, full, 0.0)
    return jnp.sum(kept.reshape(LANES // head_dim, head_dim, LANES), axis=0)


def payload(field, place, delta):
    tall, broad, lanes = field.shape
    size = REACH * broad
    top = field[:REACH].reshape(size, lanes)
    bottom = field[tall - REACH :].reshape(size, lanes)
    left = field[:, :EDGE].reshape(size, lanes)
    right = field[:, broad - EDGE :].reshape(size, lanes)
    rows = jnp.where(delta > 0, bottom, top)
    cols = jnp.where(place.col == 0, right, left)
    beside = (place.wide == 2) & (delta == jnp.where(place.col == 0, 1, -1))
    return jnp.where(beside, cols, rows)


def lanes_at(block):
    start = block * LANES
    return pl.ds(start if isinstance(start, int) else pl.multiple_of(start, LANES), LANES)


def pack_state(state, total):
    rows = jnp.concatenate([state, total, jnp.zeros((7, state.shape[1]), F32)], axis=0)
    high = rows.astype(BF16).astype(F32)
    return jnp.concatenate([high, rows - high], axis=0).astype(BF16)


def unpack_state(ref, offset):
    rows = ref[offset:].astype(F32)
    half = rows.shape[0] // 2
    return rows[:half] + rows[half:]


def total_state(own_ref, others, place, offset, others_offset):
    total = unpack_state(own_ref, offset)
    for m, other in enumerate(others, 1):
        delta = (place.index ^ m) - place.index
        total = total + jnp.where(place.same_image(delta), unpack_state(other, others_offset), 0.0)
    return total


def corner_payload(field, delta):
    tall, broad, lanes = field.shape
    corner = jnp.where(delta > 0, field[tall - REACH :, broad - EDGE :], field[:REACH, :EDGE])
    return corner.reshape(REACH * EDGE, lanes)


def fill_padded(pad_ref, field, arrived, deltas, place):
    tall, broad, lanes = field.shape
    two = place.live & (place.wide == 2)
    one = place.live & (place.wide == 1)
    first, second = two & (place.col == 0), two & (place.col == 1)

    def choose(condition, value, other):
        return jnp.where(condition, value, other)

    above = below = jnp.zeros((REACH, broad, lanes), F32)
    above_side = below_side = jnp.zeros((REACH, EDGE, lanes), F32)
    side = jnp.zeros((tall, EDGE, lanes), F32)
    for edges, delta in zip(arrived, deltas):
        edges = edges.astype(F32)
        if edges.shape[0] == REACH * EDGE:
            corner = edges.reshape(REACH, EDGE, lanes)
            above_side = choose(second & (delta == -3), corner, above_side)
            below_side = choose(first & (delta == 3), corner, below_side)
            continue
        rows, cols = edges.reshape(REACH, broad, lanes), edges.reshape(tall, EDGE, lanes)
        begin, end = rows[:, :EDGE], rows[:, broad - EDGE :]
        above = choose((one & (delta == -1)) | (two & (delta == -2)), rows, above)
        below = choose((one & (delta == 1)) | (two & (delta == 2)), rows, below)
        side = choose((first & (delta == 1)) | (second & (delta == -1)), cols, side)
        above_side = choose(first & (delta == -1), begin, choose(second & (delta == -3), end, above_side))
        below_side = choose(second & (delta == 1), end, choose(first & (delta == 3), begin, below_side))
    column = lax.broadcasted_iota(jnp.int32, (1, EDGE, lanes), 1)
    reached = (first & (column < REACH)) | (second & (column >= EDGE - REACH))
    upper, lower = slice(0, REACH), slice(REACH + tall, 2 * REACH + tall)
    pad_ref[upper, :broad] = choose(place.above, above, 0.0)
    pad_ref[lower, :broad] = choose(place.below, below, 0.0)
    pad_ref[upper, broad:] = choose(reached & place.above, above_side, 0.0)
    pad_ref[lower, broad:] = choose(reached & place.below, below_side, 0.0)
    pad_ref[REACH : REACH + tall, broad:] = choose(reached, side, 0.0)
    pad_ref[REACH : REACH + tall, :broad] = field


def convolve(pad_ref, kernel_ref, emit, flipped):
    taps = 2 * REACH + 1
    tall, broad, lanes = pad_ref.shape[0] - 2 * REACH, pad_ref.shape[1] - EDGE, pad_ref.shape[2]
    ring = broad + EDGE
    sub = 128
    for start in range(0, lanes, sub):
        at = slice(start, start + sub)
        for y in range(tall):
            rows = [pad_ref[y + a, :, at] for a in range(taps)]
            total = None
            for b in range(taps):
                part = None
                for a in range(taps):
                    tap = taps * a + b
                    if flipped:
                        tap = taps * taps - 1 - tap
                    row = rows[a][:broad] if b == REACH else rows[a]
                    term = row * kernel_ref[tap : tap + 1, at]
                    part = term if part is None else part + term
                if b != REACH:
                    part = pltpu.roll(part, (REACH - b) % ring, 0)
                total = part[:broad] if total is None else total + part[:broad]
            emit(y, at, total)


def read_field(ref, place, at=slice(None)):
    return jnp.where(place.live, ref[0, 0, :, :, at].astype(F32), 0.0)


def outgoing_kernel(routes, layout, key_ref, value_ref, *outs):
    place = Place(layout)
    for member, field_ref in enumerate((key_ref, value_ref)):
        field = field_ref[0, 0].astype(F32)
        for delta, out_ref in zip(routes.targets(place, True), outs):
            full = out_ref.shape[1] == REACH * field.shape[1]
            sent = payload(field, place, delta) if full else corner_payload(field, delta)
            out_ref[member] = sent.astype(BF16)


def thirds(ref, at):
    third = ref.shape[4] // 3
    return [slice(member * third + at.start, member * third + at.stop) for member in range(3)]


def source_state_kernel(routes, head_dim, layout, field_ref, *refs):
    weight_refs, outs, held, sems = refs[:2], refs[2:-3], refs[-3:-1], refs[-1]
    loads = [pltpu.make_async_copy(a, b, sems.at[i]) for i, (a, b) in enumerate(zip(weight_refs, held))]
    for load in loads:
        load.start()
    place = Place(layout)
    mask = same_head(head_dim)
    size = REACH * field_ref.shape[3]
    for at in parts_of(outs[0].shape[1]):
        query_at, key_at, value_at = thirds(field_ref, at)
        field = field_ref[0, 0, :, :, query_at].astype(F32)
        keys = jnp.maximum(read_field(field_ref, place, key_at).reshape(-1, LANES), 0.0)
        values = read_field(field_ref, place, value_at).reshape(-1, LANES)
        state = gather_blocks(contract(keys.astype(BF16), values.astype(BF16), TN), mask, head_dim)
        packed = pack_state(state, jnp.sum(keys, axis=0, keepdims=True))
        for delta, out_ref in zip(routes.targets(place), outs):
            out_ref[:size, at] = payload(field, place, delta).astype(BF16)
            out_ref[size:, at] = packed
    for load in loads:
        load.wait()


def forward_kernel(routes, first, count, head_dim, direct, *refs):
    layout, field_ref = refs[:2]
    place = Place(layout)
    deltas = routes.sources(place, direct)
    arrived, refs = refs[2 : 2 + len(deltas)], refs[2 + len(deltas) :]
    dw_ref, pw_ref, mixed_ref, merged_ref, padded_ref = refs[:5]
    mask = same_head(head_dim)
    per = mixed_ref.shape[2] // LANES
    size = REACH * field_ref.shape[3]

    def one_block(block, carry):
        at, member, within = lanes_at(first * per + block), block // per, lanes_at(block % per)
        field = read_field(field_ref, place, at)
        if len(arrived[0].shape) == 3:
            edges = [ref[member, :, within] for ref in arrived]
        else:
            edges = [ref[:size, within] for ref in arrived]
        padded = padded_ref.at[member, :, :, within]
        fill_padded(padded, field, edges, deltas, place)
        target = mixed_ref.at[member, :, within]
        broad = field.shape[1]

        def emit(y, sub, total):
            target[y * broad : (y + 1) * broad, sub] = total

        convolve(padded, dw_ref.at[:, at], emit, False)
        mixed = target[...]
        merged_ref[member, :, within] = dot(split(mixed), split(spread(pw_ref[:, at], mask)), NN)
        return carry

    lax.fori_loop(0, count * per, one_block, 0, unroll=2)
    if first == 0:
        return
    state_ref = refs[5]
    for at in parts_of(state_ref.shape[1]):
        keys = jnp.maximum(merged_ref[0, :, at], 0.0)
        state = gather_blocks(dot(split(keys), split(merged_ref[1, :, at]), TN), mask, head_dim)
        state_ref[:, at] = pack_state(state, jnp.sum(keys, axis=0, keepdims=True))


def parts_of(lanes):
    return [slice(start, start + LANES) for start in range(0, lanes, LANES)]


def query_gradients(raw, exactly, total, cot, head_dim, mask):
    ones = (mask.astype(BF16), None)
    query = jnp.maximum(raw, 0.0)
    pair = exact(query) if exactly else split(query)
    state = split(spread(total[:head_dim], mask))
    key_sum = total[head_dim : head_dim + 1]
    over = 1.0 / (dot(split(query * key_sum), ones, NN) + EPSILON)
    result = dot(pair, state, NN) * over
    grad_num = cot * over
    grad_den = -dot(split(cot * result), ones, NN) * over
    num_pair = split(grad_num)
    grad = jnp.where(raw > 0, dot(num_pair, state, NT) + grad_den * key_sum, 0.0)
    gstate = gather_blocks(dot(pair, num_pair, TN), mask, head_dim)
    return grad, pack_state(gstate, jnp.sum(query * grad_den, axis=0, keepdims=True))


def source_query_kernel(others, offset, others_offset, head_dim, *refs):
    layout, own_ref, received = refs[0], refs[1], refs[2 : 2 + others]
    source_ref, cot_ref, grad_ref, gstate_ref = refs[2 + others :]
    place = Place(layout)
    mask = same_head(head_dim)
    total = total_state(own_ref, received, place, offset, others_offset)
    for at in parts_of(gstate_ref.shape[1]):
        raw = read_field(source_ref, place, at).reshape(-1, LANES)
        cot = cot_ref[0, 0, :, :, at].astype(F32).reshape(raw.shape)
        grad_ref[0, :, at], gstate_ref[:, at] = query_gradients(raw, True, total[:, at], cot, head_dim, mask)


def merged_query_kernel(others, head_dim, *refs):
    layout, own_ref, received = refs[0], refs[1], refs[2 : 2 + others]
    merged_ref, mixed_ref, cot_ref, pw_ref, gstate_ref, gmix_ref, gpw_ref = refs[2 + others :]
    place = Place(layout)
    mask = same_head(head_dim)
    total = total_state(own_ref, received, place, 0, 0)
    third = gstate_ref.shape[1]
    for at in parts_of(third):
        raw = merged_ref[0, :, at]
        cot = cot_ref[0, 0, :, :, third + at.start : third + at.stop].astype(F32).reshape(raw.shape)
        grad, gstate_ref[:, at] = query_gradients(raw, False, total[:, at], cot, head_dim, mask)
        pair = split(grad)
        gmix_ref[0, :, at] = dot(pair, split(spread(pw_ref[:, at], mask)), NT)
        gpw_ref[0, :, at] = gather_blocks(dot(split(mixed_ref[0, :, at]), pair, TN), mask, head_dim)


def key_gradients(raw, key_pair, value_pair, total, head_dim, mask):
    gstate = split(spread(total[:head_dim], mask))
    gsum = total[head_dim : head_dim + 1]
    grad_keys = jnp.where(raw > 0, dot(value_pair, gstate, NT) + gsum, 0.0)
    return grad_keys, dot(key_pair, gstate, NN)


def source_value_kernel(others, offset, others_offset, head_dim, *refs):
    layout, own_ref, received = refs[0], refs[1], refs[2 : 2 + others]
    field_ref, grad_ref = refs[2 + others :]
    place = Place(layout)
    mask = same_head(head_dim)
    total = total_state(own_ref, received, place, offset, others_offset)
    for at in parts_of(grad_ref.shape[2]):
        _, key_at, value_at = thirds(field_ref, at)
        raw = read_field(field_ref, place, key_at).reshape(-1, LANES)
        values = read_field(field_ref, place, value_at).reshape(-1, LANES)
        grad_ref[0, :, at], grad_ref[1, :, at] = key_gradients(
            raw, exact(jnp.maximum(raw, 0.0)), exact(values), total[:, at], head_dim, mask
        )


def merged_value_kernel(others, routes, tall, head_dim, *refs):
    layout, own_ref, received = refs[0], refs[1], refs[2 : 2 + others]
    merged_ref, mixed_ref, pw_ref, qgmix_ref, packed_ref, gmix_ref, gpw_ref = refs[2 + others : 9 + others]
    outs = refs[9 + others :]
    place = Place(layout)
    mask = same_head(head_dim)
    total = total_state(own_ref, received, place, 0, 0)
    size = (outs[0].shape[0] - packed_ref.shape[0]) // 3

    def send(member, at, gmix):
        field = gmix.reshape(tall, -1, LANES)
        for delta, out_ref in zip(routes.targets(place), outs):
            out_ref[member * size : (member + 1) * size, at] = payload(field, place, delta).astype(BF16)

    for at in parts_of(gmix_ref.shape[2]):
        for out_ref in outs:
            out_ref[3 * size :, at] = packed_ref[:, at]
        send(0, at, qgmix_ref[0, :, at])
        raw = merged_ref[0, :, at]
        pairs = split(jnp.maximum(raw, 0.0)), split(merged_ref[1, :, at])
        grads = key_gradients(raw, *pairs, total[:, at], head_dim, mask)
        third = gmix_ref.shape[2]
        for member, grad in enumerate(grads):
            pair = split(grad)
            begin = (1 + member) * third + at.start
            gmix = dot(pair, split(spread(pw_ref[:, begin : begin + LANES], mask)), NT)
            gmix_ref[member, :, at] = gmix
            gpw_ref[member, :, at] = gather_blocks(dot(split(mixed_ref[member, :, at]), pair, TN), mask, head_dim)
            send(1 + member, at, gmix)


def weight_kernel(halves, layout, padded_ref, gmix_ref, gpw_ref, *refs):
    outs, sum_ref = refs[:-1], refs[-1]
    ring, sub = padded_ref.shape[2], 128
    tall, broad = padded_ref.shape[1] - 2 * REACH, ring - EDGE
    taps = 2 * REACH + 1
    count, head_dim, third = gpw_ref.shape
    start = sum_ref.shape[0] - head_dim
    odd = Place(layout).group % 2 == 1
    each = third // sub

    def one_block(block, carry):
        member = block // each
        at = pl.ds(pl.multiple_of(block % each * sub, sub), sub)
        out_at = pl.ds(pl.multiple_of(block * sub, sub), sub)

        def one_row(y, totals):
            grad = gmix_ref[member, pl.ds(pl.multiple_of(y * broad, broad), broad), at]
            longer = jnp.concatenate([grad, jnp.zeros((EDGE, sub), F32)], axis=0)
            moved = [grad if b == REACH else pltpu.roll(longer, (b - REACH) % ring, 0) for b in range(taps)]
            new = list(totals)
            for a in range(taps):
                row = padded_ref[member, y + a, :, at]
                for b in range(taps):
                    term = row[: moved[b].shape[0]] * moved[b]
                    term = term.reshape(term.shape[0] // 8, 8, sub)
                    new[taps * a + b] = new[taps * a + b] + jnp.sum(term, axis=0)
            return tuple(new)

        zero = jnp.zeros((8, sub), F32)
        totals = lax.fori_loop(0, tall, one_row, (zero,) * (taps * taps), unroll=4)
        for tap in range(taps * taps):
            sum_ref[tap : tap + 1] = jnp.sum(totals[tap], axis=0, keepdims=True)
        sum_ref[taps * taps : start] = jnp.zeros((start - taps * taps, sub), F32)
        sum_ref[start:] = gpw_ref[member, :, at]
        if not halves:
            outs[0][:, out_at] = sum_ref[...]
            return carry
        rows = outs[0].shape[1]
        for part in range(outs[0].shape[0]):
            even_rows = sum_ref[2 * part * rows : (2 * part + 1) * rows]
            odd_rows = sum_ref[(2 * part + 1) * rows : (2 * part + 2) * rows]
            outs[0][part, :, out_at] = jnp.where(odd, even_rows, odd_rows)
            outs[1][part, :, out_at] = jnp.where(odd, odd_rows, even_rows)
        return carry

    lax.fori_loop(0, count * each, one_block, 0)


def scatter_kernel(layout, keep_q, come_q, keep_kv, come_kv, own_ref, *outs):
    quarter = Place(layout).group // 2
    third = keep_q.shape[2]
    for m, out_ref in enumerate((own_ref,) + outs):
        at = quarter ^ m
        out_ref[:, :third] = keep_q[at] + come_q[at]
        out_ref[:, third:] = keep_kv[at] + come_kv[at]


def sum_kernel(norm, *refs):
    parts, out_ref = [ref[...] for ref in refs[:-1]], refs[-1]
    while len(parts) > 1:
        parts = [parts[i] + parts[i + 1] for i in range(0, len(parts), 2)]
    out_ref[...] = parts[0] * norm


def collect_kernel(layout, *refs):
    parts, out_ref = refs[:-1], refs[-1]
    quarter = Place(layout).group // 2
    for m, part in enumerate(parts):
        out_ref[quarter ^ m] = part[...]


def finish_kernel(taps, layout, own_ref, come_ref, dw_ref, pw_ref, whole_ref):
    odd = Place(layout).group % 2 == 1
    quarters, rows = own_ref.shape[:2]
    for part in range(quarters):
        own, come = own_ref[part], come_ref[part]
        whole_ref[2 * part * rows : (2 * part + 1) * rows] = jnp.where(odd, come, own)
        whole_ref[(2 * part + 1) * rows : (2 * part + 2) * rows] = jnp.where(odd, own, come)
    dw_ref[...] = whole_ref[:taps]
    pw_ref[...] = whole_ref[whole_ref.shape[0] - pw_ref.shape[0] :]


def copy_kernel(*refs):
    half = len(refs) // 2
    for in_ref, out_ref in zip(refs[:half], refs[half:]):
        out_ref[...] = in_ref[...]


def backward_kernel(routes, first, *refs):
    layout, gmix_ref = refs[:2]
    arrived = refs[2 : 2 + routes.arriving]
    dw_ref, grad0_ref, out_ref, pad_ref, done_ref, sems = refs[2 + routes.arriving :]
    place = Place(layout)
    deltas = routes.sources(place)
    tall, broad = out_ref.shape[2:4]
    count, _, third = gmix_ref.shape
    per, size = third // LANES, REACH * broad

    def one_block(block, carry):
        at, member, within = lanes_at(first * per + block), block // per, lanes_at(block % per)
        begin = pl.multiple_of((first + member) * size, size)
        edges = [ref[pl.ds(begin, size), within] for ref in arrived]
        field = gmix_ref[member, :, within].reshape(tall, broad, LANES)
        fill_padded(pad_ref, field, edges, deltas, place)
        grad0 = grad0_ref.at[member, :, within]

        def emit(y, sub, total):
            total = total + grad0[y * broad : (y + 1) * broad, sub]
            done_ref[block, y, :, sub] = jnp.where(place.live, total, 0.0).astype(BF16)

        convolve(pad_ref, dw_ref.at[:, at], emit, True)
        write(block).start()
        return carry

    def write(block):
        target = out_ref.at[0, 0, :, :, lanes_at(first * per + block)]
        return pltpu.make_async_copy(done_ref.at[block], target, sems.at[block])

    lax.fori_loop(0, count * per, one_block, 0, unroll=2)
    for block in range(count * per):
        write(block).wait()


def in_hbm(x):
    return pltpu.with_memory_space_constraint(x, pltpu.HBM)


def call(cost, kernel, out_shape, args, scratch=(), after=(), in_place=0, out_space=pltpu.VMEM, onto=()):
    inputs, extra = len(args), len(onto) + len(after)

    def body(*refs):
        kernel(*refs[:inputs], *refs[inputs + extra :])

    spaces = [pltpu.SMEM if x.dtype == jnp.int32 else pltpu.VMEM for x in args]
    spaces[inputs - in_place :] = [pl.ANY] * in_place
    spaces += [out_space] * len(onto) + [pl.ANY] * len(after)
    return pl.pallas_call(
        body,
        in_specs=[pl.BlockSpec(memory_space=space) for space in spaces],
        out_specs=jax.tree.map(lambda _: pl.BlockSpec(memory_space=out_space), out_shape),
        out_shape=out_shape,
        scratch_shapes=list(scratch),
        input_output_aliases={inputs: 0} if onto else {},
        compiler_params=PARAMS,
        cost_estimate=pl.CostEstimate(
            flops=0, bytes_accessed=int(cost * BYTES_PER_US), transcendentals=0
        ),
    )(*args, *onto, *after)


def local(
    qkv, cotangent, dw_weight, pw_weight, tile_image, tile_row, tile_col, image_height, image_width
):
    tall, broad, channels = qkv.shape[2:]
    positions = tall * broad
    head_dim = pw_weight.shape[0]
    taps = dw_weight.shape[0]
    third = channels // 3
    tiles, groups = lax.axis_size("tile"), lax.axis_size("img")
    routes = Routes(tiles)
    edge = REACH * broad
    packed = 2 * (head_dim + 8)
    padded_shape = (tall + 2 * REACH, broad + EDGE)
    spot = lax.axis_index("img").astype(jnp.int32)
    scalars = (tile_image, tile_row, tile_col, spot, image_height, image_width)
    layout = jnp.concatenate([x.reshape(-1) for x in scalars])
    part = functools.partial

    def wide(*dims):
        return jax.ShapeDtypeStruct(dims, F32)

    def narrow(*dims):
        return jax.ShapeDtypeStruct(dims, BF16)

    low, high = edge, edge + packed

    sent_kv = pl.pallas_call(
        part(outgoing_kernel, routes),
        grid=(1,),
        in_specs=[pl.BlockSpec(memory_space=pltpu.SMEM)]
        + [pl.BlockSpec((1, 1, tall, broad, third), lambda j, m=m: (0, 0, 0, 0, m)) for m in (1, 2)],
        out_specs=[pl.BlockSpec((2, size, third), lambda j: (0, 0, 0)) for size in routes.direct_rows(edge)],
        out_shape=[narrow(2, size, third) for size in routes.direct_rows(edge)],
        compiler_params=PARAMS,
    )(layout, in_hbm(qkv), in_hbm(qkv))
    halo_kv = routes.move_direct(sent_kv)
    *sent_q, dw_weight, pw_weight = call(
        1.0,
        part(source_state_kernel, routes, head_dim),
        [narrow(high, third)] * routes.sent + [wide(taps, channels), wide(head_dim, channels)],
        (layout, qkv, in_hbm(dw_weight), in_hbm(pw_weight)),
        [pltpu.SemaphoreType.DMA((2,))],
        in_place=2,
    )
    sent_q = call(0.3, copy_kernel, [narrow(high, third)] * routes.sent, sent_q, after=tuple(halo_kv))

    def forward(first, count, halo, direct):
        return call(
            1.5 * count * third / LANES,
            part(forward_kernel, routes, first, count, head_dim, direct),
            [wide(count, positions, third)] * 2
            + [wide(count, *padded_shape, third)]
            + [narrow(packed, third)] * (first > 0),
            (layout, qkv, *halo, dw_weight, pw_weight),
        )

    mixed_kv, merged_kv, padded_kv, state = forward(1, 2, halo_kv, True)

    def copied(far, tokens):
        return call(0.3, copy_kernel, jax.ShapeDtypeStruct(far.shape, far.dtype), (far,), after=tokens)

    halo_q = routes.move(sent_q, hand_on=lambda near, far: copied(far, (state,)))
    state_from = exchange(state, "tile")
    others = len(state_from)
    mixed_q, merged_q, padded_q = forward(0, 1, halo_q, False)

    gstate, gmix_q, gpw_q = call(
        3.0,
        part(merged_query_kernel, others, head_dim),
        [narrow(packed, third), wide(1, positions, third), wide(1, head_dim, third)],
        (layout, state, *state_from, merged_q, mixed_q, cotangent, pw_weight),
    )
    gstate_from = exchange(gstate, "tile")

    source_from = halo_q if routes.relayed else exchange(sent_q[0][low:], "tile")
    from_offset = low if routes.relayed else 0
    grad0_q, gstate0 = call(
        2.5,
        part(source_query_kernel, others, low, from_offset, head_dim),
        [wide(1, positions, third), narrow(packed, third)],
        (layout, sent_q[0], *source_from, qkv, cotangent),
        after=(gstate,),
    )

    gap = -(-taps // 8) * 8
    rows = gap + head_dim
    halves = groups == 8 and rows % groups == 0
    eighth = rows // groups

    def weights(count, padded, gmix, gpw):
        return call(
            1.0 * count * third / LANES,
            part(weight_kernel, halves),
            [wide(4, eighth, count * third)] * 2 if halves else [wide(rows, count * third)],
            (layout, padded, gmix, gpw),
            [pltpu.VMEM((rows, 128), F32)],
        )

    weights_q = weights(1, padded_q, gmix_q, gpw_q)
    total_rows = 3 * edge + packed
    gmix_kv, gpw_kv, *sent_back = call(
        3.0,
        part(merged_value_kernel, others, routes, tall, head_dim),
        [wide(2, positions, third), wide(2, head_dim, third)] + [narrow(total_rows, third)] * routes.sent,
        (layout, gstate, *gstate_from, merged_kv, mixed_kv, pw_weight, gmix_q, gstate0),
        after=(weights_q[0],),
    )
    weights_kv = weights(2, padded_kv, gmix_kv, gpw_kv)

    norm = 1.0 / math.sqrt(positions * tiles * groups)
    ready = weights_kv
    if halves:
        come_q = exchange(weights_q[0], "img", (1,))[0]
        come_kv = exchange(weights_kv[0], "img", (1,))[0]
        share_shape = wide(eighth, channels)
        shares = call(
            0.5, scatter_kernel, [share_shape] * 4, (layout, weights_q[1], come_q, weights_kv[1], come_kv)
        )
        moved = [
            lax.ppermute(share, "img", [(s, s ^ (2 * m)) for s in range(groups)])
            for m, share in enumerate(shares[1:], 1)
        ]
        ready = shares[:1]

    halo_back = routes.move(sent_back, hand_on=lambda near, far: copied(far, (near, *ready)))

    back_from = halo_back if routes.relayed else exchange(sent_back[0][3 * edge :], "tile")
    back_offset = 3 * edge if routes.relayed else 0
    grad0_kv = call(
        1.5,
        part(source_value_kernel, others, 3 * edge, back_offset, head_dim),
        wide(2, positions, third),
        (layout, sent_back[0], *back_from, qkv),
    )

    def backward(first, gmix, grad0, onto=()):
        blocks = gmix.shape[0] * third // LANES
        return call(
            1.0 * blocks,
            part(backward_kernel, routes, first),
            pltpu.HBM((1, 1, tall, broad, channels), BF16),
            (layout, gmix, *halo_back, dw_weight, grad0),
            [pltpu.VMEM((*padded_shape, LANES), F32)]
            + [pltpu.VMEM((blocks, tall, broad, LANES), BF16), pltpu.SemaphoreType.DMA((blocks,))],
            out_space=pltpu.HBM,
            onto=onto,
        )

    grad_query = in_hbm(backward(0, gmix_q, grad0_q))
    grad_source = backward(1, gmix_kv, grad0_kv, (grad_query,))

    if halves:
        total = call(0.3, part(sum_kernel, 1.0), share_shape, [shares[0]] + moved)
        total = call(
            0.3, part(sum_kernel, norm), share_shape, [total] + exchange(total, "tile"), after=(grad_query, grad0_kv)
        )
        quarters = call(
            0.5,
            collect_kernel,
            wide(4, eighth, channels),
            (layout, total, *exchange(total, "img", (2, 4, 6))),
            after=(in_hbm(grad_source),),
        )
        grad_dw, grad_pw = call(
            0.8,
            part(finish_kernel, taps),
            [wide(taps, channels), wide(head_dim, channels)],
            (layout, quarters, exchange(quarters, "img", (1,))[0]),
            [pltpu.VMEM((rows, channels), F32)],
        )
    else:
        whole = jnp.concatenate([weights_q[0], weights_kv[0]], axis=1)
        whole = lax.psum(whole, ("tile", "img")) * norm
        grad_dw, grad_pw = whole[:taps], whole[gap:]
    return grad_source, grad_dw, grad_pw


def solution(mesh):
    placed = (
        P("img", "tile", None, None, None),
        P("img", "tile", None, None, None),
        P(),
        P(),
        P("img", "tile"),
        P("img", "tile"),
        P("img", "tile"),
        P("img", None),
        P("img", None),
    )
    return jax.shard_map(
        local,
        mesh=mesh,
        in_specs=placed,
        out_specs=(P("img", "tile", None, None, None), P(), P()),
        check_vma=False,
    )
```

```python
import functools
import math

import jax
import jax.numpy as jnp
from jax import lax
from jax.experimental import pallas as pl
from jax.experimental.pallas import tpu as pltpu
from jax.sharding import PartitionSpec as P

EPSILON = 1e-06
LANES = 256
REACH = 2
EDGE = 8
BYTES_PER_US = 3_690_000
BF16 = jnp.bfloat16
F32 = jnp.float32
PARAMS = pltpu.CompilerParams(vmem_limit_bytes=16 * 1024 * 1024)


class Place:
    def __init__(self, info_ref):
        slots = (info_ref.shape[0] - 4) // 2
        slot = info_ref[0]
        tall = wide = start = jnp.int32(0)
        for s in range(slots):
            tall_s, wide_s = info_ref[4 + s], info_ref[4 + slots + s]
            tall = jnp.where(slot == s, tall_s, tall)
            wide = jnp.where(slot == s, wide_s, wide)
            start = start + jnp.where(s < slot, tall_s * wide_s, 0)
        self.live = slot < slots
        self.tall, self.wide = tall, wide
        self.row, self.col = info_ref[1], info_ref[2]
        self.group = info_ref[3]
        self.within = self.row * wide + self.col
        self.index = start + self.within
        self.above = self.live & (self.row > 0)
        self.below = self.live & (self.row < tall - 1)

    def same_image(self, delta):
        other = self.within + delta
        return self.live & (other >= 0) & (other < self.tall * self.wide)


class Routes:
    def __init__(self, count):
        self.count = count
        self.relayed = count == 4
        self.shifts = [k for k in (1, -1, 2, -2, 3, -3) if abs(k) < count]
        self.sent = 2 if self.relayed else len(self.shifts)
        self.arriving = 3 if self.relayed else len(self.shifts)

    def targets(self, place, direct=False):
        if not self.relayed:
            return [jnp.int32(k) for k in self.shifts]
        near, far, last = ((place.index ^ m) - place.index for m in (1, 2, 3))
        if direct:
            return [near, far, last, last]
        return [near, jnp.where(place.same_image(far), far, last)]

    def sources(self, place, direct=False):
        if not self.relayed:
            return [jnp.int32(-k) for k in self.shifts]
        near, far, last = ((place.index ^ m) - place.index for m in (1, 2, 3))
        if direct:
            outer = jnp.abs(last) == 3
            return [near, far, jnp.where(outer, 0, last), jnp.where(outer, last, 0)]
        return [near, far, last]

    def direct_rows(self, edge):
        return [edge, edge, edge, REACH * EDGE] if self.relayed else [edge] * self.sent

    def move(self, sent, hand_on=lambda near, far: far):
        count = self.count
        if not self.relayed:
            return [
                lax.ppermute(part, "tile", [(s, s + k) for s in range(max(0, -k), min(count, count - k))])
                for part, k in zip(sent, self.shifts)
            ]
        near, far = (
            lax.ppermute(part, "tile", [(s, s ^ m) for s in range(count)]) for part, m in zip(sent, (1, 2))
        )
        return [near, far, lax.ppermute(hand_on(near, far), "tile", [(s, s ^ 1) for s in range(count)])]

    def move_direct(self, sent):
        if not self.relayed:
            return self.move(sent)
        targets = ((1, 0, 3, 2), (2, 3, 0, 1), (0, 2, 1, 3), (3, 1, 2, 0))
        return [lax.ppermute(part, "tile", list(enumerate(to))) for part, to in zip(sent, targets)]


def exchange(value, axis, masks=None):
    count = lax.axis_size(axis)
    masks = range(1, count) if masks is None else masks
    return [lax.ppermute(value, axis, [(s, s ^ m) for s in range(count)]) for m in masks]


def split(x):
    high = x.astype(BF16)
    return high, (x - high.astype(F32)).astype(BF16)


def contract(a, b, dims):
    return lax.dot_general(a, b, (dims, ((), ())), preferred_element_type=F32)


NN = ((1,), (0,))
NT = ((1,), (1,))
TN = ((0,), (0,))


def dot(a, b, dims):
    total = contract(a[0], b[0], dims)
    if b[1] is not None:
        total = total + contract(a[0], b[1], dims)
    if a[1] is not None:
        total = total + contract(a[1], b[0], dims)
    return total


def exact(x):
    return x.astype(BF16), None


def same_head(head_dim):
    rows = lax.broadcasted_iota(jnp.int32, (LANES, LANES), 0) // head_dim
    cols = lax.broadcasted_iota(jnp.int32, (LANES, LANES), 1) // head_dim
    return rows == cols


def spread(compact, mask):
    tall = jnp.concatenate([compact] * (LANES // compact.shape[0]), axis=0)
    return jnp.where(mask, tall, 0.0)


def gather_blocks(full, mask, head_dim):
    kept = jnp.where(mask, full, 0.0)
    return jnp.sum(kept.reshape(LANES // head_dim, head_dim, LANES), axis=0)


def payload(field, place, delta):
    tall, broad, lanes = field.shape
    size = REACH * broad
    top = field[:REACH].reshape(size, lanes)
    bottom = field[tall - REACH :].reshape(size, lanes)
    left = field[:, :EDGE].reshape(size, lanes)
    right = field[:, broad - EDGE :].reshape(size, lanes)
    rows = jnp.where(delta > 0, bottom, top)
    cols = jnp.where(place.col == 0, right, left)
    beside = (place.wide == 2) & (delta == jnp.where(place.col == 0, 1, -1))
    return jnp.where(beside, cols, rows)


def lanes_at(block):
    start = block * LANES
    return pl.ds(start if isinstance(start, int) else pl.multiple_of(start, LANES), LANES)


def pack_state(state, total):
    rows = jnp.concatenate([state, total, jnp.zeros((7, state.shape[1]), F32)], axis=0)
    high = rows.astype(BF16).astype(F32)
    return jnp.concatenate([high, rows - high], axis=0).astype(BF16)


def unpack_state(ref, offset):
    rows = ref[offset:].astype(F32)
    half = rows.shape[0] // 2
    return rows[:half] + rows[half:]


def total_state(own_ref, others, place, offset, others_offset):
    total = unpack_state(own_ref, offset)
    for m, other in enumerate(others, 1):
        delta = (place.index ^ m) - place.index
        total = total + jnp.where(place.same_image(delta), unpack_state(other, others_offset), 0.0)
    return total


def corner_payload(field, delta):
    tall, broad, lanes = field.shape
    corner = jnp.where(delta > 0, field[tall - REACH :, broad - EDGE :], field[:REACH, :EDGE])
    return corner.reshape(REACH * EDGE, lanes)


def fill_padded(pad_ref, field, arrived, deltas, place):
    tall, broad, lanes = field.shape
    two = place.live & (place.wide == 2)
    one = place.live & (place.wide == 1)
    first, second = two & (place.col == 0), two & (place.col == 1)

    def choose(condition, value, other):
        return jnp.where(condition, value, other)

    above = below = jnp.zeros((REACH, broad, lanes), F32)
    above_side = below_side = jnp.zeros((REACH, EDGE, lanes), F32)
    side = jnp.zeros((tall, EDGE, lanes), F32)
    for edges, delta in zip(arrived, deltas):
        edges = edges.astype(F32)
        if edges.shape[0] == REACH * EDGE:
            corner = edges.reshape(REACH, EDGE, lanes)
            above_side = choose(second & (delta == -3), corner, above_side)
            below_side = choose(first & (delta == 3), corner, below_side)
            continue
        rows, cols = edges.reshape(REACH, broad, lanes), edges.reshape(tall, EDGE, lanes)
        begin, end = rows[:, :EDGE], rows[:, broad - EDGE :]
        above = choose((one & (delta == -1)) | (two & (delta == -2)), rows, above)
        below = choose((one & (delta == 1)) | (two & (delta == 2)), rows, below)
        side = choose((first & (delta == 1)) | (second & (delta == -1)), cols, side)
        above_side = choose(first & (delta == -1), begin, choose(second & (delta == -3), end, above_side))
        below_side = choose(second & (delta == 1), end, choose(first & (delta == 3), begin, below_side))
    column = lax.broadcasted_iota(jnp.int32, (1, EDGE, lanes), 1)
    reached = (first & (column < REACH)) | (second & (column >= EDGE - REACH))
    upper, lower = slice(0, REACH), slice(REACH + tall, 2 * REACH + tall)
    pad_ref[upper, :broad] = choose(place.above, above, 0.0)
    pad_ref[lower, :broad] = choose(place.below, below, 0.0)
    pad_ref[upper, broad:] = choose(reached & place.above, above_side, 0.0)
    pad_ref[lower, broad:] = choose(reached & place.below, below_side, 0.0)
    pad_ref[REACH : REACH + tall, broad:] = choose(reached, side, 0.0)
    pad_ref[REACH : REACH + tall, :broad] = field


def convolve(pad_ref, kernel_ref, emit, flipped):
    taps = 2 * REACH + 1
    tall, broad, lanes = pad_ref.shape[0] - 2 * REACH, pad_ref.shape[1] - EDGE, pad_ref.shape[2]
    ring = broad + EDGE
    sub = 128
    for start in range(0, lanes, sub):
        at = slice(start, start + sub)
        for y in range(tall):
            rows = [pad_ref[y + a, :, at] for a in range(taps)]
            total = None
            for b in range(taps):
                part = None
                for a in range(taps):
                    tap = taps * a + b
                    if flipped:
                        tap = taps * taps - 1 - tap
                    row = rows[a][:broad] if b == REACH else rows[a]
                    term = row * kernel_ref[tap : tap + 1, at]
                    part = term if part is None else part + term
                if b != REACH:
                    part = pltpu.roll(part, (REACH - b) % ring, 0)
                total = part[:broad] if total is None else total + part[:broad]
            emit(y, at, total)


def read_field(ref, place, at=slice(None)):
    return jnp.where(place.live, ref[0, 0, :, :, at].astype(F32), 0.0)


def outgoing_kernel(routes, layout, key_ref, value_ref, *outs):
    place = Place(layout)
    for member, field_ref in enumerate((key_ref, value_ref)):
        field = field_ref[0, 0].astype(F32)
        for delta, out_ref in zip(routes.targets(place, True), outs):
            full = out_ref.shape[1] == REACH * field.shape[1]
            sent = payload(field, place, delta) if full else corner_payload(field, delta)
            out_ref[member] = sent.astype(BF16)


def thirds(ref, at):
    third = ref.shape[4] // 3
    return [slice(member * third + at.start, member * third + at.stop) for member in range(3)]


def source_state_kernel(routes, head_dim, layout, field_ref, *refs):
    weight_refs, outs, held, sems = refs[:2], refs[2:-3], refs[-3:-1], refs[-1]
    loads = [pltpu.make_async_copy(a, b, sems.at[i]) for i, (a, b) in enumerate(zip(weight_refs, held))]
    for load in loads:
        load.start()
    place = Place(layout)
    mask = same_head(head_dim)
    size = REACH * field_ref.shape[3]
    for at in parts_of(outs[0].shape[1]):
        query_at, key_at, value_at = thirds(field_ref, at)
        field = field_ref[0, 0, :, :, query_at].astype(F32)
        keys = jnp.maximum(read_field(field_ref, place, key_at).reshape(-1, LANES), 0.0)
        values = read_field(field_ref, place, value_at).reshape(-1, LANES)
        state = gather_blocks(contract(keys.astype(BF16), values.astype(BF16), TN), mask, head_dim)
        packed = pack_state(state, jnp.sum(keys, axis=0, keepdims=True))
        for delta, out_ref in zip(routes.targets(place), outs):
            out_ref[:size, at] = payload(field, place, delta).astype(BF16)
            out_ref[size:, at] = packed
    for load in loads:
        load.wait()


def forward_kernel(routes, first, count, head_dim, direct, *refs):
    layout, field_ref = refs[:2]
    place = Place(layout)
    deltas = routes.sources(place, direct)
    arrived, refs = refs[2 : 2 + len(deltas)], refs[2 + len(deltas) :]
    dw_ref, pw_ref, mixed_ref, merged_ref, padded_ref = refs[:5]
    mask = same_head(head_dim)
    per = mixed_ref.shape[2] // LANES
    size = REACH * field_ref.shape[3]

    def one_block(block, carry):
        at, member, within = lanes_at(first * per + block), block // per, lanes_at(block % per)
        field = read_field(field_ref, place, at)
        if len(arrived[0].shape) == 3:
            edges = [ref[member, :, within] for ref in arrived]
        else:
            edges = [ref[:size, within] for ref in arrived]
        padded = padded_ref.at[member, :, :, within]
        fill_padded(padded, field, edges, deltas, place)
        target = mixed_ref.at[member, :, within]
        broad = field.shape[1]

        def emit(y, sub, total):
            target[y * broad : (y + 1) * broad, sub] = total

        convolve(padded, dw_ref.at[:, at], emit, False)
        mixed = target[...]
        merged_ref[member, :, within] = dot(split(mixed), split(spread(pw_ref[:, at], mask)), NN)
        return carry

    lax.fori_loop(0, count * per, one_block, 0, unroll=2)
    if first == 0:
        return
    state_ref = refs[5]
    for at in parts_of(state_ref.shape[1]):
        keys = jnp.maximum(merged_ref[0, :, at], 0.0)
        state = gather_blocks(dot(split(keys), split(merged_ref[1, :, at]), TN), mask, head_dim)
        state_ref[:, at] = pack_state(state, jnp.sum(keys, axis=0, keepdims=True))


def parts_of(lanes):
    return [slice(start, start + LANES) for start in range(0, lanes, LANES)]


def query_gradients(raw, exactly, total, cot, head_dim, mask):
    ones = (mask.astype(BF16), None)
    query = jnp.maximum(raw, 0.0)
    pair = exact(query) if exactly else split(query)
    state = split(spread(total[:head_dim], mask))
    key_sum = total[head_dim : head_dim + 1]
    over = 1.0 / (dot(split(query * key_sum), ones, NN) + EPSILON)
    result = dot(pair, state, NN) * over
    grad_num = cot * over
    grad_den = -dot(split(cot * result), ones, NN) * over
    num_pair = split(grad_num)
    grad = jnp.where(raw > 0, dot(num_pair, state, NT) + grad_den * key_sum, 0.0)
    gstate = gather_blocks(dot(pair, num_pair, TN), mask, head_dim)
    return grad, pack_state(gstate, jnp.sum(query * grad_den, axis=0, keepdims=True))


def source_query_kernel(others, offset, others_offset, head_dim, *refs):
    layout, own_ref, received = refs[0], refs[1], refs[2 : 2 + others]
    source_ref, cot_ref, grad_ref, gstate_ref = refs[2 + others :]
    place = Place(layout)
    mask = same_head(head_dim)
    total = total_state(own_ref, received, place, offset, others_offset)
    for at in parts_of(gstate_ref.shape[1]):
        raw = read_field(source_ref, place, at).reshape(-1, LANES)
        cot = cot_ref[0, 0, :, :, at].astype(F32).reshape(raw.shape)
        grad_ref[0, :, at], gstate_ref[:, at] = query_gradients(raw, True, total[:, at], cot, head_dim, mask)


def merged_query_kernel(others, head_dim, *refs):
    layout, own_ref, received = refs[0], refs[1], refs[2 : 2 + others]
    merged_ref, mixed_ref, cot_ref, pw_ref, gstate_ref, gmix_ref, gpw_ref = refs[2 + others :]
    place = Place(layout)
    mask = same_head(head_dim)
    total = total_state(own_ref, received, place, 0, 0)
    third = gstate_ref.shape[1]
    for at in parts_of(third):
        raw = merged_ref[0, :, at]
        cot = cot_ref[0, 0, :, :, third + at.start : third + at.stop].astype(F32).reshape(raw.shape)
        grad, gstate_ref[:, at] = query_gradients(raw, False, total[:, at], cot, head_dim, mask)
        pair = split(grad)
        gmix_ref[0, :, at] = dot(pair, split(spread(pw_ref[:, at], mask)), NT)
        gpw_ref[0, :, at] = gather_blocks(dot(split(mixed_ref[0, :, at]), pair, TN), mask, head_dim)


def key_gradients(raw, key_pair, value_pair, total, head_dim, mask):
    gstate = split(spread(total[:head_dim], mask))
    gsum = total[head_dim : head_dim + 1]
    grad_keys = jnp.where(raw > 0, dot(value_pair, gstate, NT) + gsum, 0.0)
    return grad_keys, dot(key_pair, gstate, NN)


def source_value_kernel(others, offset, others_offset, head_dim, *refs):
    layout, own_ref, received = refs[0], refs[1], refs[2 : 2 + others]
    field_ref, grad_ref = refs[2 + others :]
    place = Place(layout)
    mask = same_head(head_dim)
    total = total_state(own_ref, received, place, offset, others_offset)
    for at in parts_of(grad_ref.shape[2]):
        _, key_at, value_at = thirds(field_ref, at)
        raw = read_field(field_ref, place, key_at).reshape(-1, LANES)
        values = read_field(field_ref, place, value_at).reshape(-1, LANES)
        grad_ref[0, :, at], grad_ref[1, :, at] = key_gradients(
            raw, exact(jnp.maximum(raw, 0.0)), exact(values), total[:, at], head_dim, mask
        )


def merged_value_kernel(others, routes, tall, head_dim, *refs):
    layout, own_ref, received = refs[0], refs[1], refs[2 : 2 + others]
    merged_ref, mixed_ref, pw_ref, qgmix_ref, packed_ref, gmix_ref, gpw_ref = refs[2 + others : 9 + others]
    outs = refs[9 + others :]
    place = Place(layout)
    mask = same_head(head_dim)
    total = total_state(own_ref, received, place, 0, 0)
    size = (outs[0].shape[0] - packed_ref.shape[0]) // 3

    def send(member, at, gmix):
        field = gmix.reshape(tall, -1, LANES)
        for delta, out_ref in zip(routes.targets(place), outs):
            out_ref[member * size : (member + 1) * size, at] = payload(field, place, delta).astype(BF16)

    for at in parts_of(gmix_ref.shape[2]):
        for out_ref in outs:
            out_ref[3 * size :, at] = packed_ref[:, at]
        send(0, at, qgmix_ref[0, :, at])
        raw = merged_ref[0, :, at]
        pairs = split(jnp.maximum(raw, 0.0)), split(merged_ref[1, :, at])
        grads = key_gradients(raw, *pairs, total[:, at], head_dim, mask)
        third = gmix_ref.shape[2]
        for member, grad in enumerate(grads):
            pair = split(grad)
            begin = (1 + member) * third + at.start
            gmix = dot(pair, split(spread(pw_ref[:, begin : begin + LANES], mask)), NT)
            gmix_ref[member, :, at] = gmix
            gpw_ref[member, :, at] = gather_blocks(dot(split(mixed_ref[member, :, at]), pair, TN), mask, head_dim)
            send(1 + member, at, gmix)


def weight_kernel(halves, layout, padded_ref, gmix_ref, gpw_ref, *refs):
    outs, sum_ref = refs[:-1], refs[-1]
    ring, sub = padded_ref.shape[2], 128
    tall, broad = padded_ref.shape[1] - 2 * REACH, ring - EDGE
    taps = 2 * REACH + 1
    count, head_dim, third = gpw_ref.shape
    start = sum_ref.shape[0] - head_dim
    odd = Place(layout).group % 2 == 1
    each = third // sub

    def one_block(block, carry):
        member = block // each
        at = pl.ds(pl.multiple_of(block % each * sub, sub), sub)
        out_at = pl.ds(pl.multiple_of(block * sub, sub), sub)

        def one_row(y, totals):
            grad = gmix_ref[member, pl.ds(pl.multiple_of(y * broad, broad), broad), at]
            longer = jnp.concatenate([grad, jnp.zeros((EDGE, sub), F32)], axis=0)
            moved = [grad if b == REACH else pltpu.roll(longer, (b - REACH) % ring, 0) for b in range(taps)]
            new = list(totals)
            for a in range(taps):
                row = padded_ref[member, y + a, :, at]
                for b in range(taps):
                    term = row[: moved[b].shape[0]] * moved[b]
                    term = term.reshape(term.shape[0] // 8, 8, sub)
                    new[taps * a + b] = new[taps * a + b] + jnp.sum(term, axis=0)
            return tuple(new)

        zero = jnp.zeros((8, sub), F32)
        totals = lax.fori_loop(0, tall, one_row, (zero,) * (taps * taps), unroll=4)
        for tap in range(taps * taps):
            sum_ref[tap : tap + 1] = jnp.sum(totals[tap], axis=0, keepdims=True)
        sum_ref[taps * taps : start] = jnp.zeros((start - taps * taps, sub), F32)
        sum_ref[start:] = gpw_ref[member, :, at]
        if not halves:
            outs[0][:, out_at] = sum_ref[...]
            return carry
        rows = outs[0].shape[1]
        for part in range(outs[0].shape[0]):
            even_rows = sum_ref[2 * part * rows : (2 * part + 1) * rows]
            odd_rows = sum_ref[(2 * part + 1) * rows : (2 * part + 2) * rows]
            outs[0][part, :, out_at] = jnp.where(odd, even_rows, odd_rows)
            outs[1][part, :, out_at] = jnp.where(odd, odd_rows, even_rows)
        return carry

    lax.fori_loop(0, count * each, one_block, 0)


def scatter_kernel(layout, keep_q, come_q, keep_kv, come_kv, own_ref, *outs):
    quarter = Place(layout).group // 2
    third = keep_q.shape[2]
    for m, out_ref in enumerate((own_ref,) + outs):
        at = quarter ^ m
        out_ref[:, :third] = keep_q[at] + come_q[at]
        out_ref[:, third:] = keep_kv[at] + come_kv[at]


def sum_kernel(norm, *refs):
    parts, out_ref = [ref[...] for ref in refs[:-1]], refs[-1]
    while len(parts) > 1:
        parts = [parts[i] + parts[i + 1] for i in range(0, len(parts), 2)]
    total = parts[0] * norm
    if out_ref.shape != total.shape:
        half = total.shape[1] // 2
        total = jnp.concatenate([total[:, :half], total[:, half:]], axis=0)
    out_ref[...] = total.astype(out_ref.dtype)


def collect_kernel(layout, *refs):
    parts, out_ref = refs[:-1], refs[-1]
    quarter = Place(layout).group // 2
    for m, part in enumerate(parts):
        out_ref[quarter ^ m] = part[...]


def finish_kernel(taps, layout, own_ref, come_ref, dw_ref, pw_ref, whole_ref):
    odd = Place(layout).group % 2 == 1
    quarters, rows = own_ref.shape[0], own_ref.shape[1] // 2

    def unfold(value):
        value = value.astype(F32)
        return jnp.concatenate([value[:rows], value[rows:]], axis=1)

    for part in range(quarters):
        own, come = unfold(own_ref[part]), unfold(come_ref[part])
        whole_ref[2 * part * rows : (2 * part + 1) * rows] = jnp.where(odd, come, own)
        whole_ref[(2 * part + 1) * rows : (2 * part + 2) * rows] = jnp.where(odd, own, come)
    dw_ref[...] = whole_ref[:taps]
    pw_ref[...] = whole_ref[whole_ref.shape[0] - pw_ref.shape[0] :]


def copy_kernel(*refs):
    half = len(refs) // 2
    for in_ref, out_ref in zip(refs[:half], refs[half:]):
        out_ref[...] = in_ref[...]


def backward_kernel(routes, first, *refs):
    layout, gmix_ref = refs[:2]
    arrived = refs[2 : 2 + routes.arriving]
    dw_ref, grad0_ref, out_ref, pad_ref, done_ref, sems = refs[2 + routes.arriving :]
    place = Place(layout)
    deltas = routes.sources(place)
    tall, broad = out_ref.shape[2:4]
    count, _, third = gmix_ref.shape
    per, size = third // LANES, REACH * broad

    def one_block(block, carry):
        at, member, within = lanes_at(first * per + block), block // per, lanes_at(block % per)
        begin = pl.multiple_of((first + member) * size, size)
        edges = [ref[pl.ds(begin, size), within] for ref in arrived]
        field = gmix_ref[member, :, within].reshape(tall, broad, LANES)
        fill_padded(pad_ref, field, edges, deltas, place)
        grad0 = grad0_ref.at[member, :, within]

        def emit(y, sub, total):
            total = total + grad0[y * broad : (y + 1) * broad, sub]
            done_ref[block, y, :, sub] = jnp.where(place.live, total, 0.0).astype(BF16)

        convolve(pad_ref, dw_ref.at[:, at], emit, True)
        write(block).start()
        return carry

    def write(block):
        target = out_ref.at[0, 0, :, :, lanes_at(first * per + block)]
        return pltpu.make_async_copy(done_ref.at[block], target, sems.at[block])

    lax.fori_loop(0, count * per, one_block, 0, unroll=2)
    for block in range(count * per):
        write(block).wait()


def in_hbm(x):
    return pltpu.with_memory_space_constraint(x, pltpu.HBM)


def call(cost, kernel, out_shape, args, scratch=(), after=(), in_place=0, out_space=pltpu.VMEM, onto=()):
    inputs, extra = len(args), len(onto) + len(after)

    def body(*refs):
        kernel(*refs[:inputs], *refs[inputs + extra :])

    spaces = [pltpu.SMEM if x.dtype == jnp.int32 else pltpu.VMEM for x in args]
    spaces[inputs - in_place :] = [pl.ANY] * in_place
    spaces += [out_space] * len(onto) + [pl.ANY] * len(after)
    return pl.pallas_call(
        body,
        in_specs=[pl.BlockSpec(memory_space=space) for space in spaces],
        out_specs=jax.tree.map(lambda _: pl.BlockSpec(memory_space=out_space), out_shape),
        out_shape=out_shape,
        scratch_shapes=list(scratch),
        input_output_aliases={inputs: 0} if onto else {},
        compiler_params=PARAMS,
        cost_estimate=pl.CostEstimate(
            flops=0, bytes_accessed=int(cost * BYTES_PER_US), transcendentals=0
        ),
    )(*args, *onto, *after)


def local(
    qkv, cotangent, dw_weight, pw_weight, tile_image, tile_row, tile_col, image_height, image_width
):
    tall, broad, channels = qkv.shape[2:]
    positions = tall * broad
    head_dim = pw_weight.shape[0]
    taps = dw_weight.shape[0]
    third = channels // 3
    tiles, groups = lax.axis_size("tile"), lax.axis_size("img")
    routes = Routes(tiles)
    edge = REACH * broad
    packed = 2 * (head_dim + 8)
    padded_shape = (tall + 2 * REACH, broad + EDGE)
    spot = lax.axis_index("img").astype(jnp.int32)
    scalars = (tile_image, tile_row, tile_col, spot, image_height, image_width)
    layout = jnp.concatenate([x.reshape(-1) for x in scalars])
    part = functools.partial

    def wide(*dims):
        return jax.ShapeDtypeStruct(dims, F32)

    def narrow(*dims):
        return jax.ShapeDtypeStruct(dims, BF16)

    low, high = edge, edge + packed

    sent_kv = pl.pallas_call(
        part(outgoing_kernel, routes),
        grid=(1,),
        in_specs=[pl.BlockSpec(memory_space=pltpu.SMEM)]
        + [pl.BlockSpec((1, 1, tall, broad, third), lambda j, m=m: (0, 0, 0, 0, m)) for m in (1, 2)],
        out_specs=[pl.BlockSpec((2, size, third), lambda j: (0, 0, 0)) for size in routes.direct_rows(edge)],
        out_shape=[narrow(2, size, third) for size in routes.direct_rows(edge)],
        compiler_params=PARAMS,
    )(layout, in_hbm(qkv), in_hbm(qkv))
    halo_kv = routes.move_direct(sent_kv)
    *sent_q, dw_weight, pw_weight = call(
        1.0,
        part(source_state_kernel, routes, head_dim),
        [narrow(high, third)] * routes.sent + [wide(taps, channels), wide(head_dim, channels)],
        (layout, qkv, in_hbm(dw_weight), in_hbm(pw_weight)),
        [pltpu.SemaphoreType.DMA((2,))],
        in_place=2,
    )
    sent_q = call(0.3, copy_kernel, [narrow(high, third)] * routes.sent, sent_q, after=tuple(halo_kv))

    def forward(first, count, halo, direct):
        return call(
            1.5 * count * third / LANES,
            part(forward_kernel, routes, first, count, head_dim, direct),
            [wide(count, positions, third)] * 2
            + [wide(count, *padded_shape, third)]
            + [narrow(packed, third)] * (first > 0),
            (layout, qkv, *halo, dw_weight, pw_weight),
        )

    mixed_kv, merged_kv, padded_kv, state = forward(1, 2, halo_kv, True)

    def copied(far, tokens):
        return call(0.3, copy_kernel, jax.ShapeDtypeStruct(far.shape, far.dtype), (far,), after=tokens)

    halo_q = routes.move(sent_q, hand_on=lambda near, far: copied(far, (state,)))
    state_from = exchange(state, "tile")
    others = len(state_from)
    mixed_q, merged_q, padded_q = forward(0, 1, halo_q, False)

    gstate, gmix_q, gpw_q = call(
        3.0,
        part(merged_query_kernel, others, head_dim),
        [narrow(packed, third), wide(1, positions, third), wide(1, head_dim, third)],
        (layout, state, *state_from, merged_q, mixed_q, cotangent, pw_weight),
    )
    gstate_from = exchange(gstate, "tile")

    source_from = halo_q if routes.relayed else exchange(sent_q[0][low:], "tile")
    from_offset = low if routes.relayed else 0
    grad0_q, gstate0 = call(
        2.5,
        part(source_query_kernel, others, low, from_offset, head_dim),
        [wide(1, positions, third), narrow(packed, third)],
        (layout, sent_q[0], *source_from, qkv, cotangent),
        after=(gstate,),
    )

    gap = -(-taps // 8) * 8
    rows = gap + head_dim
    halves = groups == 8 and rows % groups == 0
    eighth = rows // groups

    def weights(count, padded, gmix, gpw):
        return call(
            1.0 * count * third / LANES,
            part(weight_kernel, halves),
            [wide(4, eighth, count * third)] * 2 if halves else [wide(rows, count * third)],
            (layout, padded, gmix, gpw),
            [pltpu.VMEM((rows, 128), F32)],
        )

    weights_q = weights(1, padded_q, gmix_q, gpw_q)
    total_rows = 3 * edge + packed
    gmix_kv, gpw_kv, *sent_back = call(
        3.0,
        part(merged_value_kernel, others, routes, tall, head_dim),
        [wide(2, positions, third), wide(2, head_dim, third)] + [narrow(total_rows, third)] * routes.sent,
        (layout, gstate, *gstate_from, merged_kv, mixed_kv, pw_weight, gmix_q, gstate0),
        after=(weights_q[0],),
    )
    weights_kv = weights(2, padded_kv, gmix_kv, gpw_kv)

    norm = 1.0 / math.sqrt(positions * tiles * groups)
    ready = weights_kv
    if halves:
        come_q = exchange(weights_q[0], "img", (1,))[0]
        come_kv = exchange(weights_kv[0], "img", (1,))[0]
        share_shape = wide(eighth, channels)
        shares = call(
            0.5, scatter_kernel, [share_shape] * 4, (layout, weights_q[1], come_q, weights_kv[1], come_kv)
        )
        moved = [
            lax.ppermute(share, "img", [(s, s ^ (2 * m)) for s in range(groups)])
            for m, share in enumerate(shares[1:], 1)
        ]
        ready = shares[:1]

    halo_back = routes.move(sent_back, hand_on=lambda near, far: copied(far, (near, *ready)))

    back_from = halo_back if routes.relayed else exchange(sent_back[0][3 * edge :], "tile")
    back_offset = 3 * edge if routes.relayed else 0
    grad0_kv = call(
        1.5,
        part(source_value_kernel, others, 3 * edge, back_offset, head_dim),
        wide(2, positions, third),
        (layout, sent_back[0], *back_from, qkv),
    )

    def backward(first, gmix, grad0, onto=()):
        blocks = gmix.shape[0] * third // LANES
        return call(
            1.0 * blocks,
            part(backward_kernel, routes, first),
            pltpu.HBM((1, 1, tall, broad, channels), BF16),
            (layout, gmix, *halo_back, dw_weight, grad0),
            [pltpu.VMEM((*padded_shape, LANES), F32)]
            + [pltpu.VMEM((blocks, tall, broad, LANES), BF16), pltpu.SemaphoreType.DMA((blocks,))],
            out_space=pltpu.HBM,
            onto=onto,
        )

    grad_query = in_hbm(backward(0, gmix_q, grad0_q))
    grad_source = backward(1, gmix_kv, grad0_kv, (grad_query,))

    if halves:
        total = call(0.3, part(sum_kernel, 1.0), share_shape, [shares[0]] + moved)
        total = call(
            0.3, part(sum_kernel, norm), narrow(2 * eighth, channels // 2), [total] + exchange(total, "tile"), after=(grad_query, grad0_kv)
        )
        quarters = call(
            0.5,
            collect_kernel,
            narrow(4, 2 * eighth, channels // 2),
            (layout, total, *exchange(total, "img", (2, 4, 6))),
            after=(in_hbm(grad_source),),
        )
        grad_dw, grad_pw = call(
            0.8,
            part(finish_kernel, taps),
            [wide(taps, channels), wide(head_dim, channels)],
            (layout, quarters, exchange(quarters, "img", (1,))[0]),
            [pltpu.VMEM((rows, channels), F32)],
        )
    else:
        whole = jnp.concatenate([weights_q[0], weights_kv[0]], axis=1)
        whole = lax.psum(whole, ("tile", "img")) * norm
        grad_dw, grad_pw = whole[:taps], whole[gap:]
    return grad_source, grad_dw, grad_pw


def solution(mesh):
    placed = (
        P("img", "tile", None, None, None),
        P("img", "tile", None, None, None),
        P(),
        P(),
        P("img", "tile"),
        P("img", "tile"),
        P("img", "tile"),
        P("img", None),
        P("img", None),
    )
    return jax.shard_map(
        local,
        mesh=mesh,
        in_specs=placed,
        out_specs=(P("img", "tile", None, None, None), P(), P()),
        check_vma=False,
    )
```
